32 devices in a mesh: tm: 4 (over z), space: 8 (over y, x, core).
Axes of the slice: x: 2, y: 2, z: 4, core: 2. Of those that a mesh axis runs over, the one named last changes fastest.
Arguments:
- forcing: float32 [4, 2, 64, 1024], P('tm', None, None, 'space'), may hold values from -6 to 6
- initial_state: float32 [2, 64, 1024], P(None, None, 'space'), may hold values from -6 to 6
- previous: float32 [4, 2, 64, 1024], P('tm', None, None, 'space'), may hold values from -60 to 60
- zone_diffusion: float32 [2, 8], replicated, may hold values from 0.2 to 5
- drift_rate: float32 [2], replicated, may hold values from 0.2 to 1
- column_zone: int32 [1024], P('space'), may hold values from 0 to 7
- bottom_flag: int32 [1024], P('space'), may hold values 0 or 1
- open_faces: int32 [64, 1024], P(None, 'space'), may hold values 0 or 1
Outputs:
- new_iterate: float32 [4, 2, 64, 1024], P('tm', None, None, 'space')
- increment_norm: float32 [], replicated
The draws below stay inside these ranges and needn't reach their ends.
All inputs are finite; a program needn't handle non-finite values. No bound on the sum of `bottom_flag` or of `open_faces` on one device may be relied on, other than what follows from the above.
Results may differ from the reference program's by a relative error of at most 0.00015.
Values sent between devices are 32-bit elements; how exact they have to be, the bound alone decides.
No kernel may reach another device: no remote copies, remote signals or barrier semaphores. Data moves between devices by JAX's collectives and lax.ppermute only.
A program may use at most 64 MiB of HBM per device.

```python
import math
import jax
import jax.numpy as jnp
import numpy as np
from jax import lax

NZ = 64
ZONES = 8
STEPS = 4
NCOL = 1024


def draw_previous(key, part):
    key_base = jax.random.fold_in(key, 11)
    key_cols = jax.random.fold_in(key, 12)
    shape = (STEPS, 2, NZ, NCOL)
    base = jnp.clip(jax.random.normal(key_base, shape, jnp.float32), -4.0, 4.0)
    step_pos = jnp.arange(STEPS).astype(jnp.float32)[:, None, None, None] / STEPS
    col_pos = jnp.arange(NCOL).astype(jnp.float32)[None, None, None, :] / NCOL
    ramp = jnp.exp(math.log(3.0) * (0.5 * step_pos + 0.5 * col_pos))
    col_scale = jnp.exp(math.log(4.0) * jax.random.uniform(key_cols, (NCOL,), jnp.float32))
    return (base * ramp * col_scale[None, None, None, :]).astype(jnp.float32)


def with_ends(array, key, smallest, largest):
    index_at = [jax.random.randint(jax.random.fold_in(key, axis), (), 0, length) for axis, length in enumerate(array.shape)]
    widest = array.shape.index(max(array.shape))
    beside = index_at[:widest] + [(index_at[widest] + 1) % array.shape[widest]] + index_at[widest + 1:]
    return array.at[tuple(index_at)].set(smallest).at[tuple(beside)].set(largest)


def level_of(stream_key, extent, pieces, least, high):
    gain = 1.0
    for dim, parts in pieces:
        draws = jax.random.uniform(jax.random.fold_in(jax.random.fold_in(stream_key, 6), dim), (parts,), jnp.float32, least / len(pieces), high / len(pieces))
        gain = gain * jnp.repeat(jnp.exp(draws), extent[dim] // parts).reshape((-1,) + (1,) * (len(extent) - 1 - dim))
    return gain


def rank_table(amount, slope):
    weights = [(1 << 20) // math.isqrt(rank ** slope) + 1 for rank in range(1, amount + 1)]
    width = 1 + sum(weights) // (1 << 30)
    return np.cumsum(np.array([max(1, weight // width) for weight in weights]))


def ranked(stream_key, dims, amount, lean):
    table = rank_table(amount, lean)
    lot = jax.random.randint(jax.random.fold_in(stream_key, 1), dims, 0, int(table[amount - 1]))
    grade = jnp.searchsorted(jnp.asarray(table, jnp.int32), lot, side="right")
    return jax.random.permutation(jax.random.fold_in(stream_key, 2), amount)[grade].astype(jnp.int32)


def noise(rng, extent, scale, most, shards=(), kind=jnp.bfloat16):
    entries = jax.random.normal(rng, extent, jnp.float32) * scale
    if len(shards) > 0:
        entries = level_of(rng, extent, shards, -0.22, 0.18) * entries
    return jnp.clip(entries, min=-most, max=most).astype(kind)


def setup_inputs(seed: int = 0) -> dict:
    streams_of = jax.random.split(jax.random.key(seed), 9)
    forcing = noise(streams_of[0], (STEPS, 2, NZ, NCOL), 1.0, 6.0, ((0, 4), (3, 8)), jnp.float32)
    initial_state = noise(streams_of[1], (2, NZ, NCOL), 1.0, 6.0, ((2, 8),), jnp.float32)
    previous = draw_previous(jax.random.fold_in(streams_of[8], 71), 0)
    zone_diffusion = jnp.clip(jnp.exp(jax.random.uniform(streams_of[3], (2, ZONES), jnp.float32, math.log(0.2), math.log(5.0))), 0.2, 5.0)
    drift_rate = jnp.clip(jax.random.uniform(streams_of[4], (2,), jnp.float32, 0.2, 1.0), 0.2, 1.0)
    column_zone = with_ends(ranked(streams_of[5], (NCOL,), ZONES, 2), jax.random.fold_in(streams_of[5], 3), 0, ZONES - 1).astype(jnp.int32)
    bottom_flag = with_ends((jax.random.randint(streams_of[6], (NCOL,), 0, 2) < 1).astype(jnp.int32), jax.random.fold_in(streams_of[6], 1), 0, 1)
    open_faces = with_ends((jax.random.randint(streams_of[7], (NZ, NCOL), 0, 4) < 3).astype(jnp.int32), jax.random.fold_in(streams_of[7], 1), 0, 1)
    return dict(forcing=forcing, initial_state=initial_state, previous=previous, zone_diffusion=zone_diffusion, drift_rate=drift_rate, column_zone=column_zone, bottom_flag=bottom_flag, open_faces=open_faces)


alpha_corner = 0.3
highest = lax.Precision.HIGHEST

def coefficients(zone_diffusion, drift_rate, column_zone, bottom_flag, open_faces):
    zone_count = zone_diffusion.shape[1]
    zone_hot = (column_zone[None, :] == jnp.arange(zone_count, dtype=jnp.int32)[:, None]).astype(jnp.float32)
    spread = jnp.dot(zone_diffusion, zone_hot, precision=highest)
    face_open = open_faces.astype(jnp.float32)
    empty_row = jnp.zeros_like(face_open[:1])
    link_below = jnp.concatenate([empty_row, face_open[:-1]], 0)
    link_above = jnp.concatenate([face_open[:-1], empty_row], 0)
    ground = jnp.concatenate([bottom_flag.astype(jnp.float32)[None], jnp.zeros_like(face_open[1:])], 0)
    diffusion = spread[:, None, :]
    drift = drift_rate[:, None, None]
    below = -(diffusion + drift) * link_below
    above = -diffusion * link_above
    centre = diffusion * (link_below + link_above) + drift + 2.0 * diffusion * ground
    return (below, centre, above)

def line_solve(below, centre, shift_imag, above, right_real, right_imag):
    moved = [jnp.moveaxis(item, -2, 0) for item in (below, centre, above, right_real, right_imag)]
    empty_field = jnp.zeros_like(moved[3][0])

    def forward(running, item):
        prime_real, prime_imag, partial_real, partial_imag = running
        lower_coef, centre_coef, upper_coef, rhs_real, rhs_imag = item
        denom_real = centre_coef - lower_coef * prime_real
        denom_imag = shift_imag - lower_coef * prime_imag
        inverse = 1.0 / (denom_real * denom_real + denom_imag * denom_imag)
        next_prime_real = upper_coef * denom_real * inverse
        next_prime_imag = -upper_coef * denom_imag * inverse
        numer_real = rhs_real - lower_coef * partial_real
        numer_imag = rhs_imag - lower_coef * partial_imag
        next_real = (numer_real * denom_real + numer_imag * denom_imag) * inverse
        next_imag = (numer_imag * denom_real - numer_real * denom_imag) * inverse
        result = (next_prime_real, next_prime_imag, next_real, next_imag)
        return (result, result)
    start_state = (empty_field, empty_field, empty_field, empty_field)
    unused, stacked = lax.scan(forward, start_state, tuple(moved))

    def backward(value, item):
        prime_real, prime_imag, partial_real, partial_imag = item
        new_real = partial_real - (prime_real * value[0] - prime_imag * value[1])
        new_imag = partial_imag - (prime_real * value[1] + prime_imag * value[0])
        return ((new_real, new_imag), (new_real, new_imag))
    unused_back, solved = lax.scan(backward, (empty_field, empty_field), stacked, reverse=True)
    return (jnp.moveaxis(solved[0], 0, -2), jnp.moveaxis(solved[1], 0, -2))

def reference(forcing, initial_state, previous, zone_diffusion, drift_rate, column_zone, bottom_flag, open_faces):
    length = forcing.shape[0]
    opening = forcing[0] + initial_state - alpha_corner * previous[length - 1]
    loaded = jnp.concatenate([opening[None], forcing[1:]], 0)
    log_alpha = math.log(alpha_corner)
    time_ids = jnp.arange(length).astype(jnp.float32)
    ramp_up = jnp.exp(log_alpha * time_ids / length)
    scaled = loaded * ramp_up[:, None, None, None]
    spectrum = jnp.fft.fft(scaled, axis=0)
    spectrum_real = jnp.real(spectrum).astype(jnp.float32)
    spectrum_imag = jnp.imag(spectrum).astype(jnp.float32)
    root_factor = math.exp(log_alpha / length)
    freq_angle = time_ids * (2.0 * math.pi / length)
    shift_real = 1.0 - root_factor * jnp.cos(freq_angle)
    shift_imag = root_factor * jnp.sin(freq_angle)
    below, centre, above = coefficients(zone_diffusion, drift_rate, column_zone, bottom_flag, open_faces)
    full_centre = centre[None] + shift_real[:, None, None, None]
    solved_real, solved_imag = line_solve(below[None], full_centre, shift_imag[:, None, None], above[None], spectrum_real, spectrum_imag)
    restored = jnp.fft.ifft(solved_real + 1j * solved_imag, axis=0)
    restored_real = jnp.real(restored).astype(jnp.float32)
    ramp_down = jnp.exp(-log_alpha * time_ids / length)
    new_iterate = (restored_real * ramp_down[:, None, None, None]).astype(jnp.float32)
    change = new_iterate - previous
    increment_norm = jnp.sqrt(jnp.mean(change * change)).astype(jnp.float32)
    return (new_iterate, increment_norm)
```

```python
import functools
import math

import jax
import jax.numpy as jnp
from jax import lax
from jax.experimental import pallas as pl
from jax.experimental.pallas import tpu as pltpu
from jax.sharding import PartitionSpec as P

alpha_corner = 0.3
tile = 8
near_steps = 3


def roll_down(block, distance):
    return pltpu.roll(block, distance, 0)


def roll_up(block, distance):
    return pltpu.roll(block, block.shape[0] - distance, 0)


def c_mul(x, y):
    if len(x) == 1 and len(y) == 1:
        return (x[0] * y[0],)
    if len(x) == 1:
        return (x[0] * y[0], x[0] * y[1])
    if len(y) == 1:
        return (x[0] * y[0], x[1] * y[0])
    return (x[0] * y[0] - x[1] * y[1], x[0] * y[1] + x[1] * y[0])


def c_add(x, y):
    return tuple(p + q for p, q in zip(x, y))


def c_sub(x, y):
    return tuple(p - q for p, q in zip(x, y))


def c_neg(x):
    return tuple(-p for p in x)


def c_inverse(x):
    if len(x) == 1:
        return (1.0 / x[0],)
    scale = 1.0 / (x[0] * x[0] + x[1] * x[1])
    return (x[0] * scale, -x[1] * scale)


def c_map(f, x):
    return tuple(f(p) for p in x)


def frequencies(length):
    root = math.exp(math.log(alpha_corner) / length)
    listed = []
    for j in range(length // 2 + 1):
        angle = 2.0 * math.pi * j / length
        if j == 0 or 2 * j == length:
            listed.append((j, (1.0 - root * math.cos(angle),)))
        else:
            listed.append((j, (1.0 - root * math.cos(angle), root * math.sin(angle))))
    return listed


def planes(length):
    return sum(len(shift) for unused, shift in frequencies(length))


def factor_kernel(length, zones_ref, drift_ref, zone_ref, flag_ref, faces_ref, near_ref, far_ref):
    cells, lanes = faces_ref.shape
    faces = faces_ref[...].astype(jnp.float32)
    row = lax.broadcasted_iota(jnp.int32, (cells, lanes), 0)
    link_above = jnp.where(row == cells - 1, 0.0, faces)
    link_below = jnp.where(row == 0, 0.0, roll_down(faces, 1))
    ground = jnp.where(row == 0, flag_ref[...].astype(jnp.float32), 0.0)
    zone = zone_ref[...]
    for species in range(2):
        diffusion = jnp.zeros(zone.shape, jnp.float32)
        for index in range(zones_ref.shape[1]):
            diffusion = jnp.where(zone == index, zones_ref[species, index], diffusion)
        drift = drift_ref[species]
        below = -(diffusion + drift) * link_below
        above = -diffusion * link_above
        centre = diffusion * (link_below + link_above) + drift + 2.0 * diffusion * ground
        plane = 0
        for unused, shift in frequencies(length):
            parts = len(shift)
            a = (below,)
            c = (above,)
            b = (centre + shift[0],)
            if parts == 2:
                b = b + (jnp.full_like(centre, shift[1]),)
            for step in range(near_steps):
                distance = 1 << step
                inverse = c_inverse(b)
                low = c_neg(c_mul(a, c_map(lambda p: roll_down(p, distance), inverse)))
                high = c_neg(c_mul(c, c_map(lambda p: roll_up(p, distance), inverse)))
                down_c = c_map(lambda p: roll_down(p, distance), c)
                up_a = c_map(lambda p: roll_up(p, distance), a)
                b = c_add(b, c_add(c_mul(low, down_c), c_mul(high, up_a)))
                a = c_mul(low, c_map(lambda p: roll_down(p, distance), a))
                c = c_mul(high, c_map(lambda p: roll_up(p, distance), c))
                for part in range(parts):
                    near_ref[species, plane + part, 2 * step] = low[part]
                    near_ref[species, plane + part, 2 * step + 1] = high[part]
            carry = None
            for block in range(cells // tile):
                rows = slice(block * tile, (block + 1) * tile)
                ak, bk, ck = (c_map(lambda p: p[rows], item) for item in (a, b, c))
                if carry is None:
                    eliminate = c_map(jnp.zeros_like, ak)
                else:
                    eliminate = c_mul(ak, carry[0])
                    bk = c_sub(bk, c_mul(eliminate, carry[1]))
                inverse = c_inverse(bk)
                substitute = c_mul(ck, inverse)
                for part in range(parts):
                    far_ref[species, plane + part, 0, rows] = eliminate[part]
                    far_ref[species, plane + part, 1, rows] = inverse[part]
                    far_ref[species, plane + part, 2, rows] = substitute[part]
                carry = (inverse, ck)
            plane += parts


def sweep_kernel(length, peers, corners, *refs):
    loads = refs[: peers + 1]
    corner_refs = refs[peers + 1 : peers + 1 + corners]
    initial_ref, previous_ref, near_ref, far_ref, new_ref, sum_ref = refs[peers + 1 + corners :]
    cells, lanes = initial_ref.shape[1:]
    me = lax.axis_index("tm")
    total = jnp.zeros((tile, lanes), jnp.float32)
    for species in range(2):
        mine = previous_ref[0, species]
        last = jnp.where(me == length - 1, mine, 0.0)
        for ref in corner_refs:
            last = last + ref[species]
        correction = initial_ref[species] - alpha_corner * last
        scaled = []
        for behind in range(length):
            factor = math.exp(-math.log(alpha_corner) * behind / length)
            load = loads[behind][0, species]
            load = jnp.where(me == behind, load + correction, load)
            scaled.append(load * jnp.where(me < behind, alpha_corner * factor, factor))
        answer = jnp.zeros((cells, lanes), jnp.float32)
        plane = 0
        for j, shift in frequencies(length):
            parts = len(shift)
            rhs = []
            for part in range(parts):
                value = jnp.zeros((cells, lanes), jnp.float32)
                for behind in range(length):
                    turn = j * behind % length * 4
                    exact = {0: (1.0, 0.0), 1: (0.0, 1.0), 2: (-1.0, 0.0), 3: (0.0, -1.0)}
                    if turn % length == 0:
                        weight = exact[turn // length][part]
                    else:
                        angle = 2.0 * math.pi * j * behind / length
                        weight = (math.cos(angle), math.sin(angle))[part]
                    if weight == 1.0:
                        value = value + scaled[behind]
                    elif weight == -1.0:
                        value = value - scaled[behind]
                    elif weight != 0.0:
                        value = value + weight * scaled[behind]
                rhs.append(value)
            rhs = tuple(rhs)
            for step in range(near_steps):
                distance = 1 << step
                low = tuple(near_ref[species, plane + p, 2 * step] for p in range(parts))
                high = tuple(near_ref[species, plane + p, 2 * step + 1] for p in range(parts))
                down = c_map(lambda p: roll_down(p, distance), rhs)
                up = c_map(lambda p: roll_up(p, distance), rhs)
                rhs = c_add(rhs, c_add(c_mul(low, down), c_mul(high, up)))
            blocks = []
            carry = None
            for block in range(cells // tile):
                rows = slice(block * tile, (block + 1) * tile)
                value = c_map(lambda p: p[rows], rhs)
                if carry is not None:
                    eliminate = tuple(far_ref[species, plane + p, 0, rows] for p in range(parts))
                    value = c_sub(value, c_mul(eliminate, carry))
                blocks.append(value)
                carry = value
            solved = [None] * len(blocks)
            carry = None
            for block in reversed(range(cells // tile)):
                rows = slice(block * tile, (block + 1) * tile)
                inverse = tuple(far_ref[species, plane + p, 1, rows] for p in range(parts))
                value = c_mul(inverse, blocks[block])
                if carry is not None:
                    substitute = tuple(far_ref[species, plane + p, 2, rows] for p in range(parts))
                    value = c_sub(value, c_mul(substitute, carry))
                solved[block] = value[0]
                carry = value
            weight = parts / length
            answer = answer + weight * jnp.concatenate(solved, 0)
            plane += parts
        new_ref[0, species] = answer
        change = answer - mine
        square = change * change
        for block in range(cells // tile):
            total = total + square[block * tile : (block + 1) * tile]
    sum_ref[...] = jnp.sum(total, axis=0, keepdims=True)


def spread_sum(value, axis):
    size = lax.axis_size(axis)
    pieces = [value]
    for step in range(1, size):
        pieces.append(lax.ppermute(value, axis, [(i, (i + step) % size) for i in range(size)]))
    result = pieces[0]
    for piece in pieces[1:]:
        result = result + piece
    return result


def shards(
    forcing,
    initial_state,
    previous,
    zone_diffusion,
    drift_rate,
    column_zone,
    bottom_flag,
    open_faces,
):
    length = lax.axis_size("tm")
    cells, lanes = open_faces.shape
    corners = [
        lax.ppermute(previous[0], "tm", [(length - 1, target)]) for target in range(length - 1)
    ]
    loads = [forcing]
    for step in range(1, length):
        loads.append(
            lax.ppermute(forcing, "tm", [(i, (i + step) % length) for i in range(length)])
        )
    whole = pl.BlockSpec(memory_space=pltpu.VMEM)
    scalars = pl.BlockSpec(memory_space=pltpu.SMEM)
    count = planes(length)
    near, far = pl.pallas_call(
        functools.partial(factor_kernel, length),
        out_shape=(
            jax.ShapeDtypeStruct((2, count, 2 * near_steps, cells, lanes), jnp.float32),
            jax.ShapeDtypeStruct((2, count, 3, cells, lanes), jnp.float32),
        ),
        in_specs=[scalars, scalars, whole, whole, whole],
        out_specs=(whole, whole),
        compiler_params=pltpu.CompilerParams(vmem_limit_bytes=40 * 1024 * 1024),
        cost_estimate=pl.CostEstimate(flops=4000000, bytes_accessed=3000000, transcendentals=0),
        name="factor_lines",
    )(zone_diffusion, drift_rate, column_zone[None], bottom_flag[None], open_faces)
    new_iterate, squares = pl.pallas_call(
        functools.partial(sweep_kernel, length, length - 1, len(corners)),
        out_shape=(
            jax.ShapeDtypeStruct(forcing.shape, jnp.float32),
            jax.ShapeDtypeStruct((1, lanes), jnp.float32),
        ),
        in_specs=[whole] * (length + len(corners) + 4),
        out_specs=(whole, whole),
        compiler_params=pltpu.CompilerParams(vmem_limit_bytes=40 * 1024 * 1024),
        cost_estimate=pl.CostEstimate(flops=4000000, bytes_accessed=3000000, transcendentals=0),
        name="solve_lines",
    )(*loads, *corners, initial_state, previous, near, far)
    total = jnp.sum(spread_sum(spread_sum(squares, "tm"), "space"))
    entry_count = length * forcing.shape[1] * cells * lanes * lax.axis_size("space")
    return (new_iterate, jnp.sqrt(total / entry_count))


def solution(mesh):
    placed = (
        P("tm", None, None, "space"),
        P(None, None, "space"),
        P("tm", None, None, "space"),
        P(),
        P(),
        P("space"),
        P("space"),
        P(None, "space"),
    )
    return jax.shard_map(
        shards,
        mesh=mesh,
        in_specs=placed,
        out_specs=(P("tm", None, None, "space"), P()),
        check_vma=False,
    )
```

```python
import functools
import math

import jax
import jax.numpy as jnp
from jax import lax
from jax.experimental import pallas as pl
from jax.experimental.pallas import tpu as pltpu
from jax.sharding import PartitionSpec as P

alpha_corner = 0.3
tile = 8
near_steps = 3


def roll_down(block, distance):
    return pltpu.roll(block, distance, 0)


def roll_up(block, distance):
    return pltpu.roll(block, block.shape[0] - distance, 0)


def c_mul(x, y):
    if len(x) == 1 and len(y) == 1:
        return (x[0] * y[0],)
    if len(x) == 1:
        return (x[0] * y[0], x[0] * y[1])
    if len(y) == 1:
        return (x[0] * y[0], x[1] * y[0])
    return (x[0] * y[0] - x[1] * y[1], x[0] * y[1] + x[1] * y[0])


def c_add(x, y):
    return tuple(p + q for p, q in zip(x, y))


def c_sub(x, y):
    return tuple(p - q for p, q in zip(x, y))


def c_neg(x):
    return tuple(-p for p in x)


def c_inverse(x):
    if len(x) == 1:
        return (1.0 / x[0],)
    scale = 1.0 / (x[0] * x[0] + x[1] * x[1])
    return (x[0] * scale, -x[1] * scale)


def c_map(f, x):
    return tuple(f(p) for p in x)


def frequencies(length):
    root = math.exp(math.log(alpha_corner) / length)
    listed = []
    for j in range(length // 2 + 1):
        angle = 2.0 * math.pi * j / length
        if j == 0 or 2 * j == length:
            listed.append((j, (1.0 - root * math.cos(angle),)))
        else:
            listed.append((j, (1.0 - root * math.cos(angle), root * math.sin(angle))))
    return listed


def planes(length):
    return sum(len(shift) for unused, shift in frequencies(length))


def factor_kernel(
    length,
    zones_hbm,
    drift_hbm,
    zone_hbm,
    flag_hbm,
    faces_hbm,
    forcing_hbm,
    previous_hbm,
    initial_hbm,
    near_ref,
    far_ref,
    forcing_ref,
    previous_ref,
    initial_ref,
    zones_ref,
    drift_ref,
    zone_ref,
    flag_ref,
    faces_ref,
    sems,
):
    pairs = (
        (faces_hbm, faces_ref),
        (zones_hbm, zones_ref),
        (drift_hbm, drift_ref),
        (zone_hbm, zone_ref),
        (flag_hbm, flag_ref),
        (forcing_hbm, forcing_ref),
        (previous_hbm, previous_ref),
        (initial_hbm, initial_ref),
    )
    copies = [
        pltpu.make_async_copy(source, target, sems.at[index])
        for index, (source, target) in enumerate(pairs)
    ]
    for copy in copies:
        copy.start()
    for copy in copies[:5]:
        copy.wait()
    cells, lanes = faces_ref.shape
    faces = faces_ref[...].astype(jnp.float32)
    row = lax.broadcasted_iota(jnp.int32, (cells, lanes), 0)
    link_above = jnp.where(row == cells - 1, 0.0, faces)
    link_below = jnp.where(row == 0, 0.0, roll_down(faces, 1))
    ground = jnp.where(row == 0, flag_ref[...].astype(jnp.float32), 0.0)
    zone = zone_ref[...]
    for species in range(2):
        diffusion = jnp.zeros(zone.shape, jnp.float32)
        for index in range(zones_ref.shape[1]):
            diffusion = jnp.where(zone == index, zones_ref[species, index], diffusion)
        drift = drift_ref[species]
        below = -(diffusion + drift) * link_below
        above = -diffusion * link_above
        centre = diffusion * (link_below + link_above) + drift + 2.0 * diffusion * ground
        plane = 0
        for unused, shift in frequencies(length):
            parts = len(shift)
            a = (below,)
            c = (above,)
            b = (centre + shift[0],)
            if parts == 2:
                b = b + (jnp.full_like(centre, shift[1]),)
            for step in range(near_steps):
                distance = 1 << step
                inverse = c_inverse(b)
                low = c_neg(c_mul(a, c_map(lambda p: roll_down(p, distance), inverse)))
                high = c_neg(c_mul(c, c_map(lambda p: roll_up(p, distance), inverse)))
                down_c = c_map(lambda p: roll_down(p, distance), c)
                up_a = c_map(lambda p: roll_up(p, distance), a)
                b = c_add(b, c_add(c_mul(low, down_c), c_mul(high, up_a)))
                a = c_mul(low, c_map(lambda p: roll_down(p, distance), a))
                c = c_mul(high, c_map(lambda p: roll_up(p, distance), c))
                for part in range(parts):
                    near_ref[species, plane + part, 2 * step] = low[part]
                    near_ref[species, plane + part, 2 * step + 1] = high[part]
            carry = None
            for block in range(cells // tile):
                rows = slice(block * tile, (block + 1) * tile)
                ak, bk, ck = (c_map(lambda p: p[rows], item) for item in (a, b, c))
                if carry is None:
                    eliminate = c_map(jnp.zeros_like, ak)
                else:
                    eliminate = c_mul(ak, carry[0])
                    bk = c_sub(bk, c_mul(eliminate, carry[1]))
                inverse = c_inverse(bk)
                substitute = c_mul(ck, inverse)
                for part in range(parts):
                    far_ref[species, plane + part, 0, rows] = eliminate[part]
                    far_ref[species, plane + part, 1, rows] = inverse[part]
                    far_ref[species, plane + part, 2, rows] = substitute[part]
                carry = (inverse, ck)
            plane += parts
    for copy in copies[5:]:
        copy.wait()


def sweep_kernel(length, *refs):
    loads = refs[:length]
    befores = refs[length : 2 * length]
    initial_ref, near_ref, far_ref, new_ref, sum_ref = refs[2 * length :]
    cells, lanes = initial_ref.shape[1:]
    me = lax.axis_index("tm")
    total = jnp.zeros((tile, lanes), jnp.float32)
    for species in range(2):
        mine = befores[0][0, species]
        last = mine
        for behind in range(1, length):
            last = jnp.where(me == (behind + length - 1) % length, befores[behind][0, species], last)
        correction = initial_ref[species] - alpha_corner * last
        scaled = []
        for behind in range(length):
            factor = math.exp(-math.log(alpha_corner) * behind / length)
            load = loads[behind][0, species]
            load = jnp.where(me == behind, load + correction, load)
            scaled.append(load * jnp.where(me < behind, alpha_corner * factor, factor))
        answer = jnp.zeros((cells, lanes), jnp.float32)
        plane = 0
        for j, shift in frequencies(length):
            parts = len(shift)
            rhs = []
            for part in range(parts):
                value = jnp.zeros((cells, lanes), jnp.float32)
                for behind in range(length):
                    turn = j * behind % length * 4
                    exact = {0: (1.0, 0.0), 1: (0.0, 1.0), 2: (-1.0, 0.0), 3: (0.0, -1.0)}
                    if turn % length == 0:
                        weight = exact[turn // length][part]
                    else:
                        angle = 2.0 * math.pi * j * behind / length
                        weight = (math.cos(angle), math.sin(angle))[part]
                    if weight == 1.0:
                        value = value + scaled[behind]
                    elif weight == -1.0:
                        value = value - scaled[behind]
                    elif weight != 0.0:
                        value = value + weight * scaled[behind]
                rhs.append(value)
            rhs = tuple(rhs)
            for step in range(near_steps):
                distance = 1 << step
                low = tuple(near_ref[species, plane + p, 2 * step] for p in range(parts))
                high = tuple(near_ref[species, plane + p, 2 * step + 1] for p in range(parts))
                down = c_map(lambda p: roll_down(p, distance), rhs)
                up = c_map(lambda p: roll_up(p, distance), rhs)
                rhs = c_add(rhs, c_add(c_mul(low, down), c_mul(high, up)))
            blocks = []
            carry = None
            for block in range(cells // tile):
                rows = slice(block * tile, (block + 1) * tile)
                value = c_map(lambda p: p[rows], rhs)
                if carry is not None:
                    eliminate = tuple(far_ref[species, plane + p, 0, rows] for p in range(parts))
                    value = c_sub(value, c_mul(eliminate, carry))
                blocks.append(value)
                carry = value
            solved = [None] * len(blocks)
            carry = None
            for block in reversed(range(cells // tile)):
                rows = slice(block * tile, (block + 1) * tile)
                inverse = tuple(far_ref[species, plane + p, 1, rows] for p in range(parts))
                value = c_mul(inverse, blocks[block])
                if carry is not None:
                    substitute = tuple(far_ref[species, plane + p, 2, rows] for p in range(parts))
                    value = c_sub(value, c_mul(substitute, carry))
                solved[block] = value[0]
                carry = value
            weight = parts / length
            answer = answer + weight * jnp.concatenate(solved, 0)
            plane += parts
        new_ref[0, species] = answer
        change = answer - mine
        square = change * change
        for block in range(cells // tile):
            total = total + square[block * tile : (block + 1) * tile]
    sum_ref[...] = jnp.broadcast_to(jnp.sum(total, axis=0, keepdims=True), sum_ref.shape)


def shards(
    forcing,
    initial_state,
    previous,
    zone_diffusion,
    drift_rate,
    column_zone,
    bottom_flag,
    open_faces,
):
    length = lax.axis_size("tm")
    cells, lanes = open_faces.shape
    ring = [[(i, (i + step) % length) for i in range(length)] for step in range(length)]
    loads = [lax.ppermute(forcing, "tm", ring[step]) for step in range(1, length)]
    befores = [lax.ppermute(previous, "tm", ring[step]) for step in range(1, length)]
    whole = pl.BlockSpec(memory_space=pltpu.VMEM)
    outside = pl.BlockSpec(memory_space=pltpu.HBM)
    count = planes(length)
    near, far, own_load, own_before, initial = pl.pallas_call(
        functools.partial(factor_kernel, length),
        out_shape=(
            jax.ShapeDtypeStruct((2, count, 2 * near_steps, cells, lanes), jnp.float32),
            jax.ShapeDtypeStruct((2, count, 3, cells, lanes), jnp.float32),
            jax.ShapeDtypeStruct(forcing.shape, jnp.float32),
            jax.ShapeDtypeStruct(previous.shape, jnp.float32),
            jax.ShapeDtypeStruct(initial_state.shape, jnp.float32),
        ),
        in_specs=[outside] * 8,
        out_specs=[whole] * 5,
        scratch_shapes=[
            pltpu.SMEM(zone_diffusion.shape, jnp.float32),
            pltpu.SMEM(drift_rate.shape, jnp.float32),
            pltpu.VMEM((1, lanes), jnp.int32),
            pltpu.VMEM((1, lanes), jnp.int32),
            pltpu.VMEM((cells, lanes), jnp.int32),
            pltpu.SemaphoreType.DMA((8,)),
        ],
        compiler_params=pltpu.CompilerParams(vmem_limit_bytes=40 * 1024 * 1024),
        cost_estimate=pl.CostEstimate(flops=4000000, bytes_accessed=3000000, transcendentals=0),
        name="factor_lines",
    )(
        zone_diffusion,
        drift_rate,
        column_zone[None],
        bottom_flag[None],
        open_faces,
        forcing,
        previous,
        initial_state,
    )
    everyone = length * lax.axis_size("space")
    new_iterate, squares = pl.pallas_call(
        functools.partial(sweep_kernel, length),
        out_shape=(
            jax.ShapeDtypeStruct(forcing.shape, jnp.float32),
            jax.ShapeDtypeStruct((everyone, 1, lanes), jnp.float32),
        ),
        in_specs=[whole] * (2 * length + 3),
        out_specs=(whole, whole),
        compiler_params=pltpu.CompilerParams(vmem_limit_bytes=40 * 1024 * 1024),
        cost_estimate=pl.CostEstimate(flops=4000000, bytes_accessed=3000000, transcendentals=0),
        name="solve_lines",
    )(own_load, *loads, own_before, *befores, initial, near, far)
    squares = lax.all_to_all(squares, ("tm", "space"), 0, 0, tiled=True)
    entry_count = everyone * forcing.shape[1] * cells * lanes
    return (new_iterate, jnp.sqrt(jnp.sum(squares) / entry_count))


def solution(mesh):
    placed = (
        P("tm", None, None, "space"),
        P(None, None, "space"),
        P("tm", None, None, "space"),
        P(),
        P(),
        P("space"),
        P("space"),
        P(None, "space"),
    )
    return jax.shard_map(
        shards,
        mesh=mesh,
        in_specs=placed,
        out_specs=(P("tm", None, None, "space"), P()),
        check_vma=False,
    )
```

```python
import functools
import math

import jax
import jax.numpy as jnp
from jax import lax
from jax.experimental import pallas as pl
from jax.experimental.pallas import tpu as pltpu
from jax.sharding import PartitionSpec as P

alpha_corner = 0.3
tile = 8
near_steps = 3


def roll_down(block, distance):
    return pltpu.roll(block, distance, 0)


def roll_up(block, distance):
    return pltpu.roll(block, block.shape[0] - distance, 0)


def c_mul(x, y):
    if len(x) == 1 and len(y) == 1:
        return (x[0] * y[0],)
    if len(x) == 1:
        return (x[0] * y[0], x[0] * y[1])
    if len(y) == 1:
        return (x[0] * y[0], x[1] * y[0])
    return (x[0] * y[0] - x[1] * y[1], x[0] * y[1] + x[1] * y[0])


def c_add(x, y):
    return tuple(p + q for p, q in zip(x, y))


def c_sub(x, y):
    return tuple(p - q for p, q in zip(x, y))


def c_neg(x):
    return tuple(-p for p in x)


def c_inverse(x):
    if len(x) == 1:
        return (1.0 / x[0],)
    scale = 1.0 / (x[0] * x[0] + x[1] * x[1])
    return (x[0] * scale, -x[1] * scale)


def c_map(f, x):
    return tuple(f(p) for p in x)


def frequencies(length):
    root = math.exp(math.log(alpha_corner) / length)
    listed = []
    for j in range(length // 2 + 1):
        angle = 2.0 * math.pi * j / length
        if j == 0 or 2 * j == length:
            listed.append((j, (1.0 - root * math.cos(angle),)))
        else:
            listed.append((j, (1.0 - root * math.cos(angle), root * math.sin(angle))))
    return listed


def planes(length):
    return sum(len(shift) for unused, shift in frequencies(length))


def turn(j, n, length):
    count = j * n % length
    if 4 * count % length == 0:
        return ((1.0, 0.0), (0.0, 1.0), (-1.0, 0.0), (0.0, -1.0))[4 * count // length]
    angle = 2.0 * math.pi * count / length
    return (math.cos(angle), math.sin(angle))


def weighted(total, weight, value):
    if weight == 0.0:
        return total
    if weight == 1.0:
        term = value
    elif weight == -1.0:
        return -value if total is None else total - value
    else:
        term = weight * value
    return term if total is None else total + term


def stack_kernel(
    forcing_hbm,
    previous_hbm,
    initial_hbm,
    zones_hbm,
    drift_hbm,
    zone_hbm,
    flag_hbm,
    faces_hbm,
    stack_ref,
    initial_ref,
    faces_ref,
    rows_ref,
    zones_ref,
    drift_ref,
    zone_ref,
    flag_ref,
    sems,
):
    pairs = (
        (zones_hbm, zones_ref),
        (drift_hbm, drift_ref),
        (zone_hbm, zone_ref),
        (flag_hbm, flag_ref),
        (forcing_hbm, stack_ref.at[0:1]),
        (previous_hbm, stack_ref.at[1:2]),
        (faces_hbm, faces_ref),
        (initial_hbm, initial_ref),
    )
    copies = [
        pltpu.make_async_copy(source, target, sems.at[index])
        for index, (source, target) in enumerate(pairs)
    ]
    for copy in copies:
        copy.start()
    for copy in copies[:4]:
        copy.wait()
    zone = zone_ref[...]
    for species in range(2):
        diffusion = jnp.zeros(zone.shape, jnp.float32)
        for index in range(zones_ref.shape[1]):
            diffusion = jnp.where(zone == index, zones_ref[species, index], diffusion)
        rows_ref[species : species + 1] = diffusion
        rows_ref[2 + species : 3 + species] = jnp.full(zone.shape, drift_ref[species], jnp.float32)
    rows_ref[4:5] = flag_ref[...].astype(jnp.float32)
    for copy in copies[4:]:
        copy.wait()


def factor_kernel(length, rows_ref, faces_ref, near_ref, far_ref):
    cells, lanes = faces_ref.shape
    faces = faces_ref[...].astype(jnp.float32)
    row = lax.broadcasted_iota(jnp.int32, (cells, lanes), 0)
    link_above = jnp.where(row == cells - 1, 0.0, faces)
    link_below = jnp.where(row == 0, 0.0, roll_down(faces, 1))
    ground = jnp.where(row == 0, rows_ref[4:5], 0.0)
    for species in range(2):
        diffusion = rows_ref[species : species + 1]
        drift = rows_ref[2 + species : 3 + species]
        below = -(diffusion + drift) * link_below
        above = -diffusion * link_above
        centre = diffusion * (link_below + link_above) + drift + 2.0 * diffusion * ground
        plane = 0
        for unused, shift in frequencies(length):
            parts = len(shift)
            a = (below,)
            c = (above,)
            b = (centre + shift[0],)
            if parts == 2:
                b = b + (jnp.full_like(centre, shift[1]),)
            for step in range(near_steps):
                distance = 1 << step
                inverse = c_inverse(b)
                low = c_neg(c_mul(a, c_map(lambda p: roll_down(p, distance), inverse)))
                high = c_neg(c_mul(c, c_map(lambda p: roll_up(p, distance), inverse)))
                down_c = c_map(lambda p: roll_down(p, distance), c)
                up_a = c_map(lambda p: roll_up(p, distance), a)
                b = c_add(b, c_add(c_mul(low, down_c), c_mul(high, up_a)))
                a = c_mul(low, c_map(lambda p: roll_down(p, distance), a))
                c = c_mul(high, c_map(lambda p: roll_up(p, distance), c))
                for part in range(parts):
                    near_ref[species, plane + part, 2 * step] = low[part]
                    near_ref[species, plane + part, 2 * step + 1] = high[part]
            carry = None
            for block in range(cells // tile):
                rows = slice(block * tile, (block + 1) * tile)
                ak, bk, ck = (c_map(lambda p: p[rows], item) for item in (a, b, c))
                if carry is None:
                    eliminate = c_map(jnp.zeros_like, ak)
                else:
                    eliminate = c_mul(ak, carry[0])
                    bk = c_sub(bk, c_mul(eliminate, carry[1]))
                inverse = c_inverse(bk)
                substitute = c_mul(ck, inverse)
                for part in range(parts):
                    far_ref[species, plane + part, 0, rows] = eliminate[part]
                    far_ref[species, plane + part, 1, rows] = inverse[part]
                    far_ref[species, plane + part, 2, rows] = substitute[part]
                carry = (inverse, ck)
            plane += parts


def in_order(me, held):
    bit = 1
    while bit < len(held):
        swap = (me & bit) != 0
        held = [
            jnp.where(swap, held[index ^ bit], held[index]) for index in range(len(held))
        ]
        bit *= 2
    return held


def sweep_kernel(length, *refs):
    stacks = refs[:length]
    initial_ref, near_ref, far_ref, new_ref, sum_ref = refs[length:]
    cells, lanes = initial_ref.shape[1:]
    log_alpha = math.log(alpha_corner)
    me = lax.axis_index("tm")
    total = jnp.zeros((tile, lanes), jnp.float32)
    for species in range(2):
        loads = in_order(me, [ref[0, species] for ref in stacks])
        befores = in_order(me, [ref[1, species] for ref in stacks])
        loads[0] = loads[0] + (initial_ref[species] - alpha_corner * befores[length - 1])
        scaled = [math.exp(log_alpha * n / length) * load for n, load in enumerate(loads)]
        spectrum = []
        plane = 0
        for j, shift in frequencies(length):
            parts = len(shift)
            rhs = [None] * parts
            for n in range(length):
                weights = turn(j, -n, length)
                for part in range(parts):
                    rhs[part] = weighted(rhs[part], weights[part], scaled[n])
            rhs = tuple(rhs)
            for step in range(near_steps):
                distance = 1 << step
                low = tuple(near_ref[species, plane + p, 2 * step] for p in range(parts))
                high = tuple(near_ref[species, plane + p, 2 * step + 1] for p in range(parts))
                down = c_map(lambda p: roll_down(p, distance), rhs)
                up = c_map(lambda p: roll_up(p, distance), rhs)
                rhs = c_add(rhs, c_add(c_mul(low, down), c_mul(high, up)))
            blocks = []
            carry = None
            for block in range(cells // tile):
                rows = slice(block * tile, (block + 1) * tile)
                value = c_map(lambda p: p[rows], rhs)
                if carry is not None:
                    eliminate = tuple(far_ref[species, plane + p, 0, rows] for p in range(parts))
                    value = c_sub(value, c_mul(eliminate, carry))
                blocks.append(value)
                carry = value
            solved = [None] * len(blocks)
            carry = None
            for block in reversed(range(cells // tile)):
                rows = slice(block * tile, (block + 1) * tile)
                inverse = tuple(far_ref[species, plane + p, 1, rows] for p in range(parts))
                value = c_mul(inverse, blocks[block])
                if carry is not None:
                    substitute = tuple(far_ref[species, plane + p, 2, rows] for p in range(parts))
                    value = c_sub(value, c_mul(substitute, carry))
                solved[block] = value
                carry = value
            spectrum.append((j, parts, solved))
            plane += parts
        for block in range(cells // tile):
            rows = slice(block * tile, (block + 1) * tile)
            mine = None
            for n in range(length):
                fresh = None
                for j, parts, solved in spectrum:
                    weights = turn(j, n, length)
                    fresh = weighted(fresh, parts * weights[0], solved[block][0])
                    if parts == 2:
                        fresh = weighted(fresh, -parts * weights[1], solved[block][1])
                fresh = fresh * (math.exp(-log_alpha * n / length) / length)
                mine = fresh if mine is None else jnp.where(me == n, fresh, mine)
                change = fresh - befores[n][rows]
                total = total + change * change
            new_ref[0, species, rows] = mine
    sum_ref[...] = jnp.broadcast_to(jnp.sum(total, axis=0, keepdims=True), sum_ref.shape)


def shards(
    forcing,
    initial_state,
    previous,
    zone_diffusion,
    drift_rate,
    column_zone,
    bottom_flag,
    open_faces,
):
    length = lax.axis_size("tm")
    space = lax.axis_size("space")
    cells, lanes = open_faces.shape
    whole = pl.BlockSpec(memory_space=pltpu.VMEM)
    outside = pl.BlockSpec(memory_space=pltpu.HBM)
    count = planes(length)
    params = pltpu.CompilerParams(vmem_limit_bytes=40 * 1024 * 1024)
    stack, initial, faces, rows = pl.pallas_call(
        stack_kernel,
        out_shape=(
            pltpu.VMEM((2,) + forcing.shape[1:], jnp.float32),
            pltpu.VMEM(initial_state.shape, jnp.float32),
            pltpu.VMEM(open_faces.shape, jnp.int32),
            pltpu.VMEM((tile, lanes), jnp.float32),
        ),
        in_specs=[outside] * 8,
        out_specs=[whole] * 4,
        scratch_shapes=[
            pltpu.SMEM(zone_diffusion.shape, jnp.float32),
            pltpu.SMEM(drift_rate.shape, jnp.float32),
            pltpu.VMEM((1, lanes), jnp.int32),
            pltpu.VMEM((1, lanes), jnp.int32),
            pltpu.SemaphoreType.DMA((8,)),
        ],
        compiler_params=pltpu.CompilerParams(vmem_limit_bytes=62 * 1024 * 1024),
        cost_estimate=pl.CostEstimate(flops=4000, bytes_accessed=500000, transcendentals=0),
        name="stack_arrays",
    )(
        forcing,
        previous,
        initial_state,
        zone_diffusion,
        drift_rate,
        column_zone[None],
        bottom_flag[None],
        open_faces,
    )
    stacks = [stack]
    for bits in range(1, length):
        stacks.append(lax.ppermute(stack, "tm", [(i, i ^ bits) for i in range(length)]))
    near, far = pl.pallas_call(
        functools.partial(factor_kernel, length),
        out_shape=(
            jax.ShapeDtypeStruct((2, count, 2 * near_steps, cells, lanes), jnp.float32),
            jax.ShapeDtypeStruct((2, count, 3, cells, lanes), jnp.float32),
        ),
        in_specs=[whole] * 2,
        out_specs=[whole] * 2,
        compiler_params=params,
        cost_estimate=pl.CostEstimate(flops=4000000, bytes_accessed=3000000, transcendentals=0),
        name="factor_lines",
    )(rows, faces)
    new_iterate, squares = pl.pallas_call(
        functools.partial(sweep_kernel, length),
        out_shape=(
            jax.ShapeDtypeStruct(forcing.shape, jnp.float32),
            jax.ShapeDtypeStruct((space, 1, lanes), jnp.float32),
        ),
        in_specs=[whole] * (length + 3),
        out_specs=(whole, whole),
        compiler_params=params,
        cost_estimate=pl.CostEstimate(flops=4000000, bytes_accessed=3000000, transcendentals=0),
        name="solve_lines",
    )(*stacks, initial, near, far)
    squares = lax.all_to_all(squares, "space", 0, 0, tiled=True)
    entry_count = length * space * forcing.shape[1] * cells * lanes
    return (new_iterate, jnp.sqrt(jnp.sum(squares) / entry_count))


def solution(mesh):
    placed = (
        P("tm", None, None, "space"),
        P(None, None, "space"),
        P("tm", None, None, "space"),
        P(),
        P(),
        P("space"),
        P("space"),
        P(None, "space"),
    )
    return jax.shard_map(
        shards,
        mesh=mesh,
        in_specs=placed,
        out_specs=(P("tm", None, None, "space"), P()),
        check_vma=False,
    )
```

```python
import functools
import math

import jax
import jax.numpy as jnp
from jax import lax
from jax.experimental import pallas as pl
from jax.experimental.pallas import tpu as pltpu
from jax.sharding import PartitionSpec as P

alpha_corner = 0.3
tile = 8
near_steps = 3


def roll_down(block, distance):
    return pltpu.roll(block, distance, 0)


def roll_up(block, distance):
    return pltpu.roll(block, block.shape[0] - distance, 0)


def c_mul(x, y):
    if len(x) == 1 and len(y) == 1:
        return (x[0] * y[0],)
    if len(x) == 1:
        return (x[0] * y[0], x[0] * y[1])
    if len(y) == 1:
        return (x[0] * y[0], x[1] * y[0])
    return (x[0] * y[0] - x[1] * y[1], x[0] * y[1] + x[1] * y[0])


def c_add(x, y):
    return tuple(p + q for p, q in zip(x, y))


def c_sub(x, y):
    return tuple(p - q for p, q in zip(x, y))


def c_neg(x):
    return tuple(-p for p in x)


def c_inverse(x):
    if len(x) == 1:
        return (1.0 / x[0],)
    scale = 1.0 / (x[0] * x[0] + x[1] * x[1])
    return (x[0] * scale, -x[1] * scale)


def c_map(f, x):
    return tuple(f(p) for p in x)


def frequencies(length):
    root = math.exp(math.log(alpha_corner) / length)
    listed = []
    for j in range(length // 2 + 1):
        angle = 2.0 * math.pi * j / length
        if j == 0 or 2 * j == length:
            listed.append((j, (1.0 - root * math.cos(angle),)))
        else:
            listed.append((j, (1.0 - root * math.cos(angle), root * math.sin(angle))))
    return listed


def planes(length):
    return sum(len(shift) for unused, shift in frequencies(length))


def turn(j, n, length):
    count = j * n % length
    if 4 * count % length == 0:
        return ((1.0, 0.0), (0.0, 1.0), (-1.0, 0.0), (0.0, -1.0))[4 * count // length]
    angle = 2.0 * math.pi * count / length
    return (math.cos(angle), math.sin(angle))


def weighted(total, weight, value):
    if weight == 0.0:
        return total
    if weight == 1.0:
        term = value
    elif weight == -1.0:
        return -value if total is None else total - value
    else:
        term = weight * value
    return term if total is None else total + term


def stack_kernel(
    forcing_hbm,
    previous_hbm,
    initial_hbm,
    zones_hbm,
    drift_hbm,
    zone_hbm,
    flag_hbm,
    faces_hbm,
    mine_ref,
    other_ref,
    initial_ref,
    faces_ref,
    rows_ref,
    zones_ref,
    drift_ref,
    zone_ref,
    flag_ref,
    sems,
):
    species = lax.axis_index("tm") % 2
    pairs = (
        (zones_hbm, zones_ref),
        (drift_hbm, drift_ref),
        (zone_hbm, zone_ref),
        (flag_hbm, flag_ref),
        (forcing_hbm.at[0, species], mine_ref.at[0]),
        (previous_hbm.at[0, species], mine_ref.at[1]),
        (forcing_hbm.at[0, 1 - species], other_ref.at[0]),
        (previous_hbm.at[0, 1 - species], other_ref.at[1]),
        (faces_hbm, faces_ref),
        (initial_hbm.at[species], initial_ref),
    )
    copies = [
        pltpu.make_async_copy(source, target, sems.at[index])
        for index, (source, target) in enumerate(pairs)
    ]
    for copy in copies:
        copy.start()
    for copy in copies[:4]:
        copy.wait()
    zone = zone_ref[...]
    diffusion = jnp.zeros(zone.shape, jnp.float32)
    for index in range(zones_ref.shape[1]):
        diffusion = jnp.where(zone == index, zones_ref[species, index], diffusion)
    rows_ref[0:1] = diffusion
    rows_ref[1:2] = jnp.full(zone.shape, drift_ref[species], jnp.float32)
    rows_ref[2:3] = flag_ref[...].astype(jnp.float32)
    for copy in copies[4:]:
        copy.wait()


def factor_kernel(length, rows_ref, faces_ref, near_ref, far_ref):
    cells, lanes = faces_ref.shape
    faces = faces_ref[...].astype(jnp.float32)
    row = lax.broadcasted_iota(jnp.int32, (cells, lanes), 0)
    link_above = jnp.where(row == cells - 1, 0.0, faces)
    link_below = jnp.where(row == 0, 0.0, roll_down(faces, 1))
    ground = jnp.where(row == 0, rows_ref[2:3], 0.0)
    diffusion = rows_ref[0:1]
    drift = rows_ref[1:2]
    below = -(diffusion + drift) * link_below
    above = -diffusion * link_above
    centre = diffusion * (link_below + link_above) + drift + 2.0 * diffusion * ground
    plane = 0
    for unused, shift in frequencies(length):
        parts = len(shift)
        a = (below,)
        c = (above,)
        b = (centre + shift[0],)
        if parts == 2:
            b = b + (jnp.full_like(centre, shift[1]),)
        for step in range(near_steps):
            distance = 1 << step
            inverse = c_inverse(b)
            low = c_neg(c_mul(a, c_map(lambda p: roll_down(p, distance), inverse)))
            high = c_neg(c_mul(c, c_map(lambda p: roll_up(p, distance), inverse)))
            down_c = c_map(lambda p: roll_down(p, distance), c)
            up_a = c_map(lambda p: roll_up(p, distance), a)
            b = c_add(b, c_add(c_mul(low, down_c), c_mul(high, up_a)))
            a = c_mul(low, c_map(lambda p: roll_down(p, distance), a))
            c = c_mul(high, c_map(lambda p: roll_up(p, distance), c))
            for part in range(parts):
                near_ref[plane + part, 2 * step] = low[part]
                near_ref[plane + part, 2 * step + 1] = high[part]
        carry = None
        for block in range(cells // tile):
            rows = slice(block * tile, (block + 1) * tile)
            ak, bk, ck = (c_map(lambda p: p[rows], item) for item in (a, b, c))
            if carry is None:
                eliminate = c_map(jnp.zeros_like, ak)
            else:
                eliminate = c_mul(ak, carry[0])
                bk = c_sub(bk, c_mul(eliminate, carry[1]))
            inverse = c_inverse(bk)
            substitute = c_mul(ck, inverse)
            for part in range(parts):
                far_ref[plane + part, 0, rows] = eliminate[part]
                far_ref[plane + part, 1, rows] = inverse[part]
                far_ref[plane + part, 2, rows] = substitute[part]
            carry = (inverse, ck)
        plane += parts


def in_order(me, held):
    bit = 1
    while bit < len(held):
        swap = (me & bit) != 0
        held = [
            jnp.where(swap, held[index ^ bit], held[index]) for index in range(len(held))
        ]
        bit *= 2
    return held


def sweep_kernel(length, *refs):
    stacks = refs[:length]
    initial_ref, near_ref, far_ref, own_ref, give_ref, sum_ref = refs[length:]
    cells, lanes = initial_ref.shape
    log_alpha = math.log(alpha_corner)
    me = lax.axis_index("tm")
    loads = in_order(me, [ref[0] for ref in stacks])
    befores = in_order(me, [ref[1] for ref in stacks])
    loads[0] = loads[0] + (initial_ref[...] - alpha_corner * befores[length - 1])
    scaled = [math.exp(log_alpha * n / length) * load for n, load in enumerate(loads)]
    spectrum = []
    plane = 0
    for j, shift in frequencies(length):
        parts = len(shift)
        rhs = [None] * parts
        for n in range(length):
            weights = turn(j, -n, length)
            for part in range(parts):
                rhs[part] = weighted(rhs[part], weights[part], scaled[n])
        rhs = tuple(rhs)
        for step in range(near_steps):
            distance = 1 << step
            low = tuple(near_ref[plane + p, 2 * step] for p in range(parts))
            high = tuple(near_ref[plane + p, 2 * step + 1] for p in range(parts))
            down = c_map(lambda p: roll_down(p, distance), rhs)
            up = c_map(lambda p: roll_up(p, distance), rhs)
            rhs = c_add(rhs, c_add(c_mul(low, down), c_mul(high, up)))
        blocks = []
        carry = None
        for block in range(cells // tile):
            rows = slice(block * tile, (block + 1) * tile)
            value = c_map(lambda p: p[rows], rhs)
            if carry is not None:
                eliminate = tuple(far_ref[plane + p, 0, rows] for p in range(parts))
                value = c_sub(value, c_mul(eliminate, carry))
            blocks.append(value)
            carry = value
        solved = [None] * len(blocks)
        carry = None
        for block in reversed(range(cells // tile)):
            rows = slice(block * tile, (block + 1) * tile)
            inverse = tuple(far_ref[plane + p, 1, rows] for p in range(parts))
            value = c_mul(inverse, blocks[block])
            if carry is not None:
                substitute = tuple(far_ref[plane + p, 2, rows] for p in range(parts))
                value = c_sub(value, c_mul(substitute, carry))
            solved[block] = value
            carry = value
        spectrum.append((j, parts, solved))
        plane += parts
    total = jnp.zeros((tile, lanes), jnp.float32)
    for block in range(cells // tile):
        rows = slice(block * tile, (block + 1) * tile)
        steps = []
        for n in range(length):
            fresh = None
            for j, parts, solved in spectrum:
                weights = turn(j, n, length)
                fresh = weighted(fresh, parts * weights[0], solved[block][0])
                if parts == 2:
                    fresh = weighted(fresh, -parts * weights[1], solved[block][1])
            fresh = fresh * (math.exp(-log_alpha * n / length) / length)
            steps.append(fresh)
            change = fresh - befores[n][rows]
            total = total + change * change
        own = steps[0]
        give = steps[1]
        for n in range(1, length):
            own = jnp.where(me == n, steps[n], own)
            give = jnp.where(me == n, steps[n ^ 1], give)
        own_ref[rows] = own
        give_ref[rows] = give
    give_ref[cells:] = total
    sum_ref[...] = total


def join_kernel(own_ref, got_ref, new_hbm, sems):
    species = lax.axis_index("tm") % 2
    cells = own_ref.shape[0]
    copies = (
        pltpu.make_async_copy(own_ref, new_hbm.at[0, species], sems.at[0]),
        pltpu.make_async_copy(got_ref.at[:cells], new_hbm.at[0, 1 - species], sems.at[1]),
    )
    for copy in copies:
        copy.start()
    for copy in copies:
        copy.wait()


def exchange(value, axis, bits):
    pairs = [(index, index ^ bits) for index in range(lax.axis_size(axis))]
    return lax.ppermute(value, axis, pairs)


def shards(
    forcing,
    initial_state,
    previous,
    zone_diffusion,
    drift_rate,
    column_zone,
    bottom_flag,
    open_faces,
):
    length = lax.axis_size("tm")
    space = lax.axis_size("space")
    cells, lanes = open_faces.shape
    whole = pl.BlockSpec(memory_space=pltpu.VMEM)
    outside = pl.BlockSpec(memory_space=pltpu.HBM)
    count = planes(length)
    params = pltpu.CompilerParams(vmem_limit_bytes=40 * 1024 * 1024)
    mine, other, initial, faces, rows = pl.pallas_call(
        stack_kernel,
        out_shape=(
            pltpu.VMEM((2, cells, lanes), jnp.float32),
            pltpu.VMEM((2, cells, lanes), jnp.float32),
            pltpu.VMEM((cells, lanes), jnp.float32),
            pltpu.VMEM((cells, lanes), jnp.int32),
            pltpu.VMEM((tile, lanes), jnp.float32),
        ),
        in_specs=[outside] * 8,
        out_specs=[whole] * 5,
        scratch_shapes=[
            pltpu.SMEM(zone_diffusion.shape, jnp.float32),
            pltpu.SMEM(drift_rate.shape, jnp.float32),
            pltpu.VMEM((1, lanes), jnp.int32),
            pltpu.VMEM((1, lanes), jnp.int32),
            pltpu.SemaphoreType.DMA((10,)),
        ],
        compiler_params=pltpu.CompilerParams(vmem_limit_bytes=62 * 1024 * 1024),
        cost_estimate=pl.CostEstimate(flops=4000, bytes_accessed=500000, transcendentals=0),
        name="stack_arrays",
    )(
        forcing,
        previous,
        initial_state,
        zone_diffusion,
        drift_rate,
        column_zone[None],
        bottom_flag[None],
        open_faces,
    )
    stacks = [mine]
    for bits in range(1, length):
        stacks.append(exchange(other if bits % 2 else mine, "tm", bits))
    near, far = pl.pallas_call(
        functools.partial(factor_kernel, length),
        out_shape=(
            jax.ShapeDtypeStruct((count, 2 * near_steps, cells, lanes), jnp.float32),
            jax.ShapeDtypeStruct((count, 3, cells, lanes), jnp.float32),
        ),
        in_specs=[whole] * 2,
        out_specs=[whole] * 2,
        compiler_params=params,
        cost_estimate=pl.CostEstimate(flops=4000000, bytes_accessed=3000000, transcendentals=0),
        name="factor_lines",
    )(rows, faces)
    own, give, squares = pl.pallas_call(
        functools.partial(sweep_kernel, length),
        out_shape=(
            pltpu.VMEM((cells, lanes), jnp.float32),
            pltpu.VMEM((cells + tile, lanes), jnp.float32),
            pltpu.VMEM((tile, lanes), jnp.float32),
        ),
        in_specs=[whole] * (length + 3),
        out_specs=[whole] * 3,
        compiler_params=params,
        cost_estimate=pl.CostEstimate(flops=4000000, bytes_accessed=3000000, transcendentals=0),
        name="solve_lines",
    )(*stacks, initial, near, far)
    got = exchange(give, "tm", 1)
    new_iterate = pl.pallas_call(
        join_kernel,
        out_shape=jax.ShapeDtypeStruct(forcing.shape, jnp.float32),
        in_specs=[whole] * 2,
        out_specs=outside,
        scratch_shapes=[pltpu.SemaphoreType.DMA((2,))],
        compiler_params=params,
        cost_estimate=pl.CostEstimate(flops=4000, bytes_accessed=100000, transcendentals=0),
        name="join_species",
    )(own, got)
    squares = squares + got[cells:]
    bits = 1
    while bits < space:
        squares = squares + exchange(squares, "space", bits)
        bits *= 2
    entry_count = length * space * forcing.shape[1] * cells * lanes
    return (new_iterate, jnp.sqrt(jnp.sum(squares) / entry_count))


def solution(mesh):
    placed = (
        P("tm", None, None, "space"),
        P(None, None, "space"),
        P("tm", None, None, "space"),
        P(),
        P(),
        P("space"),
        P("space"),
        P(None, "space"),
    )
    return jax.shard_map(
        shards,
        mesh=mesh,
        in_specs=placed,
        out_specs=(P("tm", None, None, "space"), P()),
        check_vma=False,
    )
```

```python
import functools
import math

import jax
import jax.numpy as jnp
from jax import lax
from jax.experimental import pallas as pl
from jax.experimental.pallas import tpu as pltpu
from jax.sharding import PartitionSpec as P

alpha_corner = 0.3
tile = 8
near_steps = 3


def roll_down(block, distance):
    return pltpu.roll(block, distance, 0)


def roll_up(block, distance):
    return pltpu.roll(block, block.shape[0] - distance, 0)


def c_mul(x, y):
    if len(x) == 1 and len(y) == 1:
        return (x[0] * y[0],)
    if len(x) == 1:
        return (x[0] * y[0], x[0] * y[1])
    if len(y) == 1:
        return (x[0] * y[0], x[1] * y[0])
    return (x[0] * y[0] - x[1] * y[1], x[0] * y[1] + x[1] * y[0])


def c_add(x, y):
    return tuple(p + q for p, q in zip(x, y))


def c_sub(x, y):
    return tuple(p - q for p, q in zip(x, y))


def c_neg(x):
    return tuple(-p for p in x)


def c_inverse(x):
    if len(x) == 1:
        return (1.0 / x[0],)
    scale = 1.0 / (x[0] * x[0] + x[1] * x[1])
    return (x[0] * scale, -x[1] * scale)


def c_map(f, x):
    return tuple(f(p) for p in x)


def frequencies(length):
    root = math.exp(math.log(alpha_corner) / length)
    listed = []
    for j in range(length // 2 + 1):
        angle = 2.0 * math.pi * j / length
        if j == 0 or 2 * j == length:
            listed.append((j, (1.0 - root * math.cos(angle),)))
        else:
            listed.append((j, (1.0 - root * math.cos(angle), root * math.sin(angle))))
    return listed


def planes(length):
    return sum(len(shift) for unused, shift in frequencies(length))


def turn(j, n, length):
    count = j * n % length
    if 4 * count % length == 0:
        return ((1.0, 0.0), (0.0, 1.0), (-1.0, 0.0), (0.0, -1.0))[4 * count // length]
    angle = 2.0 * math.pi * count / length
    return (math.cos(angle), math.sin(angle))


def weighted(total, weight, value):
    if weight == 0.0:
        return total
    if weight == 1.0:
        term = value
    elif weight == -1.0:
        return -value if total is None else total - value
    else:
        term = weight * value
    return term if total is None else total + term


def stack_kernel(
    forcing_hbm,
    previous_hbm,
    initial_hbm,
    zones_hbm,
    drift_hbm,
    zone_hbm,
    flag_hbm,
    faces_hbm,
    mine_ref,
    other_ref,
    initial_ref,
    faces_ref,
    rows_ref,
    zones_ref,
    drift_ref,
    zone_ref,
    flag_ref,
    sems,
):
    species = lax.axis_index("tm") % 2
    pairs = (
        (zones_hbm, zones_ref),
        (drift_hbm, drift_ref),
        (zone_hbm, zone_ref),
        (flag_hbm, flag_ref),
        (forcing_hbm.at[0, species], mine_ref.at[0]),
        (previous_hbm.at[0, species], mine_ref.at[1]),
        (forcing_hbm.at[0, 1 - species], other_ref.at[0]),
        (previous_hbm.at[0, 1 - species], other_ref.at[1]),
        (faces_hbm, faces_ref),
        (initial_hbm.at[species], initial_ref),
    )
    copies = [
        pltpu.make_async_copy(source, target, sems.at[index])
        for index, (source, target) in enumerate(pairs)
    ]
    for copy in copies:
        copy.start()
    for copy in copies[:4]:
        copy.wait()
    zone = zone_ref[...]
    diffusion = jnp.zeros(zone.shape, jnp.float32)
    for index in range(zones_ref.shape[1]):
        diffusion = jnp.where(zone == index, zones_ref[species, index], diffusion)
    rows_ref[0:1] = diffusion
    rows_ref[1:2] = jnp.full(zone.shape, drift_ref[species], jnp.float32)
    rows_ref[2:3] = flag_ref[...].astype(jnp.float32)
    for copy in copies[4:]:
        copy.wait()


def factor_kernel(length, rows_ref, faces_ref, near_ref, far_ref):
    cells, lanes = faces_ref.shape
    faces = faces_ref[...].astype(jnp.float32)
    row = lax.broadcasted_iota(jnp.int32, (cells, lanes), 0)
    link_above = jnp.where(row == cells - 1, 0.0, faces)
    link_below = jnp.where(row == 0, 0.0, roll_down(faces, 1))
    ground = jnp.where(row == 0, rows_ref[2:3], 0.0)
    diffusion = rows_ref[0:1]
    drift = rows_ref[1:2]
    below = -(diffusion + drift) * link_below
    above = -diffusion * link_above
    centre = diffusion * (link_below + link_above) + drift + 2.0 * diffusion * ground
    plane = 0
    for unused, shift in frequencies(length):
        parts = len(shift)
        a = (below,)
        c = (above,)
        b = (centre + shift[0],)
        if parts == 2:
            b = b + (jnp.full_like(centre, shift[1]),)
        for step in range(near_steps):
            distance = 1 << step
            inverse = c_inverse(b)
            low = c_neg(c_mul(a, c_map(lambda p: roll_down(p, distance), inverse)))
            high = c_neg(c_mul(c, c_map(lambda p: roll_up(p, distance), inverse)))
            down_c = c_map(lambda p: roll_down(p, distance), c)
            up_a = c_map(lambda p: roll_up(p, distance), a)
            b = c_add(b, c_add(c_mul(low, down_c), c_mul(high, up_a)))
            a = c_mul(low, c_map(lambda p: roll_down(p, distance), a))
            c = c_mul(high, c_map(lambda p: roll_up(p, distance), c))
            for part in range(parts):
                near_ref[plane + part, 2 * step] = low[part]
                near_ref[plane + part, 2 * step + 1] = high[part]
        carry = None
        for block in range(cells // tile):
            rows = slice(block * tile, (block + 1) * tile)
            ak, bk, ck = (c_map(lambda p: p[rows], item) for item in (a, b, c))
            if carry is None:
                eliminate = c_map(jnp.zeros_like, ak)
            else:
                eliminate = c_mul(ak, carry[0])
                bk = c_sub(bk, c_mul(eliminate, carry[1]))
            inverse = c_inverse(bk)
            substitute = c_mul(ck, inverse)
            for part in range(parts):
                far_ref[plane + part, 0, rows] = eliminate[part]
                far_ref[plane + part, 1, rows] = inverse[part]
                far_ref[plane + part, 2, rows] = substitute[part]
            carry = (inverse, ck)
        plane += parts


def in_order(me, held):
    bit = 1
    while bit < len(held):
        swap = (me & bit) != 0
        held = [
            jnp.where(swap, held[index ^ bit], held[index]) for index in range(len(held))
        ]
        bit *= 2
    return held


def sweep_kernel(length, *refs):
    stacks = refs[:length]
    initial_ref, near_ref, far_ref, own_ref, give_ref, sum_ref = refs[length:]
    cells, lanes = initial_ref.shape
    log_alpha = math.log(alpha_corner)
    me = lax.axis_index("tm")
    loads = in_order(me, [ref[0] for ref in stacks])
    befores = in_order(me, [ref[1] for ref in stacks])
    loads[0] = loads[0] + (initial_ref[...] - alpha_corner * befores[length - 1])
    scaled = [math.exp(log_alpha * n / length) * load for n, load in enumerate(loads)]
    spectrum = []
    plane = 0
    for j, shift in frequencies(length):
        parts = len(shift)
        rhs = [None] * parts
        for n in range(length):
            weights = turn(j, -n, length)
            for part in range(parts):
                rhs[part] = weighted(rhs[part], weights[part], scaled[n])
        rhs = tuple(rhs)
        for step in range(near_steps):
            distance = 1 << step
            low = tuple(near_ref[plane + p, 2 * step] for p in range(parts))
            high = tuple(near_ref[plane + p, 2 * step + 1] for p in range(parts))
            down = c_map(lambda p: roll_down(p, distance), rhs)
            up = c_map(lambda p: roll_up(p, distance), rhs)
            rhs = c_add(rhs, c_add(c_mul(low, down), c_mul(high, up)))
        blocks = []
        carry = None
        for block in range(cells // tile):
            rows = slice(block * tile, (block + 1) * tile)
            value = c_map(lambda p: p[rows], rhs)
            if carry is not None:
                eliminate = tuple(far_ref[plane + p, 0, rows] for p in range(parts))
                value = c_sub(value, c_mul(eliminate, carry))
            blocks.append(value)
            carry = value
        solved = [None] * len(blocks)
        carry = None
        for block in reversed(range(cells // tile)):
            rows = slice(block * tile, (block + 1) * tile)
            inverse = tuple(far_ref[plane + p, 1, rows] for p in range(parts))
            value = c_mul(inverse, blocks[block])
            if carry is not None:
                substitute = tuple(far_ref[plane + p, 2, rows] for p in range(parts))
                value = c_sub(value, c_mul(substitute, carry))
            solved[block] = value
            carry = value
        spectrum.append((j, parts, solved))
        plane += parts
    total = jnp.zeros((tile, lanes), jnp.float32)
    for block in range(cells // tile):
        rows = slice(block * tile, (block + 1) * tile)
        steps = []
        for n in range(length):
            fresh = None
            for j, parts, solved in spectrum:
                weights = turn(j, n, length)
                fresh = weighted(fresh, parts * weights[0], solved[block][0])
                if parts == 2:
                    fresh = weighted(fresh, -parts * weights[1], solved[block][1])
            fresh = fresh * (math.exp(-log_alpha * n / length) / length)
            steps.append(fresh)
            change = fresh - befores[n][rows]
            total = total + change * change
        own = steps[0]
        give = steps[1]
        for n in range(1, length):
            own = jnp.where(me == n, steps[n], own)
            give = jnp.where(me == n, steps[n ^ 1], give)
        own_ref[rows] = own
        give_ref[rows] = give
    give_ref[cells:] = total
    sum_ref[...] = total


def join_kernel(own_ref, got_ref, new_hbm, sems):
    species = lax.axis_index("tm") % 2
    cells = own_ref.shape[0]
    copies = (
        pltpu.make_async_copy(own_ref, new_hbm.at[0, species], sems.at[0]),
        pltpu.make_async_copy(got_ref.at[:cells], new_hbm.at[0, 1 - species], sems.at[1]),
    )
    for copy in copies:
        copy.start()
    for copy in copies:
        copy.wait()


def exchange(value, axis, bits):
    pairs = [(index, index ^ bits) for index in range(lax.axis_size(axis))]
    return lax.ppermute(value, axis, pairs)


def exchange_odd(value, bits):
    pairs = [(index, index ^ bits) for index in range(1, lax.axis_size("space"), 2)]
    return lax.ppermute(value, "space", pairs)


def shards(
    forcing,
    initial_state,
    previous,
    zone_diffusion,
    drift_rate,
    column_zone,
    bottom_flag,
    open_faces,
):
    length = lax.axis_size("tm")
    space = lax.axis_size("space")
    cells, lanes = open_faces.shape
    whole = pl.BlockSpec(memory_space=pltpu.VMEM)
    outside = pl.BlockSpec(memory_space=pltpu.HBM)
    count = planes(length)
    params = pltpu.CompilerParams(vmem_limit_bytes=40 * 1024 * 1024)
    mine, other, initial, faces, rows = pl.pallas_call(
        stack_kernel,
        out_shape=(
            pltpu.VMEM((2, cells, lanes), jnp.float32),
            pltpu.VMEM((2, cells, lanes), jnp.float32),
            pltpu.VMEM((cells, lanes), jnp.float32),
            pltpu.VMEM((cells, lanes), jnp.int32),
            pltpu.VMEM((tile, lanes), jnp.float32),
        ),
        in_specs=[outside] * 8,
        out_specs=[whole] * 5,
        scratch_shapes=[
            pltpu.SMEM(zone_diffusion.shape, jnp.float32),
            pltpu.SMEM(drift_rate.shape, jnp.float32),
            pltpu.VMEM((1, lanes), jnp.int32),
            pltpu.VMEM((1, lanes), jnp.int32),
            pltpu.SemaphoreType.DMA((10,)),
        ],
        compiler_params=pltpu.CompilerParams(vmem_limit_bytes=62 * 1024 * 1024),
        cost_estimate=pl.CostEstimate(flops=4000, bytes_accessed=500000, transcendentals=0),
        name="stack_arrays",
    )(
        forcing,
        previous,
        initial_state,
        zone_diffusion,
        drift_rate,
        column_zone[None],
        bottom_flag[None],
        open_faces,
    )
    stacks = [mine]
    for bits in range(1, length):
        stacks.append(exchange(other if bits % 2 else mine, "tm", bits))
    near, far = pl.pallas_call(
        functools.partial(factor_kernel, length),
        out_shape=(
            jax.ShapeDtypeStruct((count, 2 * near_steps, cells, lanes), jnp.float32),
            jax.ShapeDtypeStruct((count, 3, cells, lanes), jnp.float32),
        ),
        in_specs=[whole] * 2,
        out_specs=[whole] * 2,
        compiler_params=params,
        cost_estimate=pl.CostEstimate(flops=4000000, bytes_accessed=3000000, transcendentals=0),
        name="factor_lines",
    )(rows, faces)
    own, give, squares = pl.pallas_call(
        functools.partial(sweep_kernel, length),
        out_shape=(
            pltpu.VMEM((cells, lanes), jnp.float32),
            pltpu.VMEM((cells + tile, lanes), jnp.float32),
            pltpu.VMEM((tile, lanes), jnp.float32),
        ),
        in_specs=[whole] * (length + 3),
        out_specs=[whole] * 3,
        compiler_params=params,
        cost_estimate=pl.CostEstimate(flops=4000000, bytes_accessed=3000000, transcendentals=0),
        name="solve_lines",
    )(*stacks, initial, near, far)
    squares = squares + exchange(squares, "space", 1)
    got = exchange(give.at[cells:].set(squares), "tm", 1)
    squares = squares + got[cells:]
    bits = 2
    while bits < space:
        squares = squares + exchange_odd(squares, bits)
        bits *= 2
    odd = lax.axis_index("space") % 2 == 1
    squares = jnp.where(odd, squares, exchange(squares, "space", 1))
    new_iterate = pl.pallas_call(
        join_kernel,
        out_shape=jax.ShapeDtypeStruct(forcing.shape, jnp.float32),
        in_specs=[whole] * 2,
        out_specs=outside,
        scratch_shapes=[pltpu.SemaphoreType.DMA((2,))],
        compiler_params=params,
        cost_estimate=pl.CostEstimate(flops=4000, bytes_accessed=100000, transcendentals=0),
        name="join_species",
    )(own, got)
    entry_count = length * space * forcing.shape[1] * cells * lanes
    return (new_iterate, jnp.sqrt(jnp.sum(squares) / entry_count))


def solution(mesh):
    placed = (
        P("tm", None, None, "space"),
        P(None, None, "space"),
        P("tm", None, None, "space"),
        P(),
        P(),
        P("space"),
        P("space"),
        P(None, "space"),
    )
    return jax.shard_map(
        shards,
        mesh=mesh,
        in_specs=placed,
        out_specs=(P("tm", None, None, "space"), P()),
        check_vma=False,
    )
```

```python
import functools
import math

import jax
import jax.numpy as jnp
from jax import lax
from jax.experimental import pallas as pl
from jax.experimental.pallas import tpu as pltpu
from jax.sharding import PartitionSpec as P

alpha_corner = 0.3
tile = 8
near_steps = 3


def roll_down(block, distance):
    return pltpu.roll(block, distance, 0)


def roll_up(block, distance):
    return pltpu.roll(block, block.shape[0] - distance, 0)


def c_mul(x, y):
    if len(x) == 1 and len(y) == 1:
        return (x[0] * y[0],)
    if len(x) == 1:
        return (x[0] * y[0], x[0] * y[1])
    if len(y) == 1:
        return (x[0] * y[0], x[1] * y[0])
    return (x[0] * y[0] - x[1] * y[1], x[0] * y[1] + x[1] * y[0])


def c_add(x, y):
    return tuple(p + q for p, q in zip(x, y))


def c_sub(x, y):
    return tuple(p - q for p, q in zip(x, y))


def c_neg(x):
    return tuple(-p for p in x)


def c_inverse(x):
    if len(x) == 1:
        return (1.0 / x[0],)
    scale = 1.0 / (x[0] * x[0] + x[1] * x[1])
    return (x[0] * scale, -x[1] * scale)


def c_map(f, x):
    return tuple(f(p) for p in x)


def frequencies(length):
    root = math.exp(math.log(alpha_corner) / length)
    listed = []
    for j in range(length // 2 + 1):
        angle = 2.0 * math.pi * j / length
        if j == 0 or 2 * j == length:
            listed.append((j, (1.0 - root * math.cos(angle),)))
        else:
            listed.append((j, (1.0 - root * math.cos(angle), root * math.sin(angle))))
    return listed


def planes(length):
    return sum(len(shift) for unused, shift in frequencies(length))


def turn(j, n, length):
    count = j * n % length
    if 4 * count % length == 0:
        return ((1.0, 0.0), (0.0, 1.0), (-1.0, 0.0), (0.0, -1.0))[4 * count // length]
    angle = 2.0 * math.pi * count / length
    return (math.cos(angle), math.sin(angle))


def weighted(total, weight, value):
    if weight == 0.0:
        return total
    if weight == 1.0:
        term = value
    elif weight == -1.0:
        return -value if total is None else total - value
    else:
        term = weight * value
    return term if total is None else total + term


def stack_kernel(
    forcing_hbm,
    previous_hbm,
    initial_hbm,
    zones_hbm,
    drift_hbm,
    zone_hbm,
    flag_hbm,
    faces_hbm,
    mine_ref,
    other_ref,
    initial_ref,
    faces_ref,
    rows_ref,
    zones_ref,
    drift_ref,
    zone_ref,
    flag_ref,
    sems,
):
    species = lax.axis_index("tm") % 2
    pairs = (
        (zones_hbm, zones_ref),
        (drift_hbm, drift_ref),
        (zone_hbm, zone_ref),
        (flag_hbm, flag_ref),
        (forcing_hbm.at[0, species], mine_ref.at[0]),
        (previous_hbm.at[0, species], mine_ref.at[1]),
        (forcing_hbm.at[0, 1 - species], other_ref.at[0]),
        (previous_hbm.at[0, 1 - species], other_ref.at[1]),
        (faces_hbm, faces_ref),
        (initial_hbm.at[species], initial_ref),
    )
    copies = [
        pltpu.make_async_copy(source, target, sems.at[index])
        for index, (source, target) in enumerate(pairs)
    ]
    for copy in copies:
        copy.start()
    for copy in copies[:4]:
        copy.wait()
    zone = zone_ref[...]
    diffusion = jnp.zeros(zone.shape, jnp.float32)
    for index in range(zones_ref.shape[1]):
        diffusion = jnp.where(zone == index, zones_ref[species, index], diffusion)
    rows_ref[0:1] = diffusion
    rows_ref[1:2] = jnp.full(zone.shape, drift_ref[species], jnp.float32)
    rows_ref[2:3] = flag_ref[...].astype(jnp.float32)
    for copy in copies[4:]:
        copy.wait()


def factor_kernel(length, rows_ref, faces_ref, near_ref, far_ref):
    cells, lanes = faces_ref.shape
    faces = faces_ref[...].astype(jnp.float32)
    row = lax.broadcasted_iota(jnp.int32, (cells, lanes), 0)
    link_above = jnp.where(row == cells - 1, 0.0, faces)
    link_below = jnp.where(row == 0, 0.0, roll_down(faces, 1))
    ground = jnp.where(row == 0, rows_ref[2:3], 0.0)
    diffusion = rows_ref[0:1]
    drift = rows_ref[1:2]
    below = -(diffusion + drift) * link_below
    above = -diffusion * link_above
    centre = diffusion * (link_below + link_above) + drift + 2.0 * diffusion * ground
    plane = 0
    for unused, shift in frequencies(length):
        parts = len(shift)
        a = (below,)
        c = (above,)
        b = (centre + shift[0],)
        if parts == 2:
            b = b + (jnp.full_like(centre, shift[1]),)
        for step in range(near_steps):
            distance = 1 << step
            inverse = c_inverse(b)
            low = c_neg(c_mul(a, c_map(lambda p: roll_down(p, distance), inverse)))
            high = c_neg(c_mul(c, c_map(lambda p: roll_up(p, distance), inverse)))
            down_c = c_map(lambda p: roll_down(p, distance), c)
            up_a = c_map(lambda p: roll_up(p, distance), a)
            b = c_add(b, c_add(c_mul(low, down_c), c_mul(high, up_a)))
            a = c_mul(low, c_map(lambda p: roll_down(p, distance), a))
            c = c_mul(high, c_map(lambda p: roll_up(p, distance), c))
            for part in range(parts):
                near_ref[plane + part, 2 * step] = low[part]
                near_ref[plane + part, 2 * step + 1] = high[part]
        carry = None
        for block in range(cells // tile):
            rows = slice(block * tile, (block + 1) * tile)
            ak, bk, ck = (c_map(lambda p: p[rows], item) for item in (a, b, c))
            if carry is None:
                eliminate = c_map(jnp.zeros_like, ak)
            else:
                eliminate = c_mul(ak, carry[0])
                bk = c_sub(bk, c_mul(eliminate, carry[1]))
            inverse = c_inverse(bk)
            substitute = c_mul(ck, inverse)
            for part in range(parts):
                far_ref[plane + part, 0, rows] = eliminate[part]
                far_ref[plane + part, 1, rows] = inverse[part]
                far_ref[plane + part, 2, rows] = substitute[part]
            carry = (inverse, ck)
        plane += parts


def in_order(me, held):
    bit = 1
    while bit < len(held):
        swap = (me & bit) != 0
        held = [
            jnp.where(swap, held[index ^ bit], held[index]) for index in range(len(held))
        ]
        bit *= 2
    return held


def sweep_kernel(length, *refs):
    stacks = refs[:length]
    initial_ref, near_ref, far_ref, own_ref, give_ref, sum_ref = refs[length:]
    cells, lanes = initial_ref.shape
    log_alpha = math.log(alpha_corner)
    me = lax.axis_index("tm")
    loads = in_order(me, [ref[0] for ref in stacks])
    befores = in_order(me, [ref[1] for ref in stacks])
    loads[0] = loads[0] + (initial_ref[...] - alpha_corner * befores[length - 1])
    scaled = [math.exp(log_alpha * n / length) * load for n, load in enumerate(loads)]
    spectrum = []
    plane = 0
    for j, shift in frequencies(length):
        parts = len(shift)
        rhs = [None] * parts
        for n in range(length):
            weights = turn(j, -n, length)
            for part in range(parts):
                rhs[part] = weighted(rhs[part], weights[part], scaled[n])
        rhs = tuple(rhs)
        for step in range(near_steps):
            distance = 1 << step
            low = tuple(near_ref[plane + p, 2 * step] for p in range(parts))
            high = tuple(near_ref[plane + p, 2 * step + 1] for p in range(parts))
            down = c_map(lambda p: roll_down(p, distance), rhs)
            up = c_map(lambda p: roll_up(p, distance), rhs)
            rhs = c_add(rhs, c_add(c_mul(low, down), c_mul(high, up)))
        blocks = []
        carry = None
        for block in range(cells // tile):
            rows = slice(block * tile, (block + 1) * tile)
            value = c_map(lambda p: p[rows], rhs)
            if carry is not None:
                eliminate = tuple(far_ref[plane + p, 0, rows] for p in range(parts))
                value = c_sub(value, c_mul(eliminate, carry))
            blocks.append(value)
            carry = value
        solved = [None] * len(blocks)
        carry = None
        for block in reversed(range(cells // tile)):
            rows = slice(block * tile, (block + 1) * tile)
            inverse = tuple(far_ref[plane + p, 1, rows] for p in range(parts))
            value = c_mul(inverse, blocks[block])
            if carry is not None:
                substitute = tuple(far_ref[plane + p, 2, rows] for p in range(parts))
                value = c_sub(value, c_mul(substitute, carry))
            solved[block] = value
            carry = value
        spectrum.append((j, parts, solved))
        plane += parts
    total = jnp.zeros((tile, lanes), jnp.float32)
    for block in range(cells // tile):
        rows = slice(block * tile, (block + 1) * tile)
        steps = []
        for n in range(length):
            fresh = None
            for j, parts, solved in spectrum:
                weights = turn(j, n, length)
                fresh = weighted(fresh, parts * weights[0], solved[block][0])
                if parts == 2:
                    fresh = weighted(fresh, -parts * weights[1], solved[block][1])
            fresh = fresh * (math.exp(-log_alpha * n / length) / length)
            steps.append(fresh)
            change = fresh - befores[n][rows]
            total = total + change * change
        own = steps[0]
        give = steps[1]
        for n in range(1, length):
            own = jnp.where(me == n, steps[n], own)
            give = jnp.where(me == n, steps[n ^ 1], give)
        own_ref[rows] = own
        give_ref[rows] = give
    give_ref[cells:] = total
    sum_ref[...] = total


def join_kernel(own_ref, got_ref, new_hbm, sems):
    species = lax.axis_index("tm") % 2
    cells = own_ref.shape[0]
    copies = (
        pltpu.make_async_copy(own_ref, new_hbm.at[0, species], sems.at[0]),
        pltpu.make_async_copy(got_ref.at[:cells], new_hbm.at[0, 1 - species], sems.at[1]),
    )
    for copy in copies:
        copy.start()
    for copy in copies:
        copy.wait()


def exchange(value, axis, bits):
    pairs = [(index, index ^ bits) for index in range(lax.axis_size(axis))]
    return lax.ppermute(value, axis, pairs)


def exchange_odd(value, bits):
    pairs = [
        (index, index ^ bits if index % 2 else index) for index in range(lax.axis_size("space"))
    ]
    return lax.ppermute(value, "space", pairs)


def shards(
    forcing,
    initial_state,
    previous,
    zone_diffusion,
    drift_rate,
    column_zone,
    bottom_flag,
    open_faces,
):
    length = lax.axis_size("tm")
    space = lax.axis_size("space")
    cells, lanes = open_faces.shape
    whole = pl.BlockSpec(memory_space=pltpu.VMEM)
    outside = pl.BlockSpec(memory_space=pltpu.HBM)
    count = planes(length)
    params = pltpu.CompilerParams(vmem_limit_bytes=40 * 1024 * 1024)
    mine, other, initial, faces, rows = pl.pallas_call(
        stack_kernel,
        out_shape=(
            pltpu.VMEM((2, cells, lanes), jnp.float32),
            pltpu.VMEM((2, cells, lanes), jnp.float32),
            pltpu.VMEM((cells, lanes), jnp.float32),
            pltpu.VMEM((cells, lanes), jnp.int32),
            pltpu.VMEM((tile, lanes), jnp.float32),
        ),
        in_specs=[outside] * 8,
        out_specs=[whole] * 5,
        scratch_shapes=[
            pltpu.SMEM(zone_diffusion.shape, jnp.float32),
            pltpu.SMEM(drift_rate.shape, jnp.float32),
            pltpu.VMEM((1, lanes), jnp.int32),
            pltpu.VMEM((1, lanes), jnp.int32),
            pltpu.SemaphoreType.DMA((10,)),
        ],
        compiler_params=pltpu.CompilerParams(vmem_limit_bytes=62 * 1024 * 1024),
        cost_estimate=pl.CostEstimate(flops=4000, bytes_accessed=500000, transcendentals=0),
        name="stack_arrays",
    )(
        forcing,
        previous,
        initial_state,
        zone_diffusion,
        drift_rate,
        column_zone[None],
        bottom_flag[None],
        open_faces,
    )
    stacks = [mine]
    for bits in range(1, length):
        stacks.append(exchange(other if bits % 2 else mine, "tm", bits))
    near, far = pl.pallas_call(
        functools.partial(factor_kernel, length),
        out_shape=(
            jax.ShapeDtypeStruct((count, 2 * near_steps, cells, lanes), jnp.float32),
            jax.ShapeDtypeStruct((count, 3, cells, lanes), jnp.float32),
        ),
        in_specs=[whole] * 2,
        out_specs=[whole] * 2,
        compiler_params=params,
        cost_estimate=pl.CostEstimate(flops=4000000, bytes_accessed=3000000, transcendentals=0),
        name="factor_lines",
    )(rows, faces)
    own, give, squares = pl.pallas_call(
        functools.partial(sweep_kernel, length),
        out_shape=(
            pltpu.VMEM((cells, lanes), jnp.float32),
            pltpu.VMEM((cells + tile, lanes), jnp.float32),
            pltpu.VMEM((tile, lanes), jnp.float32),
        ),
        in_specs=[whole] * (length + 3),
        out_specs=[whole] * 3,
        compiler_params=params,
        cost_estimate=pl.CostEstimate(flops=4000000, bytes_accessed=3000000, transcendentals=0),
        name="solve_lines",
    )(*stacks, initial, near, far)
    squares = squares + exchange(squares, "space", 1)
    got = exchange(give.at[cells:].set(squares), "tm", 1)
    squares = squares + got[cells:]
    bits = 2
    while bits < space:
        squares = squares + exchange_odd(squares, bits)
        bits *= 2
    odd = lax.axis_index("space") % 2 == 1
    squares = jnp.where(odd, squares, exchange(squares, "space", 1))
    new_iterate = pl.pallas_call(
        join_kernel,
        out_shape=jax.ShapeDtypeStruct(forcing.shape, jnp.float32),
        in_specs=[whole] * 2,
        out_specs=outside,
        scratch_shapes=[pltpu.SemaphoreType.DMA((2,))],
        compiler_params=params,
        cost_estimate=pl.CostEstimate(flops=4000, bytes_accessed=100000, transcendentals=0),
        name="join_species",
    )(own, got)
    entry_count = length * space * forcing.shape[1] * cells * lanes
    return (new_iterate, jnp.sqrt(jnp.sum(squares) / entry_count))


def solution(mesh):
    placed = (
        P("tm", None, None, "space"),
        P(None, None, "space"),
        P("tm", None, None, "space"),
        P(),
        P(),
        P("space"),
        P("space"),
        P(None, "space"),
    )
    return jax.shard_map(
        shards,
        mesh=mesh,
        in_specs=placed,
        out_specs=(P("tm", None, None, "space"), P()),
        check_vma=False,
    )
```

```python
import functools
import math

import jax
import jax.numpy as jnp
from jax import lax
from jax.experimental import pallas as pl
from jax.experimental.pallas import tpu as pltpu
from jax.sharding import PartitionSpec as P

alpha_corner = 0.3
tile = 8
near_steps = 3


def roll_down(block, distance):
    return pltpu.roll(block, distance, 0)


def roll_up(block, distance):
    return pltpu.roll(block, block.shape[0] - distance, 0)


def c_mul(x, y):
    if len(x) == 1 and len(y) == 1:
        return (x[0] * y[0],)
    if len(x) == 1:
        return (x[0] * y[0], x[0] * y[1])
    if len(y) == 1:
        return (x[0] * y[0], x[1] * y[0])
    return (x[0] * y[0] - x[1] * y[1], x[0] * y[1] + x[1] * y[0])


def c_add(x, y):
    return tuple(p + q for p, q in zip(x, y))


def c_sub(x, y):
    return tuple(p - q for p, q in zip(x, y))


def c_neg(x):
    return tuple(-p for p in x)


def c_inverse(x):
    if len(x) == 1:
        return (1.0 / x[0],)
    scale = 1.0 / (x[0] * x[0] + x[1] * x[1])
    return (x[0] * scale, -x[1] * scale)


def c_map(f, x):
    return tuple(f(p) for p in x)


def frequencies(length):
    root = math.exp(math.log(alpha_corner) / length)
    listed = []
    for j in range(length // 2 + 1):
        angle = 2.0 * math.pi * j / length
        if j == 0 or 2 * j == length:
            listed.append((j, (1.0 - root * math.cos(angle),)))
        else:
            listed.append((j, (1.0 - root * math.cos(angle), root * math.sin(angle))))
    return listed


def planes(length):
    return sum(len(shift) for unused, shift in frequencies(length))


def turn(j, n, length):
    count = j * n % length
    if 4 * count % length == 0:
        return ((1.0, 0.0), (0.0, 1.0), (-1.0, 0.0), (0.0, -1.0))[4 * count // length]
    angle = 2.0 * math.pi * count / length
    return (math.cos(angle), math.sin(angle))


def weighted(total, weight, value):
    if weight == 0.0:
        return total
    if weight == 1.0:
        term = value
    elif weight == -1.0:
        return -value if total is None else total - value
    else:
        term = weight * value
    return term if total is None else total + term


def stack_kernel(
    forcing_hbm,
    previous_hbm,
    initial_hbm,
    zones_hbm,
    drift_hbm,
    zone_hbm,
    flag_hbm,
    faces_hbm,
    mine_ref,
    other_ref,
    initial_ref,
    faces_ref,
    rows_ref,
    zones_ref,
    drift_ref,
    zone_ref,
    flag_ref,
    sems,
):
    species = lax.axis_index("tm") % 2
    pairs = (
        (zones_hbm, zones_ref),
        (drift_hbm, drift_ref),
        (zone_hbm, zone_ref),
        (flag_hbm, flag_ref),
        (forcing_hbm.at[0, species], mine_ref.at[0]),
        (previous_hbm.at[0, species], mine_ref.at[1]),
        (forcing_hbm.at[0, 1 - species], other_ref.at[0]),
        (previous_hbm.at[0, 1 - species], other_ref.at[1]),
        (faces_hbm, faces_ref),
        (initial_hbm.at[species], initial_ref),
    )
    copies = [
        pltpu.make_async_copy(source, target, sems.at[index])
        for index, (source, target) in enumerate(pairs)
    ]
    for copy in copies:
        copy.start()
    for copy in copies[:4]:
        copy.wait()
    zone = zone_ref[...]
    diffusion = jnp.zeros(zone.shape, jnp.float32)
    for index in range(zones_ref.shape[1]):
        diffusion = jnp.where(zone == index, zones_ref[species, index], diffusion)
    rows_ref[0:1] = diffusion
    rows_ref[1:2] = jnp.full(zone.shape, drift_ref[species], jnp.float32)
    rows_ref[2:3] = flag_ref[...].astype(jnp.float32)
    for copy in copies[4:]:
        copy.wait()


def factor_kernel(length, rows_ref, faces_ref, near_ref, far_ref):
    cells, lanes = faces_ref.shape
    faces = faces_ref[...].astype(jnp.float32)
    row = lax.broadcasted_iota(jnp.int32, (cells, lanes), 0)
    link_above = jnp.where(row == cells - 1, 0.0, faces)
    link_below = jnp.where(row == 0, 0.0, roll_down(faces, 1))
    ground = jnp.where(row == 0, rows_ref[2:3], 0.0)
    diffusion = rows_ref[0:1]
    drift = rows_ref[1:2]
    below = -(diffusion + drift) * link_below
    above = -diffusion * link_above
    centre = diffusion * (link_below + link_above) + drift + 2.0 * diffusion * ground
    plane = 0
    for unused, shift in frequencies(length):
        parts = len(shift)
        a = (below,)
        c = (above,)
        b = (centre + shift[0],)
        if parts == 2:
            b = b + (jnp.full_like(centre, shift[1]),)
        for step in range(near_steps):
            distance = 1 << step
            inverse = c_inverse(b)
            low = c_neg(c_mul(a, c_map(lambda p: roll_down(p, distance), inverse)))
            high = c_neg(c_mul(c, c_map(lambda p: roll_up(p, distance), inverse)))
            down_c = c_map(lambda p: roll_down(p, distance), c)
            up_a = c_map(lambda p: roll_up(p, distance), a)
            b = c_add(b, c_add(c_mul(low, down_c), c_mul(high, up_a)))
            a = c_mul(low, c_map(lambda p: roll_down(p, distance), a))
            c = c_mul(high, c_map(lambda p: roll_up(p, distance), c))
            for part in range(parts):
                near_ref[plane + part, 2 * step] = low[part]
                near_ref[plane + part, 2 * step + 1] = high[part]
        carry = None
        for block in range(cells // tile):
            rows = slice(block * tile, (block + 1) * tile)
            ak, bk, ck = (c_map(lambda p: p[rows], item) for item in (a, b, c))
            if carry is None:
                eliminate = c_map(jnp.zeros_like, ak)
            else:
                eliminate = c_mul(ak, carry[0])
                bk = c_sub(bk, c_mul(eliminate, carry[1]))
            inverse = c_inverse(bk)
            substitute = c_mul(ck, inverse)
            for part in range(parts):
                far_ref[plane + part, 0, rows] = eliminate[part]
                far_ref[plane + part, 1, rows] = inverse[part]
                far_ref[plane + part, 2, rows] = substitute[part]
            carry = (inverse, ck)
        plane += parts


def in_order(me, held):
    bit = 1
    while bit < len(held):
        swap = (me & bit) != 0
        held = [
            jnp.where(swap, held[index ^ bit], held[index]) for index in range(len(held))
        ]
        bit *= 2
    return held


def sweep_kernel(length, *refs):
    stacks = refs[:length]
    initial_ref, near_ref, far_ref, own_ref, give_ref, sum_ref = refs[length:]
    cells, lanes = initial_ref.shape
    log_alpha = math.log(alpha_corner)
    me = lax.axis_index("tm")
    loads = in_order(me, [ref[0] for ref in stacks])
    befores = in_order(me, [ref[1] for ref in stacks])
    loads[0] = loads[0] + (initial_ref[...] - alpha_corner * befores[length - 1])
    scaled = [math.exp(log_alpha * n / length) * load for n, load in enumerate(loads)]
    spectrum = []
    plane = 0
    for j, shift in frequencies(length):
        parts = len(shift)
        rhs = [None] * parts
        for n in range(length):
            weights = turn(j, -n, length)
            for part in range(parts):
                rhs[part] = weighted(rhs[part], weights[part], scaled[n])
        rhs = tuple(rhs)
        for step in range(near_steps):
            distance = 1 << step
            low = tuple(near_ref[plane + p, 2 * step] for p in range(parts))
            high = tuple(near_ref[plane + p, 2 * step + 1] for p in range(parts))
            down = c_map(lambda p: roll_down(p, distance), rhs)
            up = c_map(lambda p: roll_up(p, distance), rhs)
            rhs = c_add(rhs, c_add(c_mul(low, down), c_mul(high, up)))
        blocks = []
        carry = None
        for block in range(cells // tile):
            rows = slice(block * tile, (block + 1) * tile)
            value = c_map(lambda p: p[rows], rhs)
            if carry is not None:
                eliminate = tuple(far_ref[plane + p, 0, rows] for p in range(parts))
                value = c_sub(value, c_mul(eliminate, carry))
            blocks.append(value)
            carry = value
        solved = [None] * len(blocks)
        carry = None
        for block in reversed(range(cells // tile)):
            rows = slice(block * tile, (block + 1) * tile)
            inverse = tuple(far_ref[plane + p, 1, rows] for p in range(parts))
            value = c_mul(inverse, blocks[block])
            if carry is not None:
                substitute = tuple(far_ref[plane + p, 2, rows] for p in range(parts))
                value = c_sub(value, c_mul(substitute, carry))
            solved[block] = value
            carry = value
        spectrum.append((j, parts, solved))
        plane += parts
    total = jnp.zeros((tile, lanes), jnp.float32)
    for block in range(cells // tile):
        rows = slice(block * tile, (block + 1) * tile)
        steps = []
        for n in range(length):
            fresh = None
            for j, parts, solved in spectrum:
                weights = turn(j, n, length)
                fresh = weighted(fresh, parts * weights[0], solved[block][0])
                if parts == 2:
                    fresh = weighted(fresh, -parts * weights[1], solved[block][1])
            fresh = fresh * (math.exp(-log_alpha * n / length) / length)
            steps.append(fresh)
            change = fresh - befores[n][rows]
            total = total + change * change
        own = steps[0]
        give = steps[1]
        for n in range(1, length):
            own = jnp.where(me == n, steps[n], own)
            give = jnp.where(me == n, steps[n ^ 1], give)
        own_ref[rows] = own
        give_ref[rows] = give
    sum_ref[...] = jnp.broadcast_to(jnp.sum(total, axis=0, keepdims=True), sum_ref.shape)


def join_kernel(entry_count, own_ref, got_ref, squares_ref, new_hbm, norm_ref, sems):
    species = lax.axis_index("tm") % 2
    copies = (
        pltpu.make_async_copy(own_ref, new_hbm.at[0, species], sems.at[0]),
        pltpu.make_async_copy(got_ref, new_hbm.at[0, 1 - species], sems.at[1]),
    )
    for copy in copies:
        copy.start()
    norm_ref[0, 0] = jnp.sqrt(jnp.sum(squares_ref[...]) / entry_count)
    for copy in copies:
        copy.wait()


def exchange(value, axis, bits):
    pairs = [(index, index ^ bits) for index in range(lax.axis_size(axis))]
    return lax.ppermute(value, axis, pairs)


def shards(
    forcing,
    initial_state,
    previous,
    zone_diffusion,
    drift_rate,
    column_zone,
    bottom_flag,
    open_faces,
):
    length = lax.axis_size("tm")
    space = lax.axis_size("space")
    cells, lanes = open_faces.shape
    whole = pl.BlockSpec(memory_space=pltpu.VMEM)
    outside = pl.BlockSpec(memory_space=pltpu.HBM)
    count = planes(length)
    params = pltpu.CompilerParams(vmem_limit_bytes=40 * 1024 * 1024)
    mine, other, initial, faces, rows = pl.pallas_call(
        stack_kernel,
        out_shape=(
            pltpu.VMEM((2, cells, lanes), jnp.float32),
            pltpu.VMEM((2, cells, lanes), jnp.float32),
            pltpu.VMEM((cells, lanes), jnp.float32),
            pltpu.VMEM((cells, lanes), jnp.int32),
            pltpu.VMEM((tile, lanes), jnp.float32),
        ),
        in_specs=[outside] * 8,
        out_specs=[whole] * 5,
        scratch_shapes=[
            pltpu.SMEM(zone_diffusion.shape, jnp.float32),
            pltpu.SMEM(drift_rate.shape, jnp.float32),
            pltpu.VMEM((1, lanes), jnp.int32),
            pltpu.VMEM((1, lanes), jnp.int32),
            pltpu.SemaphoreType.DMA((10,)),
        ],
        compiler_params=pltpu.CompilerParams(vmem_limit_bytes=62 * 1024 * 1024),
        cost_estimate=pl.CostEstimate(flops=4000, bytes_accessed=500000, transcendentals=0),
        name="stack_arrays",
    )(
        forcing,
        previous,
        initial_state,
        zone_diffusion,
        drift_rate,
        column_zone[None],
        bottom_flag[None],
        open_faces,
    )
    stacks = [mine]
    for bits in range(1, length):
        stacks.append(exchange(other if bits % 2 else mine, "tm", bits))
    near, far = pl.pallas_call(
        functools.partial(factor_kernel, length),
        out_shape=(
            jax.ShapeDtypeStruct((count, 2 * near_steps, cells, lanes), jnp.float32),
            jax.ShapeDtypeStruct((count, 3, cells, lanes), jnp.float32),
        ),
        in_specs=[whole] * 2,
        out_specs=[whole] * 2,
        compiler_params=params,
        cost_estimate=pl.CostEstimate(flops=4000000, bytes_accessed=3000000, transcendentals=0),
        name="factor_lines",
    )(rows, faces)
    own, give, squares = pl.pallas_call(
        functools.partial(sweep_kernel, length),
        out_shape=(
            pltpu.VMEM((cells, lanes), jnp.float32),
            pltpu.VMEM((cells, lanes), jnp.float32),
            pltpu.VMEM((2 * space, 1, lanes), jnp.float32),
        ),
        in_specs=[whole] * (length + 3),
        out_specs=[whole] * 3,
        compiler_params=params,
        cost_estimate=pl.CostEstimate(flops=4000000, bytes_accessed=3000000, transcendentals=0),
        name="solve_lines",
    )(*stacks, initial, near, far)
    got = exchange(give, "tm", 1)
    groups = [
        [(step + half) * space + index for half in range(2) for index in range(space)]
        for step in range(0, length, 2)
    ]
    squares = lax.all_to_all(
        squares, ("tm", "space"), 0, 0, axis_index_groups=groups, tiled=True
    )
    entry_count = length * space * forcing.shape[1] * cells * lanes
    new_iterate, norm = pl.pallas_call(
        functools.partial(join_kernel, entry_count),
        out_shape=(
            jax.ShapeDtypeStruct(forcing.shape, jnp.float32),
            jax.ShapeDtypeStruct((1, 1), jnp.float32),
        ),
        in_specs=[whole] * 3,
        out_specs=(outside, pl.BlockSpec(memory_space=pltpu.SMEM)),
        scratch_shapes=[pltpu.SemaphoreType.DMA((2,))],
        compiler_params=params,
        cost_estimate=pl.CostEstimate(flops=4000, bytes_accessed=100000, transcendentals=0),
        name="join_species",
    )(own, got, squares)
    return (new_iterate, norm[0, 0])


def solution(mesh):
    placed = (
        P("tm", None, None, "space"),
        P(None, None, "space"),
        P("tm", None, None, "space"),
        P(),
        P(),
        P("space"),
        P("space"),
        P(None, "space"),
    )
    return jax.shard_map(
        shards,
        mesh=mesh,
        in_specs=placed,
        out_specs=(P("tm", None, None, "space"), P()),
        check_vma=False,
    )
```

```python
import functools
import math

import jax
import jax.numpy as jnp
from jax import lax
from jax.experimental import pallas as pl
from jax.experimental.pallas import tpu as pltpu
from jax.sharding import PartitionSpec as P

alpha_corner = 0.3
tile = 8
near_steps = 3


def roll_down(block, distance):
    return pltpu.roll(block, distance, 0)


def roll_up(block, distance):
    return pltpu.roll(block, block.shape[0] - distance, 0)


def c_mul(x, y):
    if len(x) == 1 and len(y) == 1:
        return (x[0] * y[0],)
    if len(x) == 1:
        return (x[0] * y[0], x[0] * y[1])
    if len(y) == 1:
        return (x[0] * y[0], x[1] * y[0])
    return (x[0] * y[0] - x[1] * y[1], x[0] * y[1] + x[1] * y[0])


def c_add(x, y):
    return tuple(p + q for p, q in zip(x, y))


def c_sub(x, y):
    return tuple(p - q for p, q in zip(x, y))


def c_neg(x):
    return tuple(-p for p in x)


def c_inverse(x):
    if len(x) == 1:
        return (1.0 / x[0],)
    scale = 1.0 / (x[0] * x[0] + x[1] * x[1])
    return (x[0] * scale, -x[1] * scale)


def c_map(f, x):
    return tuple(f(p) for p in x)


def frequencies(length):
    root = math.exp(math.log(alpha_corner) / length)
    listed = []
    for j in range(length // 2 + 1):
        angle = 2.0 * math.pi * j / length
        if j == 0 or 2 * j == length:
            listed.append((j, (1.0 - root * math.cos(angle),)))
        else:
            listed.append((j, (1.0 - root * math.cos(angle), root * math.sin(angle))))
    return listed


def planes(length):
    return sum(len(shift) for unused, shift in frequencies(length))


def turn(j, n, length):
    count = j * n % length
    if 4 * count % length == 0:
        return ((1.0, 0.0), (0.0, 1.0), (-1.0, 0.0), (0.0, -1.0))[4 * count // length]
    angle = 2.0 * math.pi * count / length
    return (math.cos(angle), math.sin(angle))


def weighted(total, weight, value):
    if weight == 0.0:
        return total
    if weight == 1.0:
        term = value
    elif weight == -1.0:
        return -value if total is None else total - value
    else:
        term = weight * value
    return term if total is None else total + term


def stack_kernel(
    forcing_hbm,
    previous_hbm,
    initial_hbm,
    zones_hbm,
    drift_hbm,
    zone_hbm,
    flag_hbm,
    faces_hbm,
    mine_ref,
    other_ref,
    initial_ref,
    faces_ref,
    rows_ref,
    zones_ref,
    drift_ref,
    zone_ref,
    flag_ref,
    sems,
):
    species = lax.axis_index("tm") % 2
    pairs = (
        (zones_hbm, zones_ref),
        (drift_hbm, drift_ref),
        (zone_hbm, zone_ref),
        (flag_hbm, flag_ref),
        (forcing_hbm.at[0, species], mine_ref.at[0]),
        (previous_hbm.at[0, species], mine_ref.at[1]),
        (forcing_hbm.at[0, 1 - species], other_ref.at[0]),
        (previous_hbm.at[0, 1 - species], other_ref.at[1]),
        (faces_hbm, faces_ref),
        (initial_hbm.at[species], initial_ref),
    )
    copies = [
        pltpu.make_async_copy(source, target, sems.at[index])
        for index, (source, target) in enumerate(pairs)
    ]
    for copy in copies:
        copy.start()
    for copy in copies[:4]:
        copy.wait()
    zone = zone_ref[...]
    diffusion = jnp.zeros(zone.shape, jnp.float32)
    for index in range(zones_ref.shape[1]):
        diffusion = jnp.where(zone == index, zones_ref[species, index], diffusion)
    rows_ref[0:1] = diffusion
    rows_ref[1:2] = jnp.full(zone.shape, drift_ref[species], jnp.float32)
    rows_ref[2:3] = flag_ref[...].astype(jnp.float32)
    for copy in copies[4:]:
        copy.wait()


def factor_kernel(length, rows_ref, faces_ref, near_ref, far_ref):
    cells, lanes = faces_ref.shape
    faces = faces_ref[...].astype(jnp.float32)
    row = lax.broadcasted_iota(jnp.int32, (cells, lanes), 0)
    link_above = jnp.where(row == cells - 1, 0.0, faces)
    link_below = jnp.where(row == 0, 0.0, roll_down(faces, 1))
    ground = jnp.where(row == 0, rows_ref[2:3], 0.0)
    diffusion = rows_ref[0:1]
    drift = rows_ref[1:2]
    below = -(diffusion + drift) * link_below
    above = -diffusion * link_above
    centre = diffusion * (link_below + link_above) + drift + 2.0 * diffusion * ground
    plane = 0
    for unused, shift in frequencies(length):
        parts = len(shift)
        a = (below,)
        c = (above,)
        b = (centre + shift[0],)
        if parts == 2:
            b = b + (jnp.full_like(centre, shift[1]),)
        for step in range(near_steps):
            distance = 1 << step
            inverse = c_inverse(b)
            low = c_neg(c_mul(a, c_map(lambda p: roll_down(p, distance), inverse)))
            high = c_neg(c_mul(c, c_map(lambda p: roll_up(p, distance), inverse)))
            down_c = c_map(lambda p: roll_down(p, distance), c)
            up_a = c_map(lambda p: roll_up(p, distance), a)
            b = c_add(b, c_add(c_mul(low, down_c), c_mul(high, up_a)))
            a = c_mul(low, c_map(lambda p: roll_down(p, distance), a))
            c = c_mul(high, c_map(lambda p: roll_up(p, distance), c))
            for part in range(parts):
                near_ref[plane + part, 2 * step] = low[part]
                near_ref[plane + part, 2 * step + 1] = high[part]
        carry = None
        for block in range(cells // tile):
            rows = slice(block * tile, (block + 1) * tile)
            ak, bk, ck = (c_map(lambda p: p[rows], item) for item in (a, b, c))
            if carry is None:
                eliminate = c_map(jnp.zeros_like, ak)
            else:
                eliminate = c_mul(ak, carry[0])
                bk = c_sub(bk, c_mul(eliminate, carry[1]))
            inverse = c_inverse(bk)
            substitute = c_mul(ck, inverse)
            for part in range(parts):
                far_ref[plane + part, 0, rows] = eliminate[part]
                far_ref[plane + part, 1, rows] = inverse[part]
                far_ref[plane + part, 2, rows] = substitute[part]
            carry = (inverse, ck)
        plane += parts


def in_order(me, held):
    bit = 1
    while bit < len(held):
        swap = (me & bit) != 0
        held = [
            jnp.where(swap, held[index ^ bit], held[index]) for index in range(len(held))
        ]
        bit *= 2
    return held


def sweep_kernel(length, *refs):
    stacks = refs[:length]
    initial_ref, near_ref, far_ref, own_ref, give_ref, sum_ref = refs[length:]
    cells, lanes = initial_ref.shape
    log_alpha = math.log(alpha_corner)
    me = lax.axis_index("tm")
    loads = in_order(me, [ref[0] for ref in stacks])
    befores = in_order(me, [ref[1] for ref in stacks])
    loads[0] = loads[0] + (initial_ref[...] - alpha_corner * befores[length - 1])
    scaled = [math.exp(log_alpha * n / length) * load for n, load in enumerate(loads)]
    spectrum = []
    plane = 0
    for j, shift in frequencies(length):
        parts = len(shift)
        rhs = [None] * parts
        for n in range(length):
            weights = turn(j, -n, length)
            for part in range(parts):
                rhs[part] = weighted(rhs[part], weights[part], scaled[n])
        rhs = tuple(rhs)
        for step in range(near_steps):
            distance = 1 << step
            low = tuple(near_ref[plane + p, 2 * step] for p in range(parts))
            high = tuple(near_ref[plane + p, 2 * step + 1] for p in range(parts))
            down = c_map(lambda p: roll_down(p, distance), rhs)
            up = c_map(lambda p: roll_up(p, distance), rhs)
            rhs = c_add(rhs, c_add(c_mul(low, down), c_mul(high, up)))
        blocks = []
        carry = None
        for block in range(cells // tile):
            rows = slice(block * tile, (block + 1) * tile)
            value = c_map(lambda p: p[rows], rhs)
            if carry is not None:
                eliminate = tuple(far_ref[plane + p, 0, rows] for p in range(parts))
                value = c_sub(value, c_mul(eliminate, carry))
            blocks.append(value)
            carry = value
        solved = [None] * len(blocks)
        carry = None
        for block in reversed(range(cells // tile)):
            rows = slice(block * tile, (block + 1) * tile)
            inverse = tuple(far_ref[plane + p, 1, rows] for p in range(parts))
            value = c_mul(inverse, blocks[block])
            if carry is not None:
                substitute = tuple(far_ref[plane + p, 2, rows] for p in range(parts))
                value = c_sub(value, c_mul(substitute, carry))
            solved[block] = value
            carry = value
        spectrum.append((j, parts, solved))
        plane += parts
    total = jnp.zeros((tile, lanes), jnp.float32)
    for block in range(cells // tile):
        rows = slice(block * tile, (block + 1) * tile)
        steps = []
        for n in range(length):
            fresh = None
            for j, parts, solved in spectrum:
                weights = turn(j, n, length)
                fresh = weighted(fresh, parts * weights[0], solved[block][0])
                if parts == 2:
                    fresh = weighted(fresh, -parts * weights[1], solved[block][1])
            fresh = fresh * (math.exp(-log_alpha * n / length) / length)
            steps.append(fresh)
            change = fresh - befores[n][rows]
            total = total + change * change
        own = steps[0]
        give = steps[1]
        for n in range(1, length):
            own = jnp.where(me == n, steps[n], own)
            give = jnp.where(me == n, steps[n ^ 1], give)
        own_ref[rows] = own
        give_ref[rows] = give
    sum_ref[...] = jnp.broadcast_to(jnp.sum(total, axis=0, keepdims=True), sum_ref.shape)


def join_kernel(
    entry_count, own_ref, got_ref, squares_ref, new_hbm, norm_hbm, norm_ref, sems
):
    species = lax.axis_index("tm") % 2
    copies = (
        pltpu.make_async_copy(own_ref, new_hbm.at[0, species], sems.at[0]),
        pltpu.make_async_copy(got_ref, new_hbm.at[0, 1 - species], sems.at[1]),
        pltpu.make_async_copy(norm_ref, norm_hbm, sems.at[2]),
    )
    copies[0].start()
    copies[1].start()
    norm_ref[0, 0] = jnp.sqrt(jnp.sum(squares_ref[...]) / entry_count)
    copies[2].start()
    for copy in copies:
        copy.wait()


def exchange(value, axis, bits):
    pairs = [(index, index ^ bits) for index in range(lax.axis_size(axis))]
    return lax.ppermute(value, axis, pairs)


def shards(
    forcing,
    initial_state,
    previous,
    zone_diffusion,
    drift_rate,
    column_zone,
    bottom_flag,
    open_faces,
):
    length = lax.axis_size("tm")
    space = lax.axis_size("space")
    cells, lanes = open_faces.shape
    whole = pl.BlockSpec(memory_space=pltpu.VMEM)
    outside = pl.BlockSpec(memory_space=pltpu.HBM)
    count = planes(length)
    params = pltpu.CompilerParams(vmem_limit_bytes=40 * 1024 * 1024)
    mine, other, initial, faces, rows = pl.pallas_call(
        stack_kernel,
        out_shape=(
            pltpu.VMEM((2, cells, lanes), jnp.float32),
            pltpu.VMEM((2, cells, lanes), jnp.float32),
            pltpu.VMEM((cells, lanes), jnp.float32),
            pltpu.VMEM((cells, lanes), jnp.int32),
            pltpu.VMEM((tile, lanes), jnp.float32),
        ),
        in_specs=[outside] * 8,
        out_specs=[whole] * 5,
        scratch_shapes=[
            pltpu.SMEM(zone_diffusion.shape, jnp.float32),
            pltpu.SMEM(drift_rate.shape, jnp.float32),
            pltpu.VMEM((1, lanes), jnp.int32),
            pltpu.VMEM((1, lanes), jnp.int32),
            pltpu.SemaphoreType.DMA((10,)),
        ],
        compiler_params=pltpu.CompilerParams(vmem_limit_bytes=62 * 1024 * 1024),
        cost_estimate=pl.CostEstimate(flops=4000, bytes_accessed=500000, transcendentals=0),
        name="stack_arrays",
    )(
        forcing,
        previous,
        initial_state,
        zone_diffusion,
        drift_rate,
        column_zone[None],
        bottom_flag[None],
        open_faces,
    )
    stacks = [mine]
    for bits in range(1, length):
        stacks.append(exchange(other if bits % 2 else mine, "tm", bits))
    near, far = pl.pallas_call(
        functools.partial(factor_kernel, length),
        out_shape=(
            jax.ShapeDtypeStruct((count, 2 * near_steps, cells, lanes), jnp.float32),
            jax.ShapeDtypeStruct((count, 3, cells, lanes), jnp.float32),
        ),
        in_specs=[whole] * 2,
        out_specs=[whole] * 2,
        compiler_params=params,
        cost_estimate=pl.CostEstimate(flops=4000000, bytes_accessed=3000000, transcendentals=0),
        name="factor_lines",
    )(rows, faces)
    own, give, squares = pl.pallas_call(
        functools.partial(sweep_kernel, length),
        out_shape=(
            pltpu.VMEM((cells, lanes), jnp.float32),
            pltpu.VMEM((cells, lanes), jnp.float32),
            pltpu.VMEM((2 * space, 1, lanes), jnp.float32),
        ),
        in_specs=[whole] * (length + 3),
        out_specs=[whole] * 3,
        compiler_params=params,
        cost_estimate=pl.CostEstimate(flops=4000000, bytes_accessed=3000000, transcendentals=0),
        name="solve_lines",
    )(*stacks, initial, near, far)
    got = exchange(give, "tm", 1)
    groups = [
        [step * space + index for index in reversed(range(2 * space))]
        for step in range(0, length, 2)
    ]
    squares = lax.all_to_all(
        squares, ("tm", "space"), 0, 0, axis_index_groups=groups, tiled=True
    )
    entry_count = length * space * forcing.shape[1] * cells * lanes
    new_iterate, norm = pl.pallas_call(
        functools.partial(join_kernel, entry_count),
        out_shape=(
            jax.ShapeDtypeStruct(forcing.shape, jnp.float32),
            jax.ShapeDtypeStruct((1, 1), jnp.float32),
        ),
        in_specs=[whole] * 3,
        out_specs=(outside, outside),
        scratch_shapes=[pltpu.SMEM((1, 1), jnp.float32), pltpu.SemaphoreType.DMA((3,))],
        compiler_params=params,
        cost_estimate=pl.CostEstimate(flops=4000, bytes_accessed=100000, transcendentals=0),
        name="join_species",
    )(own, got, squares)
    return (new_iterate, norm[0, 0])


def solution(mesh):
    placed = (
        P("tm", None, None, "space"),
        P(None, None, "space"),
        P("tm", None, None, "space"),
        P(),
        P(),
        P("space"),
        P("space"),
        P(None, "space"),
    )
    return jax.shard_map(
        shards,
        mesh=mesh,
        in_specs=placed,
        out_specs=(P("tm", None, None, "space"), P()),
        check_vma=False,
    )
```

```python
import functools
import math

import jax
import jax.numpy as jnp
from jax import lax
from jax.experimental import pallas as pl
from jax.experimental.pallas import tpu as pltpu
from jax.sharding import PartitionSpec as P

alpha_corner = 0.3
tile = 8
near_steps = 3


def roll_down(block, distance):
    return pltpu.roll(block, distance, 0)


def roll_up(block, distance):
    return pltpu.roll(block, block.shape[0] - distance, 0)


def c_mul(x, y):
    if len(x) == 1 and len(y) == 1:
        return (x[0] * y[0],)
    if len(x) == 1:
        return (x[0] * y[0], x[0] * y[1])
    if len(y) == 1:
        return (x[0] * y[0], x[1] * y[0])
    return (x[0] * y[0] - x[1] * y[1], x[0] * y[1] + x[1] * y[0])


def c_add(x, y):
    return tuple(p + q for p, q in zip(x, y))


def c_sub(x, y):
    return tuple(p - q for p, q in zip(x, y))


def c_neg(x):
    return tuple(-p for p in x)


def c_inverse(x):
    if len(x) == 1:
        return (1.0 / x[0],)
    scale = 1.0 / (x[0] * x[0] + x[1] * x[1])
    return (x[0] * scale, -x[1] * scale)


def c_map(f, x):
    return tuple(f(p) for p in x)


def frequencies(length):
    root = math.exp(math.log(alpha_corner) / length)
    listed = []
    for j in range(length // 2 + 1):
        angle = 2.0 * math.pi * j / length
        if j == 0 or 2 * j == length:
            listed.append((j, (1.0 - root * math.cos(angle),)))
        else:
            listed.append((j, (1.0 - root * math.cos(angle), root * math.sin(angle))))
    return listed


def planes(length):
    return sum(len(shift) for unused, shift in frequencies(length))


def turn(j, n, length):
    count = j * n % length
    if 4 * count % length == 0:
        return ((1.0, 0.0), (0.0, 1.0), (-1.0, 0.0), (0.0, -1.0))[4 * count // length]
    angle = 2.0 * math.pi * count / length
    return (math.cos(angle), math.sin(angle))


def weighted(total, weight, value):
    if weight == 0.0:
        return total
    if weight == 1.0:
        term = value
    elif weight == -1.0:
        return -value if total is None else total - value
    else:
        term = weight * value
    return term if total is None else total + term


def start_all(pairs, sems):
    copies = [
        pltpu.make_async_copy(source, target, sems.at[index])
        for index, (source, target) in enumerate(pairs)
    ]
    for copy in copies:
        copy.start()
    return copies


def stack_kernel(forcing_hbm, previous_hbm, mine_ref, other_ref, sems):
    species = lax.axis_index("tm") % 2
    pairs = (
        (forcing_hbm.at[0, species], mine_ref.at[0]),
        (previous_hbm.at[0, species], mine_ref.at[1]),
        (forcing_hbm.at[0, 1 - species], other_ref.at[0]),
        (previous_hbm.at[0, 1 - species], other_ref.at[1]),
    )
    for copy in start_all(pairs, sems):
        copy.wait()


def factor_kernel(
    length,
    initial_hbm,
    zones_hbm,
    drift_hbm,
    zone_hbm,
    flag_hbm,
    faces_hbm,
    near_ref,
    far_ref,
    initial_ref,
    zones_ref,
    drift_ref,
    zone_ref,
    flag_ref,
    faces_ref,
    sems,
):
    species = lax.axis_index("tm") % 2
    pairs = (
        (zones_hbm, zones_ref),
        (drift_hbm, drift_ref),
        (zone_hbm, zone_ref),
        (flag_hbm, flag_ref),
        (faces_hbm, faces_ref),
        (initial_hbm.at[species], initial_ref),
    )
    for copy in start_all(pairs, sems):
        copy.wait()
    zone = zone_ref[...]
    diffusion = jnp.zeros(zone.shape, jnp.float32)
    for index in range(zones_ref.shape[1]):
        diffusion = jnp.where(zone == index, zones_ref[species, index], diffusion)
    drift = drift_ref[species]
    cells, lanes = faces_ref.shape
    faces = faces_ref[...].astype(jnp.float32)
    row = lax.broadcasted_iota(jnp.int32, (cells, lanes), 0)
    link_above = jnp.where(row == cells - 1, 0.0, faces)
    link_below = jnp.where(row == 0, 0.0, roll_down(faces, 1))
    ground = jnp.where(row == 0, flag_ref[...].astype(jnp.float32), 0.0)
    below = -(diffusion + drift) * link_below
    above = -diffusion * link_above
    centre = diffusion * (link_below + link_above) + drift + 2.0 * diffusion * ground
    plane = 0
    for unused, shift in frequencies(length):
        parts = len(shift)
        a = (below,)
        c = (above,)
        b = (centre + shift[0],)
        if parts == 2:
            b = b + (jnp.full_like(centre, shift[1]),)
        for step in range(near_steps):
            distance = 1 << step
            inverse = c_inverse(b)
            low = c_neg(c_mul(a, c_map(lambda p: roll_down(p, distance), inverse)))
            high = c_neg(c_mul(c, c_map(lambda p: roll_up(p, distance), inverse)))
            down_c = c_map(lambda p: roll_down(p, distance), c)
            up_a = c_map(lambda p: roll_up(p, distance), a)
            b = c_add(b, c_add(c_mul(low, down_c), c_mul(high, up_a)))
            a = c_mul(low, c_map(lambda p: roll_down(p, distance), a))
            c = c_mul(high, c_map(lambda p: roll_up(p, distance), c))
            for part in range(parts):
                near_ref[plane + part, 2 * step] = low[part]
                near_ref[plane + part, 2 * step + 1] = high[part]
        carry = None
        for block in range(cells // tile):
            rows = slice(block * tile, (block + 1) * tile)
            ak, bk, ck = (c_map(lambda p: p[rows], item) for item in (a, b, c))
            if carry is None:
                eliminate = c_map(jnp.zeros_like, ak)
            else:
                eliminate = c_mul(ak, carry[0])
                bk = c_sub(bk, c_mul(eliminate, carry[1]))
            inverse = c_inverse(bk)
            substitute = c_mul(ck, inverse)
            for part in range(parts):
                far_ref[plane + part, 0, rows] = eliminate[part]
                far_ref[plane + part, 1, rows] = inverse[part]
                far_ref[plane + part, 2, rows] = substitute[part]
            carry = (inverse, ck)
        plane += parts


def in_order(me, held):
    bit = 1
    while bit < len(held):
        swap = (me & bit) != 0
        held = [
            jnp.where(swap, held[index ^ bit], held[index]) for index in range(len(held))
        ]
        bit *= 2
    return held


def sweep_kernel(length, *refs):
    stacks = refs[:length]
    initial_ref, near_ref, far_ref, own_ref, give_ref, sum_ref = refs[length:]
    cells, lanes = initial_ref.shape
    log_alpha = math.log(alpha_corner)
    me = lax.axis_index("tm")
    loads = in_order(me, [ref[0] for ref in stacks])
    befores = in_order(me, [ref[1] for ref in stacks])
    loads[0] = loads[0] + (initial_ref[...] - alpha_corner * befores[length - 1])
    scaled = [math.exp(log_alpha * n / length) * load for n, load in enumerate(loads)]
    spectrum = []
    plane = 0
    for j, shift in frequencies(length):
        parts = len(shift)
        rhs = [None] * parts
        for n in range(length):
            weights = turn(j, -n, length)
            for part in range(parts):
                rhs[part] = weighted(rhs[part], weights[part], scaled[n])
        rhs = tuple(rhs)
        for step in range(near_steps):
            distance = 1 << step
            low = tuple(near_ref[plane + p, 2 * step] for p in range(parts))
            high = tuple(near_ref[plane + p, 2 * step + 1] for p in range(parts))
            down = c_map(lambda p: roll_down(p, distance), rhs)
            up = c_map(lambda p: roll_up(p, distance), rhs)
            rhs = c_add(rhs, c_add(c_mul(low, down), c_mul(high, up)))
        blocks = []
        carry = None
        for block in range(cells // tile):
            rows = slice(block * tile, (block + 1) * tile)
            value = c_map(lambda p: p[rows], rhs)
            if carry is not None:
                eliminate = tuple(far_ref[plane + p, 0, rows] for p in range(parts))
                value = c_sub(value, c_mul(eliminate, carry))
            blocks.append(value)
            carry = value
        solved = [None] * len(blocks)
        carry = None
        for block in reversed(range(cells // tile)):
            rows = slice(block * tile, (block + 1) * tile)
            inverse = tuple(far_ref[plane + p, 1, rows] for p in range(parts))
            value = c_mul(inverse, blocks[block])
            if carry is not None:
                substitute = tuple(far_ref[plane + p, 2, rows] for p in range(parts))
                value = c_sub(value, c_mul(substitute, carry))
            solved[block] = value
            carry = value
        spectrum.append((j, parts, solved))
        plane += parts
    total = jnp.zeros((tile, lanes), jnp.float32)
    for block in range(cells // tile):
        rows = slice(block * tile, (block + 1) * tile)
        steps = []
        for n in range(length):
            fresh = None
            for j, parts, solved in spectrum:
                weights = turn(j, n, length)
                fresh = weighted(fresh, parts * weights[0], solved[block][0])
                if parts == 2:
                    fresh = weighted(fresh, -parts * weights[1], solved[block][1])
            fresh = fresh * (math.exp(-log_alpha * n / length) / length)
            steps.append(fresh)
            change = fresh - befores[n][rows]
            total = total + change * change
        own = steps[0]
        give = steps[1]
        for n in range(1, length):
            own = jnp.where(me == n, steps[n], own)
            give = jnp.where(me == n, steps[n ^ 1], give)
        own_ref[rows] = own
        give_ref[rows] = give
    sum_ref[...] = jnp.broadcast_to(jnp.sum(total, axis=0, keepdims=True), sum_ref.shape)


def join_kernel(
    entry_count, own_ref, got_ref, squares_ref, new_hbm, norm_hbm, norm_ref, sems
):
    species = lax.axis_index("tm") % 2
    copies = (
        pltpu.make_async_copy(own_ref, new_hbm.at[0, species], sems.at[0]),
        pltpu.make_async_copy(got_ref, new_hbm.at[0, 1 - species], sems.at[1]),
        pltpu.make_async_copy(norm_ref, norm_hbm, sems.at[2]),
    )
    copies[0].start()
    copies[1].start()
    norm_ref[0, 0] = jnp.sqrt(jnp.sum(squares_ref[...]) / entry_count)
    copies[2].start()
    for copy in copies:
        copy.wait()


def exchange(value, axis, bits):
    pairs = [(index, index ^ bits) for index in range(lax.axis_size(axis))]
    return lax.ppermute(value, axis, pairs)


def shards(
    forcing,
    initial_state,
    previous,
    zone_diffusion,
    drift_rate,
    column_zone,
    bottom_flag,
    open_faces,
):
    length = lax.axis_size("tm")
    space = lax.axis_size("space")
    cells, lanes = open_faces.shape
    whole = pl.BlockSpec(memory_space=pltpu.VMEM)
    outside = pl.BlockSpec(memory_space=pltpu.HBM)
    count = planes(length)
    params = pltpu.CompilerParams(vmem_limit_bytes=40 * 1024 * 1024)
    alone = pltpu.CompilerParams(vmem_limit_bytes=56 * 1024 * 1024)
    mine, other = pl.pallas_call(
        stack_kernel,
        out_shape=(
            pltpu.VMEM((2, cells, lanes), jnp.float32),
            pltpu.VMEM((2, cells, lanes), jnp.float32),
        ),
        in_specs=[outside] * 2,
        out_specs=[whole] * 2,
        scratch_shapes=[pltpu.SemaphoreType.DMA((4,))],
        compiler_params=alone,
        cost_estimate=pl.CostEstimate(flops=4000, bytes_accessed=500000, transcendentals=0),
        name="stack_arrays",
    )(forcing, previous)
    stacks = [mine]
    for bits in range(1, length):
        stacks.append(exchange(other if bits % 2 else mine, "tm", bits))
    near, far, initial = pl.pallas_call(
        functools.partial(factor_kernel, length),
        out_shape=(
            pltpu.VMEM((count, 2 * near_steps, cells, lanes), jnp.float32),
            pltpu.VMEM((count, 3, cells, lanes), jnp.float32),
            pltpu.VMEM((cells, lanes), jnp.float32),
        ),
        in_specs=[outside] * 6,
        out_specs=[whole] * 3,
        scratch_shapes=[
            pltpu.SMEM(zone_diffusion.shape, jnp.float32),
            pltpu.SMEM(drift_rate.shape, jnp.float32),
            pltpu.VMEM((1, lanes), jnp.int32),
            pltpu.VMEM((1, lanes), jnp.int32),
            pltpu.VMEM((cells, lanes), jnp.int32),
            pltpu.SemaphoreType.DMA((6,)),
        ],
        compiler_params=alone,
        cost_estimate=pl.CostEstimate(flops=4000000, bytes_accessed=3000000, transcendentals=0),
        name="factor_lines",
    )(initial_state, zone_diffusion, drift_rate, column_zone[None], bottom_flag[None], open_faces)
    own, give, squares = pl.pallas_call(
        functools.partial(sweep_kernel, length),
        out_shape=(
            pltpu.VMEM((cells, lanes), jnp.float32),
            pltpu.VMEM((cells, lanes), jnp.float32),
            pltpu.VMEM((2 * space, 1, lanes), jnp.float32),
        ),
        in_specs=[whole] * (length + 3),
        out_specs=[whole] * 3,
        compiler_params=params,
        cost_estimate=pl.CostEstimate(flops=4000000, bytes_accessed=3000000, transcendentals=0),
        name="solve_lines",
    )(*stacks, initial, near, far)
    got = exchange(give, "tm", 1)
    groups = [
        [step * space + index for index in reversed(range(2 * space))]
        for step in range(0, length, 2)
    ]
    squares = lax.all_to_all(
        squares, ("tm", "space"), 0, 0, axis_index_groups=groups, tiled=True
    )
    entry_count = length * space * forcing.shape[1] * cells * lanes
    new_iterate, norm = pl.pallas_call(
        functools.partial(join_kernel, entry_count),
        out_shape=(
            jax.ShapeDtypeStruct(forcing.shape, jnp.float32),
            jax.ShapeDtypeStruct((1, 1), jnp.float32),
        ),
        in_specs=[whole] * 3,
        out_specs=(outside, outside),
        scratch_shapes=[pltpu.SMEM((1, 1), jnp.float32), pltpu.SemaphoreType.DMA((3,))],
        compiler_params=params,
        cost_estimate=pl.CostEstimate(flops=4000, bytes_accessed=100000, transcendentals=0),
        name="join_species",
    )(own, got, squares)
    return (new_iterate, norm[0, 0])


def solution(mesh):
    placed = (
        P("tm", None, None, "space"),
        P(None, None, "space"),
        P("tm", None, None, "space"),
        P(),
        P(),
        P("space"),
        P("space"),
        P(None, "space"),
    )
    return jax.shard_map(
        shards,
        mesh=mesh,
        in_specs=placed,
        out_specs=(P("tm", None, None, "space"), P()),
        check_vma=False,
    )
```

```python
import functools
import math

import jax
import jax.numpy as jnp
from jax import lax
from jax.experimental import pallas as pl
from jax.experimental.pallas import tpu as pltpu
from jax.sharding import PartitionSpec as P

alpha_corner = 0.3
tile = 8
near_steps = 3


def roll_down(block, distance):
    return pltpu.roll(block, distance, 0)


def roll_up(block, distance):
    return pltpu.roll(block, block.shape[0] - distance, 0)


def c_mul(x, y):
    if len(x) == 1 and len(y) == 1:
        return (x[0] * y[0],)
    if len(x) == 1:
        return (x[0] * y[0], x[0] * y[1])
    if len(y) == 1:
        return (x[0] * y[0], x[1] * y[0])
    return (x[0] * y[0] - x[1] * y[1], x[0] * y[1] + x[1] * y[0])


def c_add(x, y):
    return tuple(p + q for p, q in zip(x, y))


def c_sub(x, y):
    return tuple(p - q for p, q in zip(x, y))


def c_neg(x):
    return tuple(-p for p in x)


def c_inverse(x):
    if len(x) == 1:
        return (1.0 / x[0],)
    scale = 1.0 / (x[0] * x[0] + x[1] * x[1])
    return (x[0] * scale, -x[1] * scale)


def c_map(f, x):
    return tuple(f(p) for p in x)


def frequencies(length):
    root = math.exp(math.log(alpha_corner) / length)
    listed = []
    for j in range(length // 2 + 1):
        angle = 2.0 * math.pi * j / length
        if j == 0 or 2 * j == length:
            listed.append((j, (1.0 - root * math.cos(angle),)))
        else:
            listed.append((j, (1.0 - root * math.cos(angle), root * math.sin(angle))))
    return listed


def planes(length):
    return sum(len(shift) for unused, shift in frequencies(length))


def turn(j, n, length):
    count = j * n % length
    if 4 * count % length == 0:
        return ((1.0, 0.0), (0.0, 1.0), (-1.0, 0.0), (0.0, -1.0))[4 * count // length]
    angle = 2.0 * math.pi * count / length
    return (math.cos(angle), math.sin(angle))


def weighted(total, weight, value):
    if weight == 0.0:
        return total
    if weight == 1.0:
        term = value
    elif weight == -1.0:
        return -value if total is None else total - value
    else:
        term = weight * value
    return term if total is None else total + term


def start_all(pairs, sems):
    copies = [
        pltpu.make_async_copy(source, target, sems.at[index])
        for index, (source, target) in enumerate(pairs)
    ]
    for copy in copies:
        copy.start()
    return copies


def stack_kernel(forcing_hbm, previous_hbm, mine_ref, other_ref, sems):
    species = lax.axis_index("tm") % 2
    pairs = (
        (forcing_hbm.at[0, species], mine_ref.at[0]),
        (previous_hbm.at[0, species], mine_ref.at[1]),
        (forcing_hbm.at[0, 1 - species], other_ref.at[0]),
        (previous_hbm.at[0, 1 - species], other_ref.at[1]),
    )
    for copy in start_all(pairs, sems):
        copy.wait()


def factor_kernel(
    length,
    initial_hbm,
    zones_hbm,
    drift_hbm,
    zone_hbm,
    flag_hbm,
    faces_hbm,
    near_ref,
    far_ref,
    initial_ref,
    zones_ref,
    drift_ref,
    zone_ref,
    flag_ref,
    faces_ref,
    sems,
):
    species = lax.axis_index("tm") % 2
    pairs = (
        (zones_hbm, zones_ref),
        (drift_hbm, drift_ref),
        (zone_hbm, zone_ref),
        (flag_hbm, flag_ref),
        (faces_hbm, faces_ref),
        (initial_hbm.at[species], initial_ref),
    )
    for copy in start_all(pairs, sems):
        copy.wait()
    zone = zone_ref[...]
    diffusion = jnp.zeros(zone.shape, jnp.float32)
    for index in range(zones_ref.shape[1]):
        diffusion = jnp.where(zone == index, zones_ref[species, index], diffusion)
    drift = drift_ref[species]
    cells, lanes = faces_ref.shape
    faces = faces_ref[...].astype(jnp.float32)
    row = lax.broadcasted_iota(jnp.int32, (cells, lanes), 0)
    link_above = jnp.where(row == cells - 1, 0.0, faces)
    link_below = jnp.where(row == 0, 0.0, roll_down(faces, 1))
    ground = jnp.where(row == 0, flag_ref[...].astype(jnp.float32), 0.0)
    below = -(diffusion + drift) * link_below
    above = -diffusion * link_above
    centre = diffusion * (link_below + link_above) + drift + 2.0 * diffusion * ground
    plane = 0
    for unused, shift in frequencies(length):
        parts = len(shift)
        a = (below,)
        c = (above,)
        b = (centre + shift[0],)
        if parts == 2:
            b = b + (jnp.full_like(centre, shift[1]),)
        for step in range(near_steps):
            distance = 1 << step
            inverse = c_inverse(b)
            low = c_neg(c_mul(a, c_map(lambda p: roll_down(p, distance), inverse)))
            high = c_neg(c_mul(c, c_map(lambda p: roll_up(p, distance), inverse)))
            down_c = c_map(lambda p: roll_down(p, distance), c)
            up_a = c_map(lambda p: roll_up(p, distance), a)
            b = c_add(b, c_add(c_mul(low, down_c), c_mul(high, up_a)))
            a = c_mul(low, c_map(lambda p: roll_down(p, distance), a))
            c = c_mul(high, c_map(lambda p: roll_up(p, distance), c))
            for part in range(parts):
                near_ref[plane + part, 2 * step] = low[part]
                near_ref[plane + part, 2 * step + 1] = high[part]
        carry = None
        for block in range(cells // tile):
            rows = slice(block * tile, (block + 1) * tile)
            ak, bk, ck = (c_map(lambda p: p[rows], item) for item in (a, b, c))
            if carry is None:
                eliminate = c_map(jnp.zeros_like, ak)
            else:
                eliminate = c_mul(ak, carry[0])
                bk = c_sub(bk, c_mul(eliminate, carry[1]))
            inverse = c_inverse(bk)
            substitute = c_mul(ck, inverse)
            for part in range(parts):
                far_ref[plane + part, 0, rows] = eliminate[part]
                far_ref[plane + part, 1, rows] = inverse[part]
                far_ref[plane + part, 2, rows] = substitute[part]
            carry = (inverse, ck)
        plane += parts


def in_order(me, held):
    bit = 1
    while bit < len(held):
        swap = (me & bit) != 0
        held = [
            jnp.where(swap, held[index ^ bit], held[index]) for index in range(len(held))
        ]
        bit *= 2
    return held


def sweep_kernel(length, *refs):
    stacks = refs[:length]
    initial_ref, near_ref, far_ref, own_ref, give_ref, sum_ref = refs[length:]
    cells, lanes = initial_ref.shape
    log_alpha = math.log(alpha_corner)
    me = lax.axis_index("tm")
    loads = in_order(me, [ref[0] for ref in stacks])
    befores = in_order(me, [ref[1] for ref in stacks])
    loads[0] = loads[0] + (initial_ref[...] - alpha_corner * befores[length - 1])
    scaled = [math.exp(log_alpha * n / length) * load for n, load in enumerate(loads)]
    spectrum = []
    plane = 0
    for j, shift in frequencies(length):
        parts = len(shift)
        rhs = [None] * parts
        for n in range(length):
            weights = turn(j, -n, length)
            for part in range(parts):
                rhs[part] = weighted(rhs[part], weights[part], scaled[n])
        rhs = tuple(rhs)
        for step in range(near_steps):
            distance = 1 << step
            low = tuple(near_ref[plane + p, 2 * step] for p in range(parts))
            high = tuple(near_ref[plane + p, 2 * step + 1] for p in range(parts))
            down = c_map(lambda p: roll_down(p, distance), rhs)
            up = c_map(lambda p: roll_up(p, distance), rhs)
            rhs = c_add(rhs, c_add(c_mul(low, down), c_mul(high, up)))
        blocks = []
        carry = None
        for block in range(cells // tile):
            rows = slice(block * tile, (block + 1) * tile)
            value = c_map(lambda p: p[rows], rhs)
            if carry is not None:
                eliminate = tuple(far_ref[plane + p, 0, rows] for p in range(parts))
                value = c_sub(value, c_mul(eliminate, carry))
            blocks.append(value)
            carry = value
        solved = [None] * len(blocks)
        carry = None
        for block in reversed(range(cells // tile)):
            rows = slice(block * tile, (block + 1) * tile)
            inverse = tuple(far_ref[plane + p, 1, rows] for p in range(parts))
            value = c_mul(inverse, blocks[block])
            if carry is not None:
                substitute = tuple(far_ref[plane + p, 2, rows] for p in range(parts))
                value = c_sub(value, c_mul(substitute, carry))
            solved[block] = value
            carry = value
        spectrum.append((j, parts, solved))
        plane += parts
    total = jnp.zeros((tile, lanes), jnp.float32)
    for block in range(cells // tile):
        rows = slice(block * tile, (block + 1) * tile)
        steps = []
        for n in range(length):
            fresh = None
            for j, parts, solved in spectrum:
                weights = turn(j, n, length)
                fresh = weighted(fresh, parts * weights[0], solved[block][0])
                if parts == 2:
                    fresh = weighted(fresh, -parts * weights[1], solved[block][1])
            fresh = fresh * (math.exp(-log_alpha * n / length) / length)
            steps.append(fresh)
            change = fresh - befores[n][rows]
            total = total + change * change
        own = steps[0]
        give = steps[1]
        for n in range(1, length):
            own = jnp.where(me == n, steps[n], own)
            give = jnp.where(me == n, steps[n ^ 1], give)
        own_ref[rows] = own
        give_ref[rows] = give
    sum_ref[...] = jnp.broadcast_to(jnp.sum(total, axis=0, keepdims=True), sum_ref.shape)


def join_kernel(
    entry_count, own_ref, got_ref, squares_ref, new_hbm, norm_hbm, norm_ref, sems
):
    species = lax.axis_index("tm") % 2
    copies = (
        pltpu.make_async_copy(own_ref, new_hbm.at[0, species], sems.at[0]),
        pltpu.make_async_copy(got_ref, new_hbm.at[0, 1 - species], sems.at[1]),
        pltpu.make_async_copy(norm_ref, norm_hbm, sems.at[2]),
    )
    copies[0].start()
    copies[1].start()
    norm_ref[0, 0] = jnp.sqrt(jnp.sum(squares_ref[...]) / entry_count)
    copies[2].start()
    for copy in copies:
        copy.wait()


def exchange(value, axis, bits):
    pairs = [(index, index ^ bits) for index in range(lax.axis_size(axis))]
    return lax.ppermute(value, axis, pairs)


def shards(
    forcing,
    initial_state,
    previous,
    zone_diffusion,
    drift_rate,
    column_zone,
    bottom_flag,
    open_faces,
):
    length = lax.axis_size("tm")
    space = lax.axis_size("space")
    cells, lanes = open_faces.shape
    whole = pl.BlockSpec(memory_space=pltpu.VMEM)
    outside = pl.BlockSpec(memory_space=pltpu.HBM)
    count = planes(length)
    params = pltpu.CompilerParams(vmem_limit_bytes=40 * 1024 * 1024)
    alone = pltpu.CompilerParams(vmem_limit_bytes=56 * 1024 * 1024)
    mine, other = pl.pallas_call(
        stack_kernel,
        out_shape=(
            pltpu.VMEM((2, cells, lanes), jnp.float32),
            pltpu.VMEM((2, cells, lanes), jnp.float32),
        ),
        in_specs=[outside] * 2,
        out_specs=[whole] * 2,
        scratch_shapes=[pltpu.SemaphoreType.DMA((4,))],
        compiler_params=alone,
        cost_estimate=pl.CostEstimate(flops=4000, bytes_accessed=500000, transcendentals=0),
        name="stack_arrays",
    )(forcing, previous)
    stacks = [mine]
    for bits in range(1, length):
        stacks.append(exchange(other if bits % 2 else mine, "tm", bits))
    near, far, initial = pl.pallas_call(
        functools.partial(factor_kernel, length),
        out_shape=(
            pltpu.VMEM((count, 2 * near_steps, cells, lanes), jnp.float32),
            pltpu.VMEM((count, 3, cells, lanes), jnp.float32),
            pltpu.VMEM((cells, lanes), jnp.float32),
        ),
        in_specs=[outside] * 6,
        out_specs=[whole] * 3,
        scratch_shapes=[
            pltpu.SMEM(zone_diffusion.shape, jnp.float32),
            pltpu.SMEM(drift_rate.shape, jnp.float32),
            pltpu.VMEM((1, lanes), jnp.int32),
            pltpu.VMEM((1, lanes), jnp.int32),
            pltpu.VMEM((cells, lanes), jnp.int32),
            pltpu.SemaphoreType.DMA((6,)),
        ],
        compiler_params=alone,
        cost_estimate=pl.CostEstimate(flops=4000000, bytes_accessed=3000000, transcendentals=0),
        name="factor_lines",
    )(initial_state, zone_diffusion, drift_rate, column_zone[None], bottom_flag[None], open_faces)
    own, give, squares = pl.pallas_call(
        functools.partial(sweep_kernel, length),
        out_shape=(
            pltpu.VMEM((cells, lanes), jnp.float32),
            pltpu.VMEM((cells, lanes), jnp.float32),
            pltpu.VMEM((2 * space, 1, lanes), jnp.float32),
        ),
        in_specs=[whole] * (length + 3),
        out_specs=[whole] * 3,
        compiler_params=params,
        cost_estimate=pl.CostEstimate(flops=4000000, bytes_accessed=3000000, transcendentals=0),
        name="solve_lines",
    )(*stacks, initial, near, far)
    got = exchange(give, "tm", 1)
    last = 2 * space - 1
    order = [last, *range(2, last, 2), *range(3, last, 2), 1, 0]
    groups = [[step * space + index for index in order] for step in range(0, length, 2)]
    squares = lax.all_to_all(
        squares, ("tm", "space"), 0, 0, axis_index_groups=groups, tiled=True
    )
    entry_count = length * space * forcing.shape[1] * cells * lanes
    new_iterate, norm = pl.pallas_call(
        functools.partial(join_kernel, entry_count),
        out_shape=(
            jax.ShapeDtypeStruct(forcing.shape, jnp.float32),
            jax.ShapeDtypeStruct((1, 1), jnp.float32),
        ),
        in_specs=[whole] * 3,
        out_specs=(outside, outside),
        scratch_shapes=[pltpu.SMEM((1, 1), jnp.float32), pltpu.SemaphoreType.DMA((3,))],
        compiler_params=params,
        cost_estimate=pl.CostEstimate(flops=4000, bytes_accessed=100000, transcendentals=0),
        name="join_species",
    )(own, got, squares)
    return (new_iterate, norm[0, 0])


def solution(mesh):
    placed = (
        P("tm", None, None, "space"),
        P(None, None, "space"),
        P("tm", None, None, "space"),
        P(),
        P(),
        P("space"),
        P("space"),
        P(None, "space"),
    )
    return jax.shard_map(
        shards,
        mesh=mesh,
        in_specs=placed,
        out_specs=(P("tm", None, None, "space"), P()),
        check_vma=False,
    )
```

```python
import functools
import math

import jax
import jax.numpy as jnp
from jax import lax
from jax.experimental import pallas as pl
from jax.experimental.pallas import tpu as pltpu
from jax.sharding import PartitionSpec as P

alpha_corner = 0.3
tile = 8
near_steps = 3


def roll_down(block, distance):
    return pltpu.roll(block, distance, 0)


def roll_up(block, distance):
    return pltpu.roll(block, block.shape[0] - distance, 0)


def c_mul(x, y):
    if len(x) == 1 and len(y) == 1:
        return (x[0] * y[0],)
    if len(x) == 1:
        return (x[0] * y[0], x[0] * y[1])
    if len(y) == 1:
        return (x[0] * y[0], x[1] * y[0])
    return (x[0] * y[0] - x[1] * y[1], x[0] * y[1] + x[1] * y[0])


def c_add(x, y):
    return tuple(p + q for p, q in zip(x, y))


def c_sub(x, y):
    return tuple(p - q for p, q in zip(x, y))


def c_neg(x):
    return tuple(-p for p in x)


def c_inverse(x):
    if len(x) == 1:
        return (1.0 / x[0],)
    scale = 1.0 / (x[0] * x[0] + x[1] * x[1])
    return (x[0] * scale, -x[1] * scale)


def c_map(f, x):
    return tuple(f(p) for p in x)


def frequencies(length):
    root = math.exp(math.log(alpha_corner) / length)
    listed = []
    for j in range(length // 2 + 1):
        angle = 2.0 * math.pi * j / length
        if j == 0 or 2 * j == length:
            listed.append((j, (1.0 - root * math.cos(angle),)))
        else:
            listed.append((j, (1.0 - root * math.cos(angle), root * math.sin(angle))))
    return listed


def planes(length):
    return sum(len(shift) for unused, shift in frequencies(length))


def turn(j, n, length):
    count = j * n % length
    if 4 * count % length == 0:
        return ((1.0, 0.0), (0.0, 1.0), (-1.0, 0.0), (0.0, -1.0))[4 * count // length]
    angle = 2.0 * math.pi * count / length
    return (math.cos(angle), math.sin(angle))


def weighted(total, weight, value):
    if weight == 0.0:
        return total
    if weight == 1.0:
        term = value
    elif weight == -1.0:
        return -value if total is None else total - value
    else:
        term = weight * value
    return term if total is None else total + term


def start_all(pairs, sems):
    copies = [
        pltpu.make_async_copy(source, target, sems.at[index])
        for index, (source, target) in enumerate(pairs)
    ]
    for copy in copies:
        copy.start()
    return copies


def stack_kernel(forcing_hbm, previous_hbm, mine_ref, other_ref, sems):
    species = lax.axis_index("tm") % 2
    pairs = (
        (forcing_hbm.at[0, species], mine_ref.at[0]),
        (previous_hbm.at[0, species], mine_ref.at[1]),
        (forcing_hbm.at[0, 1 - species], other_ref.at[0]),
        (previous_hbm.at[0, 1 - species], other_ref.at[1]),
    )
    for copy in start_all(pairs, sems):
        copy.wait()


def factor_kernel(
    length,
    initial_hbm,
    zones_hbm,
    drift_hbm,
    zone_hbm,
    flag_hbm,
    faces_hbm,
    near_ref,
    far_ref,
    initial_ref,
    zones_ref,
    drift_ref,
    zone_ref,
    flag_ref,
    faces_ref,
    sems,
):
    species = lax.axis_index("tm") % 2
    pairs = (
        (zones_hbm, zones_ref),
        (drift_hbm, drift_ref),
        (zone_hbm, zone_ref),
        (flag_hbm, flag_ref),
        (faces_hbm, faces_ref),
        (initial_hbm.at[species], initial_ref),
    )
    for copy in start_all(pairs, sems):
        copy.wait()
    zone = zone_ref[...]
    diffusion = jnp.zeros(zone.shape, jnp.float32)
    for index in range(zones_ref.shape[1]):
        diffusion = jnp.where(zone == index, zones_ref[species, index], diffusion)
    drift = drift_ref[species]
    cells, lanes = faces_ref.shape
    faces = faces_ref[...].astype(jnp.float32)
    row = lax.broadcasted_iota(jnp.int32, (cells, lanes), 0)
    link_above = jnp.where(row == cells - 1, 0.0, faces)
    link_below = jnp.where(row == 0, 0.0, roll_down(faces, 1))
    ground = jnp.where(row == 0, flag_ref[...].astype(jnp.float32), 0.0)
    below = -(diffusion + drift) * link_below
    above = -diffusion * link_above
    centre = diffusion * (link_below + link_above) + drift + 2.0 * diffusion * ground
    plane = 0
    for unused, shift in frequencies(length):
        parts = len(shift)
        a = (below,)
        c = (above,)
        b = (centre + shift[0],)
        if parts == 2:
            b = b + (jnp.full_like(centre, shift[1]),)
        for step in range(near_steps):
            distance = 1 << step
            inverse = c_inverse(b)
            low = c_neg(c_mul(a, c_map(lambda p: roll_down(p, distance), inverse)))
            high = c_neg(c_mul(c, c_map(lambda p: roll_up(p, distance), inverse)))
            down_c = c_map(lambda p: roll_down(p, distance), c)
            up_a = c_map(lambda p: roll_up(p, distance), a)
            b = c_add(b, c_add(c_mul(low, down_c), c_mul(high, up_a)))
            a = c_mul(low, c_map(lambda p: roll_down(p, distance), a))
            c = c_mul(high, c_map(lambda p: roll_up(p, distance), c))
            for part in range(parts):
                near_ref[plane + part, 2 * step] = low[part]
                near_ref[plane + part, 2 * step + 1] = high[part]
        carry = None
        for block in range(cells // tile):
            rows = slice(block * tile, (block + 1) * tile)
            ak, bk, ck = (c_map(lambda p: p[rows], item) for item in (a, b, c))
            if carry is None:
                eliminate = c_map(jnp.zeros_like, ak)
            else:
                eliminate = c_mul(ak, carry[0])
                bk = c_sub(bk, c_mul(eliminate, carry[1]))
            inverse = c_inverse(bk)
            substitute = c_mul(ck, inverse)
            for part in range(parts):
                far_ref[plane + part, 0, rows] = eliminate[part]
                far_ref[plane + part, 1, rows] = inverse[part]
                far_ref[plane + part, 2, rows] = substitute[part]
            carry = (inverse, ck)
        plane += parts


def in_order(me, held):
    bit = 1
    while bit < len(held):
        swap = (me & bit) != 0
        held = [
            jnp.where(swap, held[index ^ bit], held[index]) for index in range(len(held))
        ]
        bit *= 2
    return held


def sweep_kernel(length, *refs):
    stacks = refs[:length]
    initial_ref, near_ref, far_ref, own_ref, give_ref, sum_ref = refs[length:]
    cells, lanes = initial_ref.shape
    log_alpha = math.log(alpha_corner)
    me = lax.axis_index("tm")
    loads = in_order(me, [ref[0] for ref in stacks])
    befores = in_order(me, [ref[1] for ref in stacks])
    loads[0] = loads[0] + (initial_ref[...] - alpha_corner * befores[length - 1])
    scaled = [math.exp(log_alpha * n / length) * load for n, load in enumerate(loads)]
    spectrum = []
    plane = 0
    for j, shift in frequencies(length):
        parts = len(shift)
        rhs = [None] * parts
        for n in range(length):
            weights = turn(j, -n, length)
            for part in range(parts):
                rhs[part] = weighted(rhs[part], weights[part], scaled[n])
        rhs = tuple(rhs)
        for step in range(near_steps):
            distance = 1 << step
            low = tuple(near_ref[plane + p, 2 * step] for p in range(parts))
            high = tuple(near_ref[plane + p, 2 * step + 1] for p in range(parts))
            down = c_map(lambda p: roll_down(p, distance), rhs)
            up = c_map(lambda p: roll_up(p, distance), rhs)
            rhs = c_add(rhs, c_add(c_mul(low, down), c_mul(high, up)))
        blocks = []
        carry = None
        for block in range(cells // tile):
            rows = slice(block * tile, (block + 1) * tile)
            value = c_map(lambda p: p[rows], rhs)
            if carry is not None:
                eliminate = tuple(far_ref[plane + p, 0, rows] for p in range(parts))
                value = c_sub(value, c_mul(eliminate, carry))
            blocks.append(value)
            carry = value
        solved = [None] * len(blocks)
        carry = None
        for block in reversed(range(cells // tile)):
            rows = slice(block * tile, (block + 1) * tile)
            inverse = tuple(far_ref[plane + p, 1, rows] for p in range(parts))
            value = c_mul(inverse, blocks[block])
            if carry is not None:
                substitute = tuple(far_ref[plane + p, 2, rows] for p in range(parts))
                value = c_sub(value, c_mul(substitute, carry))
            solved[block] = value
            carry = value
        spectrum.append((j, parts, solved))
        plane += parts
    total = jnp.zeros((tile, lanes), jnp.float32)
    for block in range(cells // tile):
        rows = slice(block * tile, (block + 1) * tile)
        steps = []
        for n in range(length):
            fresh = None
            for j, parts, solved in spectrum:
                weights = turn(j, n, length)
                fresh = weighted(fresh, parts * weights[0], solved[block][0])
                if parts == 2:
                    fresh = weighted(fresh, -parts * weights[1], solved[block][1])
            fresh = fresh * (math.exp(-log_alpha * n / length) / length)
            steps.append(fresh)
            change = fresh - befores[n][rows]
            total = total + change * change
        own = steps[0]
        give = steps[1]
        for n in range(1, length):
            own = jnp.where(me == n, steps[n], own)
            give = jnp.where(me == n, steps[n ^ 1], give)
        own_ref[rows] = own
        give_ref[rows] = give
    sum_ref[...] = jnp.broadcast_to(jnp.sum(total, axis=0, keepdims=True), sum_ref.shape)


def join_kernel(
    entry_count, own_ref, got_ref, squares_ref, new_hbm, norm_hbm, norm_ref, sems
):
    species = lax.axis_index("tm") % 2
    copies = (
        pltpu.make_async_copy(own_ref, new_hbm.at[0, species], sems.at[0]),
        pltpu.make_async_copy(got_ref, new_hbm.at[0, 1 - species], sems.at[1]),
        pltpu.make_async_copy(norm_ref, norm_hbm, sems.at[2]),
    )
    copies[0].start()
    copies[1].start()
    norm_ref[0, 0] = jnp.sqrt(jnp.sum(squares_ref[...]) / entry_count)
    copies[2].start()
    for copy in copies:
        copy.wait()


def exchange(value, axis, bits):
    pairs = [(index, index ^ bits) for index in range(lax.axis_size(axis))]
    return lax.ppermute(value, axis, pairs)


def shards(
    forcing,
    initial_state,
    previous,
    zone_diffusion,
    drift_rate,
    column_zone,
    bottom_flag,
    open_faces,
):
    length = lax.axis_size("tm")
    space = lax.axis_size("space")
    cells, lanes = open_faces.shape
    whole = pl.BlockSpec(memory_space=pltpu.VMEM)
    outside = pl.BlockSpec(memory_space=pltpu.HBM)
    count = planes(length)
    params = pltpu.CompilerParams(vmem_limit_bytes=40 * 1024 * 1024)
    alone = pltpu.CompilerParams(vmem_limit_bytes=56 * 1024 * 1024)
    mine, other = pl.pallas_call(
        stack_kernel,
        out_shape=(
            pltpu.VMEM((2, cells, lanes), jnp.float32),
            pltpu.VMEM((2, cells, lanes), jnp.float32),
        ),
        in_specs=[outside] * 2,
        out_specs=[whole] * 2,
        scratch_shapes=[pltpu.SemaphoreType.DMA((4,))],
        compiler_params=alone,
        cost_estimate=pl.CostEstimate(flops=4000, bytes_accessed=500000, transcendentals=0),
        name="stack_arrays",
    )(forcing, previous)
    stacks = [mine]
    for bits in range(1, length):
        stacks.append(exchange(other if bits % 2 else mine, "tm", bits))
    near, far, initial = pl.pallas_call(
        functools.partial(factor_kernel, length),
        out_shape=(
            pltpu.VMEM((count, 2 * near_steps, cells, lanes), jnp.float32),
            pltpu.VMEM((count, 3, cells, lanes), jnp.float32),
            pltpu.VMEM((cells, lanes), jnp.float32),
        ),
        in_specs=[outside] * 6,
        out_specs=[whole] * 3,
        scratch_shapes=[
            pltpu.SMEM(zone_diffusion.shape, jnp.float32),
            pltpu.SMEM(drift_rate.shape, jnp.float32),
            pltpu.VMEM((1, lanes), jnp.int32),
            pltpu.VMEM((1, lanes), jnp.int32),
            pltpu.VMEM((cells, lanes), jnp.int32),
            pltpu.SemaphoreType.DMA((6,)),
        ],
        compiler_params=alone,
        cost_estimate=pl.CostEstimate(flops=4000000, bytes_accessed=3000000, transcendentals=0),
        name="factor_lines",
    )(initial_state, zone_diffusion, drift_rate, column_zone[None], bottom_flag[None], open_faces)
    own, give, squares = pl.pallas_call(
        functools.partial(sweep_kernel, length),
        out_shape=(
            pltpu.VMEM((cells, lanes), jnp.float32),
            pltpu.VMEM((cells, lanes), jnp.float32),
            pltpu.VMEM((2 * space, 1, lanes), jnp.float32),
        ),
        in_specs=[whole] * (length + 3),
        out_specs=[whole] * 3,
        compiler_params=params,
        cost_estimate=pl.CostEstimate(flops=4000000, bytes_accessed=3000000, transcendentals=0),
        name="solve_lines",
    )(*stacks, initial, near, far)
    got = exchange(give, "tm", 1)
    last = 2 * space - 1
    order = [last, *range(last)]
    groups = [[step * space + index for index in order] for step in range(0, length, 2)]
    squares = lax.all_to_all(
        squares, ("tm", "space"), 0, 0, axis_index_groups=groups, tiled=True
    )
    entry_count = length * space * forcing.shape[1] * cells * lanes
    new_iterate, norm = pl.pallas_call(
        functools.partial(join_kernel, entry_count),
        out_shape=(
            jax.ShapeDtypeStruct(forcing.shape, jnp.float32),
            jax.ShapeDtypeStruct((1, 1), jnp.float32),
        ),
        in_specs=[whole] * 3,
        out_specs=(outside, outside),
        scratch_shapes=[pltpu.SMEM((1, 1), jnp.float32), pltpu.SemaphoreType.DMA((3,))],
        compiler_params=params,
        cost_estimate=pl.CostEstimate(flops=4000, bytes_accessed=100000, transcendentals=0),
        name="join_species",
    )(own, got, squares)
    return (new_iterate, norm[0, 0])


def solution(mesh):
    placed = (
        P("tm", None, None, "space"),
        P(None, None, "space"),
        P("tm", None, None, "space"),
        P(),
        P(),
        P("space"),
        P("space"),
        P(None, "space"),
    )
    return jax.shard_map(
        shards,
        mesh=mesh,
        in_specs=placed,
        out_specs=(P("tm", None, None, "space"), P()),
        check_vma=False,
    )
```

```python
import functools
import math

import jax
import jax.numpy as jnp
from jax import lax
from jax.experimental import pallas as pl
from jax.experimental.pallas import tpu as pltpu
from jax.sharding import PartitionSpec as P

alpha_corner = 0.3
tile = 8
near_steps = 3


def roll_down(block, distance):
    return pltpu.roll(block, distance, 0)


def roll_up(block, distance):
    return pltpu.roll(block, block.shape[0] - distance, 0)


def c_mul(x, y):
    if len(x) == 1 and len(y) == 1:
        return (x[0] * y[0],)
    if len(x) == 1:
        return (x[0] * y[0], x[0] * y[1])
    if len(y) == 1:
        return (x[0] * y[0], x[1] * y[0])
    return (x[0] * y[0] - x[1] * y[1], x[0] * y[1] + x[1] * y[0])


def c_add(x, y):
    return tuple(p + q for p, q in zip(x, y))


def c_sub(x, y):
    return tuple(p - q for p, q in zip(x, y))


def c_neg(x):
    return tuple(-p for p in x)


def c_inverse(x):
    if len(x) == 1:
        return (1.0 / x[0],)
    scale = 1.0 / (x[0] * x[0] + x[1] * x[1])
    return (x[0] * scale, -x[1] * scale)


def c_map(f, x):
    return tuple(f(p) for p in x)


def frequencies(length):
    root = math.exp(math.log(alpha_corner) / length)
    listed = []
    for j in range(length // 2 + 1):
        angle = 2.0 * math.pi * j / length
        if j == 0 or 2 * j == length:
            listed.append((j, (1.0 - root * math.cos(angle),)))
        else:
            listed.append((j, (1.0 - root * math.cos(angle), root * math.sin(angle))))
    return listed


def planes(length):
    return sum(len(shift) for unused, shift in frequencies(length))


def turn(j, n, length):
    count = j * n % length
    if 4 * count % length == 0:
        return ((1.0, 0.0), (0.0, 1.0), (-1.0, 0.0), (0.0, -1.0))[4 * count // length]
    angle = 2.0 * math.pi * count / length
    return (math.cos(angle), math.sin(angle))


def weighted(total, weight, value):
    if weight == 0.0:
        return total
    if weight == 1.0:
        term = value
    elif weight == -1.0:
        return -value if total is None else total - value
    else:
        term = weight * value
    return term if total is None else total + term


def start_all(pairs, sems):
    copies = [
        pltpu.make_async_copy(source, target, sems.at[index])
        for index, (source, target) in enumerate(pairs)
    ]
    for copy in copies:
        copy.start()
    return copies


def stack_kernel(forcing_hbm, previous_hbm, mine_ref, other_ref, sems):
    species = lax.axis_index("tm") % 2
    pairs = (
        (forcing_hbm.at[0, species], mine_ref.at[0]),
        (previous_hbm.at[0, species], mine_ref.at[1]),
        (forcing_hbm.at[0, 1 - species], other_ref.at[0]),
        (previous_hbm.at[0, 1 - species], other_ref.at[1]),
    )
    for copy in start_all(pairs, sems):
        copy.wait()


def factor_kernel(
    length,
    initial_hbm,
    zones_hbm,
    drift_hbm,
    zone_hbm,
    flag_hbm,
    faces_hbm,
    near_ref,
    far_ref,
    initial_ref,
    zones_ref,
    drift_ref,
    zone_ref,
    flag_ref,
    faces_ref,
    sems,
):
    species = lax.axis_index("tm") % 2
    pairs = (
        (zones_hbm, zones_ref),
        (drift_hbm, drift_ref),
        (zone_hbm, zone_ref),
        (flag_hbm, flag_ref),
        (faces_hbm, faces_ref),
        (initial_hbm.at[species], initial_ref),
    )
    for copy in start_all(pairs, sems):
        copy.wait()
    zone = zone_ref[...]
    diffusion = jnp.zeros(zone.shape, jnp.float32)
    for index in range(zones_ref.shape[1]):
        diffusion = jnp.where(zone == index, zones_ref[species, index], diffusion)
    drift = drift_ref[species]
    cells, lanes = faces_ref.shape
    faces = faces_ref[...].astype(jnp.float32)
    row = lax.broadcasted_iota(jnp.int32, (cells, lanes), 0)
    link_above = jnp.where(row == cells - 1, 0.0, faces)
    link_below = jnp.where(row == 0, 0.0, roll_down(faces, 1))
    ground = jnp.where(row == 0, flag_ref[...].astype(jnp.float32), 0.0)
    below = -(diffusion + drift) * link_below
    above = -diffusion * link_above
    centre = diffusion * (link_below + link_above) + drift + 2.0 * diffusion * ground
    plane = 0
    for unused, shift in frequencies(length):
        parts = len(shift)
        a = (below,)
        c = (above,)
        b = (centre + shift[0],)
        if parts == 2:
            b = b + (jnp.full_like(centre, shift[1]),)
        for step in range(near_steps):
            distance = 1 << step
            inverse = c_inverse(b)
            low = c_neg(c_mul(a, c_map(lambda p: roll_down(p, distance), inverse)))
            high = c_neg(c_mul(c, c_map(lambda p: roll_up(p, distance), inverse)))
            down_c = c_map(lambda p: roll_down(p, distance), c)
            up_a = c_map(lambda p: roll_up(p, distance), a)
            b = c_add(b, c_add(c_mul(low, down_c), c_mul(high, up_a)))
            a = c_mul(low, c_map(lambda p: roll_down(p, distance), a))
            c = c_mul(high, c_map(lambda p: roll_up(p, distance), c))
            for part in range(parts):
                near_ref[plane + part, 2 * step] = low[part]
                near_ref[plane + part, 2 * step + 1] = high[part]
        carry = None
        for block in range(cells // tile):
            rows = slice(block * tile, (block + 1) * tile)
            ak, bk, ck = (c_map(lambda p: p[rows], item) for item in (a, b, c))
            if carry is None:
                eliminate = c_map(jnp.zeros_like, ak)
            else:
                eliminate = c_mul(ak, carry[0])
                bk = c_sub(bk, c_mul(eliminate, carry[1]))
            inverse = c_inverse(bk)
            substitute = c_mul(ck, inverse)
            for part in range(parts):
                far_ref[plane + part, 0, rows] = eliminate[part]
                far_ref[plane + part, 1, rows] = inverse[part]
                far_ref[plane + part, 2, rows] = substitute[part]
            carry = (inverse, ck)
        plane += parts


def in_order(me, held):
    bit = 1
    while bit < len(held):
        swap = (me & bit) != 0
        held = [
            jnp.where(swap, held[index ^ bit], held[index]) for index in range(len(held))
        ]
        bit *= 2
    return held


def sweep_kernel(length, *refs):
    stacks = refs[:length]
    initial_ref, near_ref, far_ref, own_ref, give_ref, sum_ref = refs[length:]
    cells, lanes = initial_ref.shape
    log_alpha = math.log(alpha_corner)
    me = lax.axis_index("tm")
    loads = in_order(me, [ref[0] for ref in stacks])
    befores = in_order(me, [ref[1] for ref in stacks])
    loads[0] = loads[0] + (initial_ref[...] - alpha_corner * befores[length - 1])
    scaled = [math.exp(log_alpha * n / length) * load for n, load in enumerate(loads)]
    spectrum = []
    plane = 0
    for j, shift in frequencies(length):
        parts = len(shift)
        rhs = [None] * parts
        for n in range(length):
            weights = turn(j, -n, length)
            for part in range(parts):
                rhs[part] = weighted(rhs[part], weights[part], scaled[n])
        rhs = tuple(rhs)
        for step in range(near_steps):
            distance = 1 << step
            low = tuple(near_ref[plane + p, 2 * step] for p in range(parts))
            high = tuple(near_ref[plane + p, 2 * step + 1] for p in range(parts))
            down = c_map(lambda p: roll_down(p, distance), rhs)
            up = c_map(lambda p: roll_up(p, distance), rhs)
            rhs = c_add(rhs, c_add(c_mul(low, down), c_mul(high, up)))
        blocks = []
        carry = None
        for block in range(cells // tile):
            rows = slice(block * tile, (block + 1) * tile)
            value = c_map(lambda p: p[rows], rhs)
            if carry is not None:
                eliminate = tuple(far_ref[plane + p, 0, rows] for p in range(parts))
                value = c_sub(value, c_mul(eliminate, carry))
            blocks.append(value)
            carry = value
        solved = [None] * len(blocks)
        carry = None
        for block in reversed(range(cells // tile)):
            rows = slice(block * tile, (block + 1) * tile)
            inverse = tuple(far_ref[plane + p, 1, rows] for p in range(parts))
            value = c_mul(inverse, blocks[block])
            if carry is not None:
                substitute = tuple(far_ref[plane + p, 2, rows] for p in range(parts))
                value = c_sub(value, c_mul(substitute, carry))
            solved[block] = value
            carry = value
        spectrum.append((j, parts, solved))
        plane += parts
    total = jnp.zeros((tile, lanes), jnp.float32)
    for block in range(cells // tile):
        rows = slice(block * tile, (block + 1) * tile)
        steps = []
        for n in range(length):
            fresh = None
            for j, parts, solved in spectrum:
                weights = turn(j, n, length)
                fresh = weighted(fresh, parts * weights[0], solved[block][0])
                if parts == 2:
                    fresh = weighted(fresh, -parts * weights[1], solved[block][1])
            fresh = fresh * (math.exp(-log_alpha * n / length) / length)
            steps.append(fresh)
            change = fresh - befores[n][rows]
            total = total + change * change
        own = steps[0]
        give = steps[1]
        for n in range(1, length):
            own = jnp.where(me == n, steps[n], own)
            give = jnp.where(me == n, steps[n ^ 1], give)
        own_ref[rows] = own
        give_ref[rows] = give
    sum_ref[...] = jnp.broadcast_to(jnp.sum(total, axis=0, keepdims=True), sum_ref.shape)


def join_kernel(
    entry_count, own_ref, got_ref, squares_ref, new_hbm, norm_hbm, norm_ref, sems
):
    species = lax.axis_index("tm") % 2
    copies = (
        pltpu.make_async_copy(own_ref, new_hbm.at[0, species], sems.at[0]),
        pltpu.make_async_copy(got_ref, new_hbm.at[0, 1 - species], sems.at[1]),
        pltpu.make_async_copy(norm_ref, norm_hbm, sems.at[2]),
    )
    copies[0].start()
    copies[1].start()
    norm_ref[0, 0] = jnp.sqrt(jnp.sum(squares_ref[...]) / entry_count)
    copies[2].start()
    for copy in copies:
        copy.wait()


def exchange(value, axis, bits):
    pairs = [(index, index ^ bits) for index in range(lax.axis_size(axis))]
    return lax.ppermute(value, axis, pairs)


def shards(
    forcing,
    initial_state,
    previous,
    zone_diffusion,
    drift_rate,
    column_zone,
    bottom_flag,
    open_faces,
):
    length = lax.axis_size("tm")
    space = lax.axis_size("space")
    cells, lanes = open_faces.shape
    whole = pl.BlockSpec(memory_space=pltpu.VMEM)
    outside = pl.BlockSpec(memory_space=pltpu.HBM)
    count = planes(length)
    params = pltpu.CompilerParams(vmem_limit_bytes=40 * 1024 * 1024)
    alone = pltpu.CompilerParams(vmem_limit_bytes=56 * 1024 * 1024)
    mine, other = pl.pallas_call(
        stack_kernel,
        out_shape=(
            pltpu.VMEM((2, cells, lanes), jnp.float32),
            pltpu.VMEM((2, cells, lanes), jnp.float32),
        ),
        in_specs=[outside] * 2,
        out_specs=[whole] * 2,
        scratch_shapes=[pltpu.SemaphoreType.DMA((4,))],
        compiler_params=alone,
        cost_estimate=pl.CostEstimate(flops=4000, bytes_accessed=500000, transcendentals=0),
        name="stack_arrays",
    )(forcing, previous)
    stacks = [mine]
    for bits in range(1, length):
        stacks.append(exchange(other if bits % 2 else mine, "tm", bits))
    near, far, initial = pl.pallas_call(
        functools.partial(factor_kernel, length),
        out_shape=(
            pltpu.VMEM((count, 2 * near_steps, cells, lanes), jnp.float32),
            pltpu.VMEM((count, 3, cells, lanes), jnp.float32),
            pltpu.VMEM((cells, lanes), jnp.float32),
        ),
        in_specs=[outside] * 6,
        out_specs=[whole] * 3,
        scratch_shapes=[
            pltpu.SMEM(zone_diffusion.shape, jnp.float32),
            pltpu.SMEM(drift_rate.shape, jnp.float32),
            pltpu.VMEM((1, lanes), jnp.int32),
            pltpu.VMEM((1, lanes), jnp.int32),
            pltpu.VMEM((cells, lanes), jnp.int32),
            pltpu.SemaphoreType.DMA((6,)),
        ],
        compiler_params=alone,
        cost_estimate=pl.CostEstimate(flops=4000000, bytes_accessed=3000000, transcendentals=0),
        name="factor_lines",
    )(initial_state, zone_diffusion, drift_rate, column_zone[None], bottom_flag[None], open_faces)
    own, give, squares = pl.pallas_call(
        functools.partial(sweep_kernel, length),
        out_shape=(
            pltpu.VMEM((cells, lanes), jnp.float32),
            pltpu.VMEM((cells, lanes), jnp.float32),
            pltpu.VMEM((2 * space, 1, lanes), jnp.float32),
        ),
        in_specs=[whole] * (length + 3),
        out_specs=[whole] * 3,
        compiler_params=params,
        cost_estimate=pl.CostEstimate(flops=4000000, bytes_accessed=3000000, transcendentals=0),
        name="solve_lines",
    )(*stacks, initial, near, far)
    got = exchange(give, "tm", 1)
    order = [*reversed(range(space)), *reversed(range(space, 2 * space))]
    groups = [[step * space + index for index in order] for step in range(0, length, 2)]
    squares = lax.all_to_all(
        squares, ("tm", "space"), 0, 0, axis_index_groups=groups, tiled=True
    )
    entry_count = length * space * forcing.shape[1] * cells * lanes
    new_iterate, norm = pl.pallas_call(
        functools.partial(join_kernel, entry_count),
        out_shape=(
            jax.ShapeDtypeStruct(forcing.shape, jnp.float32),
            jax.ShapeDtypeStruct((1, 1), jnp.float32),
        ),
        in_specs=[whole] * 3,
        out_specs=(outside, outside),
        scratch_shapes=[pltpu.SMEM((1, 1), jnp.float32), pltpu.SemaphoreType.DMA((3,))],
        compiler_params=params,
        cost_estimate=pl.CostEstimate(flops=4000, bytes_accessed=100000, transcendentals=0),
        name="join_species",
    )(own, got, squares)
    return (new_iterate, norm[0, 0])


def solution(mesh):
    placed = (
        P("tm", None, None, "space"),
        P(None, None, "space"),
        P("tm", None, None, "space"),
        P(),
        P(),
        P("space"),
        P("space"),
        P(None, "space"),
    )
    return jax.shard_map(
        shards,
        mesh=mesh,
        in_specs=placed,
        out_specs=(P("tm", None, None, "space"), P()),
        check_vma=False,
    )
```

```python
import functools
import math

import jax
import jax.numpy as jnp
from jax import lax
from jax.experimental import pallas as pl
from jax.experimental.pallas import tpu as pltpu
from jax.sharding import PartitionSpec as P

alpha_corner = 0.3
tile = 8
near_steps = 3


def roll_down(block, distance):
    return pltpu.roll(block, distance, 0)


def roll_up(block, distance):
    return pltpu.roll(block, block.shape[0] - distance, 0)


def c_mul(x, y):
    if len(x) == 1 and len(y) == 1:
        return (x[0] * y[0],)
    if len(x) == 1:
        return (x[0] * y[0], x[0] * y[1])
    if len(y) == 1:
        return (x[0] * y[0], x[1] * y[0])
    return (x[0] * y[0] - x[1] * y[1], x[0] * y[1] + x[1] * y[0])


def c_add(x, y):
    return tuple(p + q for p, q in zip(x, y))


def c_sub(x, y):
    return tuple(p - q for p, q in zip(x, y))


def c_neg(x):
    return tuple(-p for p in x)


def c_inverse(x):
    if len(x) == 1:
        return (1.0 / x[0],)
    scale = 1.0 / (x[0] * x[0] + x[1] * x[1])
    return (x[0] * scale, -x[1] * scale)


def c_map(f, x):
    return tuple(f(p) for p in x)


def frequencies(length):
    root = math.exp(math.log(alpha_corner) / length)
    listed = []
    for j in range(length // 2 + 1):
        angle = 2.0 * math.pi * j / length
        if j == 0 or 2 * j == length:
            listed.append((j, (1.0 - root * math.cos(angle),)))
        else:
            listed.append((j, (1.0 - root * math.cos(angle), root * math.sin(angle))))
    return listed


def planes(length):
    return sum(len(shift) for unused, shift in frequencies(length))


def turn(j, n, length):
    count = j * n % length
    if 4 * count % length == 0:
        return ((1.0, 0.0), (0.0, 1.0), (-1.0, 0.0), (0.0, -1.0))[4 * count // length]
    angle = 2.0 * math.pi * count / length
    return (math.cos(angle), math.sin(angle))


def weighted(total, weight, value):
    if weight == 0.0:
        return total
    if weight == 1.0:
        term = value
    elif weight == -1.0:
        return -value if total is None else total - value
    else:
        term = weight * value
    return term if total is None else total + term


def start_all(pairs, sems):
    copies = [
        pltpu.make_async_copy(source, target, sems.at[index])
        for index, (source, target) in enumerate(pairs)
    ]
    for copy in copies:
        copy.start()
    return copies


def stack_kernel(forcing_hbm, previous_hbm, mine_ref, other_ref, sems):
    species = lax.axis_index("tm") % 2
    pairs = (
        (forcing_hbm.at[0, species], mine_ref.at[0]),
        (previous_hbm.at[0, species], mine_ref.at[1]),
        (forcing_hbm.at[0, 1 - species], other_ref.at[0]),
        (previous_hbm.at[0, 1 - species], other_ref.at[1]),
    )
    for copy in start_all(pairs, sems):
        copy.wait()


def factor_kernel(
    length,
    initial_hbm,
    zones_hbm,
    drift_hbm,
    zone_hbm,
    flag_hbm,
    faces_hbm,
    near_ref,
    far_ref,
    initial_ref,
    zones_ref,
    drift_ref,
    zone_ref,
    flag_ref,
    faces_ref,
    sems,
):
    species = lax.axis_index("tm") % 2
    pairs = (
        (zones_hbm, zones_ref),
        (drift_hbm, drift_ref),
        (zone_hbm, zone_ref),
        (flag_hbm, flag_ref),
        (faces_hbm, faces_ref),
        (initial_hbm.at[species], initial_ref),
    )
    for copy in start_all(pairs, sems):
        copy.wait()
    zone = zone_ref[...]
    diffusion = jnp.zeros(zone.shape, jnp.float32)
    for index in range(zones_ref.shape[1]):
        diffusion = jnp.where(zone == index, zones_ref[species, index], diffusion)
    drift = drift_ref[species]
    cells, lanes = faces_ref.shape
    faces = faces_ref[...].astype(jnp.float32)
    row = lax.broadcasted_iota(jnp.int32, (cells, lanes), 0)
    link_above = jnp.where(row == cells - 1, 0.0, faces)
    link_below = jnp.where(row == 0, 0.0, roll_down(faces, 1))
    ground = jnp.where(row == 0, flag_ref[...].astype(jnp.float32), 0.0)
    below = -(diffusion + drift) * link_below
    above = -diffusion * link_above
    centre = diffusion * (link_below + link_above) + drift + 2.0 * diffusion * ground
    plane = 0
    for unused, shift in frequencies(length):
        parts = len(shift)
        a = (below,)
        c = (above,)
        b = (centre + shift[0],)
        if parts == 2:
            b = b + (jnp.full_like(centre, shift[1]),)
        for step in range(near_steps):
            distance = 1 << step
            inverse = c_inverse(b)
            low = c_neg(c_mul(a, c_map(lambda p: roll_down(p, distance), inverse)))
            high = c_neg(c_mul(c, c_map(lambda p: roll_up(p, distance), inverse)))
            down_c = c_map(lambda p: roll_down(p, distance), c)
            up_a = c_map(lambda p: roll_up(p, distance), a)
            b = c_add(b, c_add(c_mul(low, down_c), c_mul(high, up_a)))
            a = c_mul(low, c_map(lambda p: roll_down(p, distance), a))
            c = c_mul(high, c_map(lambda p: roll_up(p, distance), c))
            for part in range(parts):
                near_ref[plane + part, 2 * step] = low[part]
                near_ref[plane + part, 2 * step + 1] = high[part]
        carry = None
        for block in range(cells // tile):
            rows = slice(block * tile, (block + 1) * tile)
            ak, bk, ck = (c_map(lambda p: p[rows], item) for item in (a, b, c))
            if carry is None:
                eliminate = c_map(jnp.zeros_like, ak)
            else:
                eliminate = c_mul(ak, carry[0])
                bk = c_sub(bk, c_mul(eliminate, carry[1]))
            inverse = c_inverse(bk)
            substitute = c_mul(ck, inverse)
            for part in range(parts):
                far_ref[plane + part, 0, rows] = eliminate[part]
                far_ref[plane + part, 1, rows] = inverse[part]
                far_ref[plane + part, 2, rows] = substitute[part]
            carry = (inverse, ck)
        plane += parts


def in_order(me, held):
    bit = 1
    while bit < len(held):
        swap = (me & bit) != 0
        held = [
            jnp.where(swap, held[index ^ bit], held[index]) for index in range(len(held))
        ]
        bit *= 2
    return held


def sweep_kernel(length, *refs):
    stacks = refs[:length]
    initial_ref, near_ref, far_ref, own_ref, give_ref, sum_ref = refs[length:]
    cells, lanes = initial_ref.shape
    log_alpha = math.log(alpha_corner)
    me = lax.axis_index("tm")
    loads = in_order(me, [ref[0] for ref in stacks])
    befores = in_order(me, [ref[1] for ref in stacks])
    loads[0] = loads[0] + (initial_ref[...] - alpha_corner * befores[length - 1])
    scaled = [math.exp(log_alpha * n / length) * load for n, load in enumerate(loads)]
    spectrum = []
    plane = 0
    for j, shift in frequencies(length):
        parts = len(shift)
        rhs = [None] * parts
        for n in range(length):
            weights = turn(j, -n, length)
            for part in range(parts):
                rhs[part] = weighted(rhs[part], weights[part], scaled[n])
        rhs = tuple(rhs)
        for step in range(near_steps):
            distance = 1 << step
            low = tuple(near_ref[plane + p, 2 * step] for p in range(parts))
            high = tuple(near_ref[plane + p, 2 * step + 1] for p in range(parts))
            down = c_map(lambda p: roll_down(p, distance), rhs)
            up = c_map(lambda p: roll_up(p, distance), rhs)
            rhs = c_add(rhs, c_add(c_mul(low, down), c_mul(high, up)))
        blocks = []
        carry = None
        for block in range(cells // tile):
            rows = slice(block * tile, (block + 1) * tile)
            value = c_map(lambda p: p[rows], rhs)
            if carry is not None:
                eliminate = tuple(far_ref[plane + p, 0, rows] for p in range(parts))
                value = c_sub(value, c_mul(eliminate, carry))
            blocks.append(value)
            carry = value
        solved = [None] * len(blocks)
        carry = None
        for block in reversed(range(cells // tile)):
            rows = slice(block * tile, (block + 1) * tile)
            inverse = tuple(far_ref[plane + p, 1, rows] for p in range(parts))
            value = c_mul(inverse, blocks[block])
            if carry is not None:
                substitute = tuple(far_ref[plane + p, 2, rows] for p in range(parts))
                value = c_sub(value, c_mul(substitute, carry))
            solved[block] = value
            carry = value
        spectrum.append((j, parts, solved))
        plane += parts
    total = jnp.zeros((tile, lanes), jnp.float32)
    for block in range(cells // tile):
        rows = slice(block * tile, (block + 1) * tile)
        steps = []
        for n in range(length):
            fresh = None
            for j, parts, solved in spectrum:
                weights = turn(j, n, length)
                fresh = weighted(fresh, parts * weights[0], solved[block][0])
                if parts == 2:
                    fresh = weighted(fresh, -parts * weights[1], solved[block][1])
            fresh = fresh * (math.exp(-log_alpha * n / length) / length)
            steps.append(fresh)
            change = fresh - befores[n][rows]
            total = total + change * change
        own = steps[0]
        give = steps[1]
        for n in range(1, length):
            own = jnp.where(me == n, steps[n], own)
            give = jnp.where(me == n, steps[n ^ 1], give)
        own_ref[rows] = own
        give_ref[rows] = give
    sum_ref[...] = jnp.broadcast_to(jnp.sum(total, axis=0, keepdims=True), sum_ref.shape)


def join_kernel(
    entry_count, own_ref, got_ref, squares_ref, new_hbm, norm_hbm, norm_ref, sems
):
    species = lax.axis_index("tm") % 2
    copies = (
        pltpu.make_async_copy(own_ref, new_hbm.at[0, species], sems.at[0]),
        pltpu.make_async_copy(got_ref, new_hbm.at[0, 1 - species], sems.at[1]),
        pltpu.make_async_copy(norm_ref, norm_hbm, sems.at[2]),
    )
    copies[0].start()
    copies[1].start()
    norm_ref[0, 0] = jnp.sqrt(jnp.sum(squares_ref[...]) / entry_count)
    copies[2].start()
    for copy in copies:
        copy.wait()


def exchange(value, axis, bits):
    pairs = [(index, index ^ bits) for index in range(lax.axis_size(axis))]
    return lax.ppermute(value, axis, pairs)


def shards(
    forcing,
    initial_state,
    previous,
    zone_diffusion,
    drift_rate,
    column_zone,
    bottom_flag,
    open_faces,
):
    length = lax.axis_size("tm")
    space = lax.axis_size("space")
    cells, lanes = open_faces.shape
    whole = pl.BlockSpec(memory_space=pltpu.VMEM)
    outside = pl.BlockSpec(memory_space=pltpu.HBM)
    count = planes(length)
    params = pltpu.CompilerParams(vmem_limit_bytes=40 * 1024 * 1024)
    alone = pltpu.CompilerParams(vmem_limit_bytes=56 * 1024 * 1024)
    mine, other = pl.pallas_call(
        stack_kernel,
        out_shape=(
            pltpu.VMEM((2, cells, lanes), jnp.float32),
            pltpu.VMEM((2, cells, lanes), jnp.float32),
        ),
        in_specs=[outside] * 2,
        out_specs=[whole] * 2,
        scratch_shapes=[pltpu.SemaphoreType.DMA((4,))],
        compiler_params=alone,
        cost_estimate=pl.CostEstimate(flops=4000, bytes_accessed=500000, transcendentals=0),
        name="stack_arrays",
    )(forcing, previous)
    stacks = [mine]
    for bits in range(1, length):
        stacks.append(exchange(other if bits % 2 else mine, "tm", bits))
    near, far, initial = pl.pallas_call(
        functools.partial(factor_kernel, length),
        out_shape=(
            pltpu.VMEM((count, 2 * near_steps, cells, lanes), jnp.float32),
            pltpu.VMEM((count, 3, cells, lanes), jnp.float32),
            pltpu.VMEM((cells, lanes), jnp.float32),
        ),
        in_specs=[outside] * 6,
        out_specs=[whole] * 3,
        scratch_shapes=[
            pltpu.SMEM(zone_diffusion.shape, jnp.float32),
            pltpu.SMEM(drift_rate.shape, jnp.float32),
            pltpu.VMEM((1, lanes), jnp.int32),
            pltpu.VMEM((1, lanes), jnp.int32),
            pltpu.VMEM((cells, lanes), jnp.int32),
            pltpu.SemaphoreType.DMA((6,)),
        ],
        compiler_params=alone,
        cost_estimate=pl.CostEstimate(flops=4000000, bytes_accessed=3000000, transcendentals=0),
        name="factor_lines",
    )(initial_state, zone_diffusion, drift_rate, column_zone[None], bottom_flag[None], open_faces)
    own, give, squares = pl.pallas_call(
        functools.partial(sweep_kernel, length),
        out_shape=(
            pltpu.VMEM((cells, lanes), jnp.float32),
            pltpu.VMEM((cells, lanes), jnp.float32),
            pltpu.VMEM((1, lanes), jnp.float32),
        ),
        in_specs=[whole] * (length + 3),
        out_specs=[whole] * 3,
        compiler_params=params,
        cost_estimate=pl.CostEstimate(flops=4000000, bytes_accessed=3000000, transcendentals=0),
        name="solve_lines",
    )(*stacks, initial, near, far)
    got = exchange(give, "tm", 1)
    last = 2 * space - 1
    order = [last, *range(2, last, 2), *range(3, last, 2), 1, 0]
    groups = [[step * space + index for index in order] for step in range(0, length, 2)]
    squares = lax.all_gather(squares, ("tm", "space"), axis_index_groups=groups, tiled=True)
    entry_count = length * space * forcing.shape[1] * cells * lanes
    new_iterate, norm = pl.pallas_call(
        functools.partial(join_kernel, entry_count),
        out_shape=(
            jax.ShapeDtypeStruct(forcing.shape, jnp.float32),
            jax.ShapeDtypeStruct((1, 1), jnp.float32),
        ),
        in_specs=[whole] * 3,
        out_specs=(outside, outside),
        scratch_shapes=[pltpu.SMEM((1, 1), jnp.float32), pltpu.SemaphoreType.DMA((3,))],
        compiler_params=params,
        cost_estimate=pl.CostEstimate(flops=4000, bytes_accessed=100000, transcendentals=0),
        name="join_species",
    )(own, got, squares)
    return (new_iterate, norm[0, 0])


def solution(mesh):
    placed = (
        P("tm", None, None, "space"),
        P(None, None, "space"),
        P("tm", None, None, "space"),
        P(),
        P(),
        P("space"),
        P("space"),
        P(None, "space"),
    )
    return jax.shard_map(
        shards,
        mesh=mesh,
        in_specs=placed,
        out_specs=(P("tm", None, None, "space"), P()),
        check_vma=False,
    )
```

```python
import functools
import math

import jax
import jax.numpy as jnp
from jax import lax
from jax.experimental import pallas as pl
from jax.experimental.pallas import tpu as pltpu
from jax.sharding import PartitionSpec as P

alpha_corner = 0.3
tile = 8
near_steps = 3


def roll_down(block, distance):
    return pltpu.roll(block, distance, 0)


def roll_up(block, distance):
    return pltpu.roll(block, block.shape[0] - distance, 0)


def c_mul(x, y):
    if len(x) == 1 and len(y) == 1:
        return (x[0] * y[0],)
    if len(x) == 1:
        return (x[0] * y[0], x[0] * y[1])
    if len(y) == 1:
        return (x[0] * y[0], x[1] * y[0])
    return (x[0] * y[0] - x[1] * y[1], x[0] * y[1] + x[1] * y[0])


def c_add(x, y):
    return tuple(p + q for p, q in zip(x, y))


def c_sub(x, y):
    return tuple(p - q for p, q in zip(x, y))


def c_neg(x):
    return tuple(-p for p in x)


def c_inverse(x):
    if len(x) == 1:
        return (1.0 / x[0],)
    scale = 1.0 / (x[0] * x[0] + x[1] * x[1])
    return (x[0] * scale, -x[1] * scale)


def c_map(f, x):
    return tuple(f(p) for p in x)


def frequencies(length):
    root = math.exp(math.log(alpha_corner) / length)
    listed = []
    for j in range(length // 2 + 1):
        angle = 2.0 * math.pi * j / length
        if j == 0 or 2 * j == length:
            listed.append((j, (1.0 - root * math.cos(angle),)))
        else:
            listed.append((j, (1.0 - root * math.cos(angle), root * math.sin(angle))))
    return listed


def planes(length):
    return sum(len(shift) for unused, shift in frequencies(length))


def turn(j, n, length):
    count = j * n % length
    if 4 * count % length == 0:
        return ((1.0, 0.0), (0.0, 1.0), (-1.0, 0.0), (0.0, -1.0))[4 * count // length]
    angle = 2.0 * math.pi * count / length
    return (math.cos(angle), math.sin(angle))


def weighted(total, weight, value):
    if weight == 0.0:
        return total
    if weight == 1.0:
        term = value
    elif weight == -1.0:
        return -value if total is None else total - value
    else:
        term = weight * value
    return term if total is None else total + term


def start_all(pairs, sems):
    copies = [
        pltpu.make_async_copy(source, target, sems.at[index])
        for index, (source, target) in enumerate(pairs)
    ]
    for copy in copies:
        copy.start()
    return copies


def line_operator(cells, lanes, species, zones_ref, drift_ref, zone_ref, flag_ref, faces_ref):
    zone = zone_ref[...]
    diffusion = jnp.zeros(zone.shape, jnp.float32)
    for index in range(zones_ref.shape[1]):
        diffusion = jnp.where(zone == index, zones_ref[species, index], diffusion)
    drift = drift_ref[species]
    faces = faces_ref[...].astype(jnp.float32)
    row = lax.broadcasted_iota(jnp.int32, (cells, lanes), 0)
    link_above = jnp.where(row == cells - 1, 0.0, faces)
    link_below = jnp.where(row == 0, 0.0, roll_down(faces, 1))
    ground = jnp.where(row == 0, flag_ref[...].astype(jnp.float32), 0.0)
    below = -(diffusion + drift) * link_below
    above = -diffusion * link_above
    centre = diffusion * (link_below + link_above) + drift + 2.0 * diffusion * ground
    return (below, centre, above)


def stack_kernel(
    length,
    forcing_hbm,
    previous_hbm,
    zones_hbm,
    drift_hbm,
    zone_hbm,
    flag_hbm,
    faces_hbm,
    mine_ref,
    mine_before_ref,
    other_ref,
    other_before_ref,
    zones_ref,
    drift_ref,
    zone_ref,
    flag_ref,
    faces_ref,
    sems,
):
    me = lax.axis_index("tm")
    species = me % 2
    pairs = (
        (forcing_hbm.at[0, species], mine_ref),
        (previous_hbm.at[0, species], mine_before_ref),
        (forcing_hbm.at[0, 1 - species], other_ref),
        (previous_hbm.at[0, 1 - species], other_before_ref),
        (zones_hbm, zones_ref),
        (drift_hbm, drift_ref),
        (zone_hbm, zone_ref),
        (flag_hbm, flag_ref),
        (faces_hbm, faces_ref),
    )
    for copy in start_all(pairs, sems):
        copy.wait()

    @pl.when(me == length - 1)
    def shift_load():
        cells, lanes = faces_ref.shape
        for part, before in ((species, mine_before_ref[...]), (1 - species, other_before_ref[...])):
            below, centre, above = line_operator(
                cells, lanes, part, zones_ref, drift_ref, zone_ref, flag_ref, faces_ref
            )
            applied = (
                before
                + centre * before
                + below * roll_down(before, 1)
                + above * roll_up(before, 1)
            )
            if part is species:
                mine_ref[...] = mine_ref[...] - applied
            else:
                other_ref[...] = other_ref[...] - applied


def factor_kernel(
    length,
    initial_hbm,
    previous_hbm,
    zones_hbm,
    drift_hbm,
    zone_hbm,
    flag_hbm,
    faces_hbm,
    near_ref,
    far_ref,
    initial_ref,
    other_before_ref,
    zones_ref,
    drift_ref,
    zone_ref,
    flag_ref,
    faces_ref,
    sems,
):
    species = lax.axis_index("tm") % 2
    pairs = (
        (zones_hbm, zones_ref),
        (drift_hbm, drift_ref),
        (zone_hbm, zone_ref),
        (flag_hbm, flag_ref),
        (faces_hbm, faces_ref),
        (initial_hbm.at[species], initial_ref),
        (previous_hbm.at[0, 1 - species], other_before_ref),
    )
    for copy in start_all(pairs, sems):
        copy.wait()
    cells, lanes = faces_ref.shape
    below, centre, above = line_operator(
        cells, lanes, species, zones_ref, drift_ref, zone_ref, flag_ref, faces_ref
    )
    plane = 0
    for unused, shift in frequencies(length):
        parts = len(shift)
        a = (below,)
        c = (above,)
        b = (centre + shift[0],)
        if parts == 2:
            b = b + (jnp.full_like(centre, shift[1]),)
        for step in range(near_steps):
            distance = 1 << step
            inverse = c_inverse(b)
            low = c_neg(c_mul(a, c_map(lambda p: roll_down(p, distance), inverse)))
            high = c_neg(c_mul(c, c_map(lambda p: roll_up(p, distance), inverse)))
            down_c = c_map(lambda p: roll_down(p, distance), c)
            up_a = c_map(lambda p: roll_up(p, distance), a)
            b = c_add(b, c_add(c_mul(low, down_c), c_mul(high, up_a)))
            a = c_mul(low, c_map(lambda p: roll_down(p, distance), a))
            c = c_mul(high, c_map(lambda p: roll_up(p, distance), c))
            for part in range(parts):
                near_ref[plane + part, 2 * step] = low[part]
                near_ref[plane + part, 2 * step + 1] = high[part]
        carry = None
        for block in range(cells // tile):
            rows = slice(block * tile, (block + 1) * tile)
            ak, bk, ck = (c_map(lambda p: p[rows], item) for item in (a, b, c))
            if carry is None:
                eliminate = c_map(jnp.zeros_like, ak)
            else:
                eliminate = c_mul(ak, carry[0])
                bk = c_sub(bk, c_mul(eliminate, carry[1]))
            inverse = c_inverse(bk)
            substitute = c_mul(ck, inverse)
            for part in range(parts):
                far_ref[plane + part, 0, rows] = eliminate[part]
                far_ref[plane + part, 1, rows] = inverse[part]
                far_ref[plane + part, 2, rows] = substitute[part]
            carry = (inverse, ck)
        plane += parts


def in_order(me, held):
    bit = 1
    while bit < len(held):
        swap = (me & bit) != 0
        held = [
            jnp.where(swap, held[index ^ bit], held[index]) for index in range(len(held))
        ]
        bit *= 2
    return held


def sweep_kernel(length, *refs):
    initial_ref, near_ref, far_ref, own_ref, give_ref = refs[length:]
    cells, lanes = initial_ref.shape
    log_alpha = math.log(alpha_corner)
    me = lax.axis_index("tm")
    loads = in_order(me, [ref[...] for ref in refs[:length]])
    loads[0] = loads[0] + initial_ref[...]
    scaled = [math.exp(log_alpha * n / length) * load for n, load in enumerate(loads)]
    spectrum = []
    plane = 0
    for j, shift in frequencies(length):
        parts = len(shift)
        rhs = [None] * parts
        for n in range(length):
            weights = turn(j, -n, length)
            for part in range(parts):
                rhs[part] = weighted(rhs[part], weights[part], scaled[n])
        rhs = tuple(rhs)
        for step in range(near_steps):
            distance = 1 << step
            low = tuple(near_ref[plane + p, 2 * step] for p in range(parts))
            high = tuple(near_ref[plane + p, 2 * step + 1] for p in range(parts))
            down = c_map(lambda p: roll_down(p, distance), rhs)
            up = c_map(lambda p: roll_up(p, distance), rhs)
            rhs = c_add(rhs, c_add(c_mul(low, down), c_mul(high, up)))
        blocks = []
        carry = None
        for block in range(cells // tile):
            rows = slice(block * tile, (block + 1) * tile)
            value = c_map(lambda p: p[rows], rhs)
            if carry is not None:
                eliminate = tuple(far_ref[plane + p, 0, rows] for p in range(parts))
                value = c_sub(value, c_mul(eliminate, carry))
            blocks.append(value)
            carry = value
        solved = [None] * len(blocks)
        carry = None
        for block in reversed(range(cells // tile)):
            rows = slice(block * tile, (block + 1) * tile)
            inverse = tuple(far_ref[plane + p, 1, rows] for p in range(parts))
            value = c_mul(inverse, blocks[block])
            if carry is not None:
                substitute = tuple(far_ref[plane + p, 2, rows] for p in range(parts))
                value = c_sub(value, c_mul(substitute, carry))
            solved[block] = value
            carry = value
        spectrum.append((j, parts, solved))
        plane += parts
    for block in range(cells // tile):
        rows = slice(block * tile, (block + 1) * tile)
        steps = []
        for n in range(length):
            fresh = None
            for j, parts, solved in spectrum:
                weights = turn(j, n, length)
                fresh = weighted(fresh, parts * weights[0], solved[block][0])
                if parts == 2:
                    fresh = weighted(fresh, -parts * weights[1], solved[block][1])
            fresh = fresh * (math.exp(-log_alpha * n / length) / length)
            steps.append(fresh)
        own = steps[0]
        give = steps[1]
        for n in range(1, length):
            own = jnp.where(me == n, steps[n], own)
            give = jnp.where(me == n, steps[n ^ 1], give)
        own_ref[rows] = own
        give_ref[rows] = give


def change_kernel(length, own_ref, give_ref, mine_before_ref, beside_before_ref, sum_ref):
    cells, lanes = own_ref.shape
    me = lax.axis_index("tm")
    total = jnp.zeros((tile, lanes), jnp.float32)
    for block in range(cells // tile):
        rows = slice(block * tile, (block + 1) * tile)
        own_before = jnp.where(me == length - 1, 0.0, mine_before_ref[rows])
        give_before = jnp.where(me == (length - 1) ^ 1, 0.0, beside_before_ref[rows])
        own_change = own_ref[rows] - own_before
        give_change = give_ref[rows] - give_before
        total = total + own_change * own_change + give_change * give_change
    sum_ref[...] = jnp.broadcast_to(jnp.sum(total, axis=0, keepdims=True), sum_ref.shape)


def join_kernel(
    length,
    entry_count,
    own_ref,
    got_ref,
    mine_before_ref,
    other_before_ref,
    squares_ref,
    new_hbm,
    norm_hbm,
    mine_ref,
    other_ref,
    norm_ref,
    sems,
):
    me = lax.axis_index("tm")
    species = me % 2
    copies = (
        pltpu.make_async_copy(mine_ref, new_hbm.at[0, species], sems.at[0]),
        pltpu.make_async_copy(other_ref, new_hbm.at[0, 1 - species], sems.at[1]),
        pltpu.make_async_copy(norm_ref, norm_hbm, sems.at[2]),
    )
    last = me == length - 1
    mine_ref[...] = own_ref[...] + jnp.where(last, mine_before_ref[...], 0.0)
    other_ref[...] = got_ref[...] + jnp.where(last, other_before_ref[...], 0.0)
    copies[0].start()
    copies[1].start()
    norm_ref[0, 0] = jnp.sqrt(jnp.sum(squares_ref[...]) / entry_count)
    copies[2].start()
    for copy in copies:
        copy.wait()


def exchange(value, axis, bits):
    pairs = [(index, index ^ bits) for index in range(lax.axis_size(axis))]
    return lax.ppermute(value, axis, pairs)


def shards(
    forcing,
    initial_state,
    previous,
    zone_diffusion,
    drift_rate,
    column_zone,
    bottom_flag,
    open_faces,
):
    length = lax.axis_size("tm")
    space = lax.axis_size("space")
    cells, lanes = open_faces.shape
    whole = pl.BlockSpec(memory_space=pltpu.VMEM)
    outside = pl.BlockSpec(memory_space=pltpu.HBM)
    count = planes(length)
    everyone = length * space
    params = pltpu.CompilerParams(vmem_limit_bytes=40 * 1024 * 1024)
    alone = pltpu.CompilerParams(vmem_limit_bytes=56 * 1024 * 1024)
    mine, mine_before, other = pl.pallas_call(
        functools.partial(stack_kernel, length),
        out_shape=(
            pltpu.VMEM((cells, lanes), jnp.float32),
            pltpu.VMEM((cells, lanes), jnp.float32),
            pltpu.VMEM((cells, lanes), jnp.float32),
        ),
        in_specs=[outside] * 7,
        out_specs=[whole] * 3,
        scratch_shapes=[
            pltpu.VMEM((cells, lanes), jnp.float32),
            pltpu.SMEM(zone_diffusion.shape, jnp.float32),
            pltpu.SMEM(drift_rate.shape, jnp.float32),
            pltpu.VMEM((1, lanes), jnp.int32),
            pltpu.VMEM((1, lanes), jnp.int32),
            pltpu.VMEM((cells, lanes), jnp.int32),
            pltpu.SemaphoreType.DMA((9,)),
        ],
        compiler_params=alone,
        cost_estimate=pl.CostEstimate(flops=4000, bytes_accessed=500000, transcendentals=0),
        name="stack_arrays",
    )(
        forcing,
        previous,
        zone_diffusion,
        drift_rate,
        column_zone[None],
        bottom_flag[None],
        open_faces,
    )
    loads = [mine]
    for bits in range(1, length):
        loads.append(exchange(other if bits % 2 else mine, "tm", bits))
    near, far, initial, other_before = pl.pallas_call(
        functools.partial(factor_kernel, length),
        out_shape=(
            pltpu.VMEM((count, 2 * near_steps, cells, lanes), jnp.float32),
            pltpu.VMEM((count, 3, cells, lanes), jnp.float32),
            pltpu.VMEM((cells, lanes), jnp.float32),
            pltpu.VMEM((cells, lanes), jnp.float32),
        ),
        in_specs=[outside] * 7,
        out_specs=[whole] * 4,
        scratch_shapes=[
            pltpu.SMEM(zone_diffusion.shape, jnp.float32),
            pltpu.SMEM(drift_rate.shape, jnp.float32),
            pltpu.VMEM((1, lanes), jnp.int32),
            pltpu.VMEM((1, lanes), jnp.int32),
            pltpu.VMEM((cells, lanes), jnp.int32),
            pltpu.SemaphoreType.DMA((7,)),
        ],
        compiler_params=alone,
        cost_estimate=pl.CostEstimate(flops=4000000, bytes_accessed=3000000, transcendentals=0),
        name="factor_lines",
    )(
        initial_state,
        previous,
        zone_diffusion,
        drift_rate,
        column_zone[None],
        bottom_flag[None],
        open_faces,
    )
    own, give = pl.pallas_call(
        functools.partial(sweep_kernel, length),
        out_shape=(
            pltpu.VMEM((cells, lanes), jnp.float32),
            pltpu.VMEM((cells, lanes), jnp.float32),
        ),
        in_specs=[whole] * (length + 3),
        out_specs=[whole] * 2,
        compiler_params=params,
        cost_estimate=pl.CostEstimate(flops=4000000, bytes_accessed=3000000, transcendentals=0),
        name="solve_lines",
    )(*loads, initial, near, far)
    got = exchange(give, "tm", 1)
    squares = pl.pallas_call(
        functools.partial(change_kernel, length),
        out_shape=pltpu.VMEM((everyone, 1, lanes), jnp.float32),
        in_specs=[whole] * 4,
        out_specs=whole,
        compiler_params=params,
        cost_estimate=pl.CostEstimate(flops=40000, bytes_accessed=200000, transcendentals=0),
        name="change_squares",
    )(own, give, mine_before, exchange(other_before, "tm", 1))
    first = length // 2 * space + space - 1
    order = [first] + [index for index in reversed(range(everyone)) if index != first]
    squares = lax.all_to_all(
        squares, ("tm", "space"), 0, 0, axis_index_groups=[order], tiled=True
    )
    entry_count = everyone * forcing.shape[1] * cells * lanes
    new_iterate, norm = pl.pallas_call(
        functools.partial(join_kernel, length, entry_count),
        out_shape=(
            jax.ShapeDtypeStruct(forcing.shape, jnp.float32),
            jax.ShapeDtypeStruct((1, 1), jnp.float32),
        ),
        in_specs=[whole] * 5,
        out_specs=(outside, outside),
        scratch_shapes=[
            pltpu.VMEM((cells, lanes), jnp.float32),
            pltpu.VMEM((cells, lanes), jnp.float32),
            pltpu.SMEM((1, 1), jnp.float32),
            pltpu.SemaphoreType.DMA((3,)),
        ],
        compiler_params=params,
        cost_estimate=pl.CostEstimate(flops=4000, bytes_accessed=100000, transcendentals=0),
        name="join_species",
    )(own, got, mine_before, other_before, squares)
    return (new_iterate, norm[0, 0])


def solution(mesh):
    placed = (
        P("tm", None, None, "space"),
        P(None, None, "space"),
        P("tm", None, None, "space"),
        P(),
        P(),
        P("space"),
        P("space"),
        P(None, "space"),
    )
    return jax.shard_map(
        shards,
        mesh=mesh,
        in_specs=placed,
        out_specs=(P("tm", None, None, "space"), P()),
        check_vma=False,
    )
```

```python
import functools
import math

import jax
import jax.numpy as jnp
from jax import lax
from jax.experimental import pallas as pl
from jax.experimental.pallas import tpu as pltpu
from jax.sharding import PartitionSpec as P

alpha_corner = 0.3
tile = 8
near_steps = 3


def roll_down(block, distance):
    return pltpu.roll(block, distance, 0)


def roll_up(block, distance):
    return pltpu.roll(block, block.shape[0] - distance, 0)


def c_mul(x, y):
    if len(x) == 1 and len(y) == 1:
        return (x[0] * y[0],)
    if len(x) == 1:
        return (x[0] * y[0], x[0] * y[1])
    if len(y) == 1:
        return (x[0] * y[0], x[1] * y[0])
    return (x[0] * y[0] - x[1] * y[1], x[0] * y[1] + x[1] * y[0])


def c_add(x, y):
    return tuple(p + q for p, q in zip(x, y))


def c_sub(x, y):
    return tuple(p - q for p, q in zip(x, y))


def c_neg(x):
    return tuple(-p for p in x)


def c_inverse(x):
    if len(x) == 1:
        return (1.0 / x[0],)
    scale = 1.0 / (x[0] * x[0] + x[1] * x[1])
    return (x[0] * scale, -x[1] * scale)


def c_map(f, x):
    return tuple(f(p) for p in x)


def frequencies(length):
    root = math.exp(math.log(alpha_corner) / length)
    listed = []
    for j in range(length // 2 + 1):
        angle = 2.0 * math.pi * j / length
        if j == 0 or 2 * j == length:
            listed.append((j, (1.0 - root * math.cos(angle),)))
        else:
            listed.append((j, (1.0 - root * math.cos(angle), root * math.sin(angle))))
    return listed


def planes(length):
    return sum(len(shift) for unused, shift in frequencies(length))


def turn(j, n, length):
    count = j * n % length
    if 4 * count % length == 0:
        return ((1.0, 0.0), (0.0, 1.0), (-1.0, 0.0), (0.0, -1.0))[4 * count // length]
    angle = 2.0 * math.pi * count / length
    return (math.cos(angle), math.sin(angle))


def weighted(total, weight, value):
    if weight == 0.0:
        return total
    if weight == 1.0:
        term = value
    elif weight == -1.0:
        return -value if total is None else total - value
    else:
        term = weight * value
    return term if total is None else total + term


def start_all(pairs, sems):
    copies = [
        pltpu.make_async_copy(source, target, sems.at[index])
        for index, (source, target) in enumerate(pairs)
    ]
    for copy in copies:
        copy.start()
    return copies


def stack_kernel(forcing_hbm, previous_hbm, mine_ref, other_ref, sems):
    species = lax.axis_index("tm") % 2
    pairs = (
        (forcing_hbm.at[0, species], mine_ref.at[0]),
        (previous_hbm.at[0, species], mine_ref.at[1]),
        (forcing_hbm.at[0, 1 - species], other_ref.at[0]),
        (previous_hbm.at[0, 1 - species], other_ref.at[1]),
    )
    for copy in start_all(pairs, sems):
        copy.wait()


def factor_kernel(
    length,
    initial_hbm,
    zones_hbm,
    drift_hbm,
    zone_hbm,
    flag_hbm,
    faces_hbm,
    near_ref,
    far_ref,
    initial_ref,
    zones_ref,
    drift_ref,
    zone_ref,
    flag_ref,
    faces_ref,
    sems,
):
    species = lax.axis_index("tm") % 2
    pairs = (
        (zones_hbm, zones_ref),
        (drift_hbm, drift_ref),
        (zone_hbm, zone_ref),
        (flag_hbm, flag_ref),
        (faces_hbm, faces_ref),
        (initial_hbm.at[species], initial_ref),
    )
    for copy in start_all(pairs, sems):
        copy.wait()
    zone = zone_ref[...]
    diffusion = jnp.zeros(zone.shape, jnp.float32)
    for index in range(zones_ref.shape[1]):
        diffusion = jnp.where(zone == index, zones_ref[species, index], diffusion)
    drift = drift_ref[species]
    cells, lanes = faces_ref.shape
    faces = faces_ref[...].astype(jnp.float32)
    row = lax.broadcasted_iota(jnp.int32, (cells, lanes), 0)
    link_above = jnp.where(row == cells - 1, 0.0, faces)
    link_below = jnp.where(row == 0, 0.0, roll_down(faces, 1))
    ground = jnp.where(row == 0, flag_ref[...].astype(jnp.float32), 0.0)
    below = -(diffusion + drift) * link_below
    above = -diffusion * link_above
    centre = diffusion * (link_below + link_above) + drift + 2.0 * diffusion * ground
    plane = 0
    for unused, shift in frequencies(length):
        parts = len(shift)
        a = (below,)
        c = (above,)
        b = (centre + shift[0],)
        if parts == 2:
            b = b + (jnp.full_like(centre, shift[1]),)
        for step in range(near_steps):
            distance = 1 << step
            inverse = c_inverse(b)
            low = c_neg(c_mul(a, c_map(lambda p: roll_down(p, distance), inverse)))
            high = c_neg(c_mul(c, c_map(lambda p: roll_up(p, distance), inverse)))
            down_c = c_map(lambda p: roll_down(p, distance), c)
            up_a = c_map(lambda p: roll_up(p, distance), a)
            b = c_add(b, c_add(c_mul(low, down_c), c_mul(high, up_a)))
            a = c_mul(low, c_map(lambda p: roll_down(p, distance), a))
            c = c_mul(high, c_map(lambda p: roll_up(p, distance), c))
            for part in range(parts):
                near_ref[plane + part, 2 * step] = low[part]
                near_ref[plane + part, 2 * step + 1] = high[part]
        carry = None
        for block in range(cells // tile):
            rows = slice(block * tile, (block + 1) * tile)
            ak, bk, ck = (c_map(lambda p: p[rows], item) for item in (a, b, c))
            if carry is None:
                eliminate = c_map(jnp.zeros_like, ak)
            else:
                eliminate = c_mul(ak, carry[0])
                bk = c_sub(bk, c_mul(eliminate, carry[1]))
            inverse = c_inverse(bk)
            substitute = c_mul(ck, inverse)
            for part in range(parts):
                far_ref[plane + part, 0, rows] = eliminate[part]
                far_ref[plane + part, 1, rows] = inverse[part]
                far_ref[plane + part, 2, rows] = substitute[part]
            carry = (inverse, ck)
        plane += parts


def in_order(me, held):
    bit = 1
    while bit < len(held):
        swap = (me & bit) != 0
        held = [
            jnp.where(swap, held[index ^ bit], held[index]) for index in range(len(held))
        ]
        bit *= 2
    return held


def sweep_kernel(length, *refs):
    stacks = refs[:length]
    initial_ref, near_ref, far_ref, own_ref, give_ref, sum_ref = refs[length:]
    cells, lanes = initial_ref.shape
    log_alpha = math.log(alpha_corner)
    me = lax.axis_index("tm")
    loads = in_order(me, [ref[0] for ref in stacks])
    befores = in_order(me, [ref[1] for ref in stacks])
    loads[0] = loads[0] + (initial_ref[...] - alpha_corner * befores[length - 1])
    scaled = [math.exp(log_alpha * n / length) * load for n, load in enumerate(loads)]
    spectrum = []
    plane = 0
    for j, shift in frequencies(length):
        parts = len(shift)
        rhs = [None] * parts
        for n in range(length):
            weights = turn(j, -n, length)
            for part in range(parts):
                rhs[part] = weighted(rhs[part], weights[part], scaled[n])
        rhs = tuple(rhs)
        for step in range(near_steps):
            distance = 1 << step
            low = tuple(near_ref[plane + p, 2 * step] for p in range(parts))
            high = tuple(near_ref[plane + p, 2 * step + 1] for p in range(parts))
            down = c_map(lambda p: roll_down(p, distance), rhs)
            up = c_map(lambda p: roll_up(p, distance), rhs)
            rhs = c_add(rhs, c_add(c_mul(low, down), c_mul(high, up)))
        blocks = []
        carry = None
        for block in range(cells // tile):
            rows = slice(block * tile, (block + 1) * tile)
            value = c_map(lambda p: p[rows], rhs)
            if carry is not None:
                eliminate = tuple(far_ref[plane + p, 0, rows] for p in range(parts))
                value = c_sub(value, c_mul(eliminate, carry))
            blocks.append(value)
            carry = value
        solved = [None] * len(blocks)
        carry = None
        for block in reversed(range(cells // tile)):
            rows = slice(block * tile, (block + 1) * tile)
            inverse = tuple(far_ref[plane + p, 1, rows] for p in range(parts))
            value = c_mul(inverse, blocks[block])
            if carry is not None:
                substitute = tuple(far_ref[plane + p, 2, rows] for p in range(parts))
                value = c_sub(value, c_mul(substitute, carry))
            solved[block] = value
            carry = value
        spectrum.append((j, parts, solved))
        plane += parts
    total = jnp.zeros((tile, lanes), jnp.float32)
    for block in range(cells // tile):
        rows = slice(block * tile, (block + 1) * tile)
        steps = []
        for n in range(length):
            fresh = None
            for j, parts, solved in spectrum:
                weights = turn(j, n, length)
                fresh = weighted(fresh, parts * weights[0], solved[block][0])
                if parts == 2:
                    fresh = weighted(fresh, -parts * weights[1], solved[block][1])
            fresh = fresh * (math.exp(-log_alpha * n / length) / length)
            steps.append(fresh)
            change = fresh - befores[n][rows]
            total = total + change * change
        own = steps[0]
        give = steps[1]
        for n in range(1, length):
            own = jnp.where(me == n, steps[n], own)
            give = jnp.where(me == n, steps[n ^ 1], give)
        own_ref[rows] = own
        give_ref[rows] = give
    sum_ref[...] = jnp.broadcast_to(jnp.sum(total, axis=0, keepdims=True), sum_ref.shape)


def join_kernel(
    entry_count, own_ref, got_ref, squares_ref, new_hbm, norm_hbm, norm_ref, sems
):
    species = lax.axis_index("tm") % 2
    copies = (
        pltpu.make_async_copy(own_ref, new_hbm.at[0, species], sems.at[0]),
        pltpu.make_async_copy(got_ref, new_hbm.at[0, 1 - species], sems.at[1]),
        pltpu.make_async_copy(norm_ref, norm_hbm, sems.at[2]),
    )
    copies[0].start()
    copies[1].start()
    norm_ref[0, 0] = jnp.sqrt(jnp.sum(squares_ref[...]) / entry_count)
    copies[2].start()
    for copy in copies:
        copy.wait()


def exchange(value, axis, bits):
    pairs = [(index, index ^ bits) for index in range(lax.axis_size(axis))]
    return lax.ppermute(value, axis, pairs)


def shards(
    forcing,
    initial_state,
    previous,
    zone_diffusion,
    drift_rate,
    column_zone,
    bottom_flag,
    open_faces,
):
    length = lax.axis_size("tm")
    space = lax.axis_size("space")
    cells, lanes = open_faces.shape
    whole = pl.BlockSpec(memory_space=pltpu.VMEM)
    outside = pl.BlockSpec(memory_space=pltpu.HBM)
    count = planes(length)
    params = pltpu.CompilerParams(vmem_limit_bytes=40 * 1024 * 1024)
    alone = pltpu.CompilerParams(vmem_limit_bytes=56 * 1024 * 1024)
    mine, other = pl.pallas_call(
        stack_kernel,
        out_shape=(
            pltpu.VMEM((2, cells, lanes), jnp.float32),
            pltpu.VMEM((2, cells, lanes), jnp.float32),
        ),
        in_specs=[outside] * 2,
        out_specs=[whole] * 2,
        scratch_shapes=[pltpu.SemaphoreType.DMA((4,))],
        compiler_params=alone,
        cost_estimate=pl.CostEstimate(flops=4000, bytes_accessed=500000, transcendentals=0),
        name="stack_arrays",
    )(forcing, previous)
    stacks = [mine]
    for bits in range(1, length):
        stacks.append(exchange(other if bits % 2 else mine, "tm", bits))
    near, far, initial = pl.pallas_call(
        functools.partial(factor_kernel, length),
        out_shape=(
            pltpu.VMEM((count, 2 * near_steps, cells, lanes), jnp.float32),
            pltpu.VMEM((count, 3, cells, lanes), jnp.float32),
            pltpu.VMEM((cells, lanes), jnp.float32),
        ),
        in_specs=[outside] * 6,
        out_specs=[whole] * 3,
        scratch_shapes=[
            pltpu.SMEM(zone_diffusion.shape, jnp.float32),
            pltpu.SMEM(drift_rate.shape, jnp.float32),
            pltpu.VMEM((1, lanes), jnp.int32),
            pltpu.VMEM((1, lanes), jnp.int32),
            pltpu.VMEM((cells, lanes), jnp.int32),
            pltpu.SemaphoreType.DMA((6,)),
        ],
        compiler_params=alone,
        cost_estimate=pl.CostEstimate(flops=4000000, bytes_accessed=3000000, transcendentals=0),
        name="factor_lines",
    )(initial_state, zone_diffusion, drift_rate, column_zone[None], bottom_flag[None], open_faces)
    own, give, squares = pl.pallas_call(
        functools.partial(sweep_kernel, length),
        out_shape=(
            pltpu.VMEM((cells, lanes), jnp.float32),
            pltpu.VMEM((cells, lanes), jnp.float32),
            pltpu.VMEM((1, lanes), jnp.float32),
        ),
        in_specs=[whole] * (length + 3),
        out_specs=[whole] * 3,
        compiler_params=params,
        cost_estimate=pl.CostEstimate(flops=4000000, bytes_accessed=3000000, transcendentals=0),
        name="solve_lines",
    )(*stacks, initial, near, far)
    last = 2 * space - 1
    squares = squares + exchange(squares, "space", 1)
    got = exchange(give, "tm", 1)
    groups = [
        [step * space + index for index in reversed(range(core, 2 * space, 2))]
        for step in range(0, length, 2)
        for core in range(2)
    ]
    squares = lax.all_to_all(
        jnp.broadcast_to(squares[None], (space,) + squares.shape),
        ("tm", "space"),
        0,
        0,
        axis_index_groups=groups,
        tiled=True,
    )
    entry_count = length * space * forcing.shape[1] * cells * lanes
    new_iterate, norm = pl.pallas_call(
        functools.partial(join_kernel, entry_count),
        out_shape=(
            jax.ShapeDtypeStruct(forcing.shape, jnp.float32),
            jax.ShapeDtypeStruct((1, 1), jnp.float32),
        ),
        in_specs=[whole] * 3,
        out_specs=(outside, outside),
        scratch_shapes=[pltpu.SMEM((1, 1), jnp.float32), pltpu.SemaphoreType.DMA((3,))],
        compiler_params=params,
        cost_estimate=pl.CostEstimate(flops=4000, bytes_accessed=100000, transcendentals=0),
        name="join_species",
    )(own, got, squares)
    return (new_iterate, norm[0, 0])


def solution(mesh):
    placed = (
        P("tm", None, None, "space"),
        P(None, None, "space"),
        P("tm", None, None, "space"),
        P(),
        P(),
        P("space"),
        P("space"),
        P(None, "space"),
    )
    return jax.shard_map(
        shards,
        mesh=mesh,
        in_specs=placed,
        out_specs=(P("tm", None, None, "space"), P()),
        check_vma=False,
    )
```

```python
import functools
import math

import jax
import jax.numpy as jnp
from jax import lax
from jax.experimental import pallas as pl
from jax.experimental.pallas import tpu as pltpu
from jax.sharding import PartitionSpec as P

alpha_corner = 0.3
tile = 8
near_steps = 3


def roll_down(block, distance):
    return pltpu.roll(block, distance, 0)


def roll_up(block, distance):
    return pltpu.roll(block, block.shape[0] - distance, 0)


def c_mul(x, y):
    if len(x) == 1 and len(y) == 1:
        return (x[0] * y[0],)
    if len(x) == 1:
        return (x[0] * y[0], x[0] * y[1])
    if len(y) == 1:
        return (x[0] * y[0], x[1] * y[0])
    return (x[0] * y[0] - x[1] * y[1], x[0] * y[1] + x[1] * y[0])


def c_add(x, y):
    return tuple(p + q for p, q in zip(x, y))


def c_sub(x, y):
    return tuple(p - q for p, q in zip(x, y))


def c_neg(x):
    return tuple(-p for p in x)


def c_inverse(x):
    if len(x) == 1:
        return (1.0 / x[0],)
    scale = 1.0 / (x[0] * x[0] + x[1] * x[1])
    return (x[0] * scale, -x[1] * scale)


def c_map(f, x):
    return tuple(f(p) for p in x)


def frequencies(length):
    root = math.exp(math.log(alpha_corner) / length)
    listed = []
    for j in range(length // 2 + 1):
        angle = 2.0 * math.pi * j / length
        if j == 0 or 2 * j == length:
            listed.append((j, (1.0 - root * math.cos(angle),)))
        else:
            listed.append((j, (1.0 - root * math.cos(angle), root * math.sin(angle))))
    return listed


def planes(length):
    return sum(len(shift) for unused, shift in frequencies(length))


def turn(j, n, length):
    count = j * n % length
    if 4 * count % length == 0:
        return ((1.0, 0.0), (0.0, 1.0), (-1.0, 0.0), (0.0, -1.0))[4 * count // length]
    angle = 2.0 * math.pi * count / length
    return (math.cos(angle), math.sin(angle))


def weighted(total, weight, value):
    if weight == 0.0:
        return total
    if weight == 1.0:
        term = value
    elif weight == -1.0:
        return -value if total is None else total - value
    else:
        term = weight * value
    return term if total is None else total + term


def start_all(pairs, sems):
    copies = [
        pltpu.make_async_copy(source, target, sems.at[index])
        for index, (source, target) in enumerate(pairs)
    ]
    for copy in copies:
        copy.start()
    return copies


def stack_kernel(forcing_hbm, previous_hbm, mine_ref, other_ref, sems):
    species = lax.axis_index("tm") % 2
    pairs = (
        (forcing_hbm.at[0, species], mine_ref.at[0]),
        (previous_hbm.at[0, species], mine_ref.at[1]),
        (forcing_hbm.at[0, 1 - species], other_ref.at[0]),
        (previous_hbm.at[0, 1 - species], other_ref.at[1]),
    )
    for copy in start_all(pairs, sems):
        copy.wait()


def factor_kernel(
    length,
    initial_hbm,
    zones_hbm,
    drift_hbm,
    zone_hbm,
    flag_hbm,
    faces_hbm,
    near_ref,
    far_ref,
    initial_ref,
    zones_ref,
    drift_ref,
    zone_ref,
    flag_ref,
    faces_ref,
    sems,
):
    species = lax.axis_index("tm") % 2
    pairs = (
        (zones_hbm, zones_ref),
        (drift_hbm, drift_ref),
        (zone_hbm, zone_ref),
        (flag_hbm, flag_ref),
        (faces_hbm, faces_ref),
        (initial_hbm.at[species], initial_ref),
    )
    for copy in start_all(pairs, sems):
        copy.wait()
    zone = zone_ref[...]
    diffusion = jnp.zeros(zone.shape, jnp.float32)
    for index in range(zones_ref.shape[1]):
        diffusion = jnp.where(zone == index, zones_ref[species, index], diffusion)
    drift = drift_ref[species]
    cells, lanes = faces_ref.shape
    faces = faces_ref[...].astype(jnp.float32)
    row = lax.broadcasted_iota(jnp.int32, (cells, lanes), 0)
    link_above = jnp.where(row == cells - 1, 0.0, faces)
    link_below = jnp.where(row == 0, 0.0, roll_down(faces, 1))
    ground = jnp.where(row == 0, flag_ref[...].astype(jnp.float32), 0.0)
    below = -(diffusion + drift) * link_below
    above = -diffusion * link_above
    centre = diffusion * (link_below + link_above) + drift + 2.0 * diffusion * ground
    plane = 0
    for unused, shift in frequencies(length):
        parts = len(shift)
        a = (below,)
        c = (above,)
        b = (centre + shift[0],)
        if parts == 2:
            b = b + (jnp.full_like(centre, shift[1]),)
        for step in range(near_steps):
            distance = 1 << step
            inverse = c_inverse(b)
            low = c_neg(c_mul(a, c_map(lambda p: roll_down(p, distance), inverse)))
            high = c_neg(c_mul(c, c_map(lambda p: roll_up(p, distance), inverse)))
            down_c = c_map(lambda p: roll_down(p, distance), c)
            up_a = c_map(lambda p: roll_up(p, distance), a)
            b = c_add(b, c_add(c_mul(low, down_c), c_mul(high, up_a)))
            a = c_mul(low, c_map(lambda p: roll_down(p, distance), a))
            c = c_mul(high, c_map(lambda p: roll_up(p, distance), c))
            for part in range(parts):
                near_ref[plane + part, 2 * step] = low[part]
                near_ref[plane + part, 2 * step + 1] = high[part]
        carry = None
        for block in range(cells // tile):
            rows = slice(block * tile, (block + 1) * tile)
            ak, bk, ck = (c_map(lambda p: p[rows], item) for item in (a, b, c))
            if carry is None:
                eliminate = c_map(jnp.zeros_like, ak)
            else:
                eliminate = c_mul(ak, carry[0])
                bk = c_sub(bk, c_mul(eliminate, carry[1]))
            inverse = c_inverse(bk)
            substitute = c_mul(ck, inverse)
            for part in range(parts):
                far_ref[plane + part, 0, rows] = eliminate[part]
                far_ref[plane + part, 1, rows] = inverse[part]
                far_ref[plane + part, 2, rows] = substitute[part]
            carry = (inverse, ck)
        plane += parts


def in_order(me, held):
    bit = 1
    while bit < len(held):
        swap = (me & bit) != 0
        held = [
            jnp.where(swap, held[index ^ bit], held[index]) for index in range(len(held))
        ]
        bit *= 2
    return held


def sweep_kernel(length, *refs):
    stacks = refs[:length]
    initial_ref, near_ref, far_ref, own_ref, give_ref, sum_ref = refs[length:]
    cells, lanes = initial_ref.shape
    log_alpha = math.log(alpha_corner)
    me = lax.axis_index("tm")
    loads = in_order(me, [ref[0] for ref in stacks])
    befores = in_order(me, [ref[1] for ref in stacks])
    loads[0] = loads[0] + (initial_ref[...] - alpha_corner * befores[length - 1])
    scaled = [math.exp(log_alpha * n / length) * load for n, load in enumerate(loads)]
    spectrum = []
    plane = 0
    for j, shift in frequencies(length):
        parts = len(shift)
        rhs = [None] * parts
        for n in range(length):
            weights = turn(j, -n, length)
            for part in range(parts):
                rhs[part] = weighted(rhs[part], weights[part], scaled[n])
        rhs = tuple(rhs)
        for step in range(near_steps):
            distance = 1 << step
            low = tuple(near_ref[plane + p, 2 * step] for p in range(parts))
            high = tuple(near_ref[plane + p, 2 * step + 1] for p in range(parts))
            down = c_map(lambda p: roll_down(p, distance), rhs)
            up = c_map(lambda p: roll_up(p, distance), rhs)
            rhs = c_add(rhs, c_add(c_mul(low, down), c_mul(high, up)))
        blocks = []
        carry = None
        for block in range(cells // tile):
            rows = slice(block * tile, (block + 1) * tile)
            value = c_map(lambda p: p[rows], rhs)
            if carry is not None:
                eliminate = tuple(far_ref[plane + p, 0, rows] for p in range(parts))
                value = c_sub(value, c_mul(eliminate, carry))
            blocks.append(value)
            carry = value
        solved = [None] * len(blocks)
        carry = None
        for block in reversed(range(cells // tile)):
            rows = slice(block * tile, (block + 1) * tile)
            inverse = tuple(far_ref[plane + p, 1, rows] for p in range(parts))
            value = c_mul(inverse, blocks[block])
            if carry is not None:
                substitute = tuple(far_ref[plane + p, 2, rows] for p in range(parts))
                value = c_sub(value, c_mul(substitute, carry))
            solved[block] = value
            carry = value
        spectrum.append((j, parts, solved))
        plane += parts
    total = jnp.zeros((tile, lanes), jnp.float32)
    for block in range(cells // tile):
        rows = slice(block * tile, (block + 1) * tile)
        steps = []
        for n in range(length):
            fresh = None
            for j, parts, solved in spectrum:
                weights = turn(j, n, length)
                fresh = weighted(fresh, parts * weights[0], solved[block][0])
                if parts == 2:
                    fresh = weighted(fresh, -parts * weights[1], solved[block][1])
            fresh = fresh * (math.exp(-log_alpha * n / length) / length)
            steps.append(fresh)
            change = fresh - befores[n][rows]
            total = total + change * change
        own = steps[0]
        give = steps[1]
        for n in range(1, length):
            own = jnp.where(me == n, steps[n], own)
            give = jnp.where(me == n, steps[n ^ 1], give)
        own_ref[rows] = own
        give_ref[rows] = give
    sum_ref[...] = jnp.broadcast_to(jnp.sum(total, axis=0, keepdims=True), sum_ref.shape)


def join_kernel(
    entry_count, own_ref, got_ref, squares_ref, new_hbm, norm_hbm, norm_ref, sems
):
    species = lax.axis_index("tm") % 2
    copies = (
        pltpu.make_async_copy(own_ref, new_hbm.at[0, species], sems.at[0]),
        pltpu.make_async_copy(got_ref, new_hbm.at[0, 1 - species], sems.at[1]),
        pltpu.make_async_copy(norm_ref, norm_hbm, sems.at[2]),
    )
    copies[0].start()
    copies[1].start()
    norm_ref[0, 0] = jnp.sqrt(jnp.sum(squares_ref[...]) / entry_count)
    copies[2].start()
    for copy in copies:
        copy.wait()


def exchange(value, axis, bits):
    pairs = [(index, index ^ bits) for index in range(lax.axis_size(axis))]
    return lax.ppermute(value, axis, pairs)


def shards(
    forcing,
    initial_state,
    previous,
    zone_diffusion,
    drift_rate,
    column_zone,
    bottom_flag,
    open_faces,
):
    length = lax.axis_size("tm")
    space = lax.axis_size("space")
    cells, lanes = open_faces.shape
    whole = pl.BlockSpec(memory_space=pltpu.VMEM)
    outside = pl.BlockSpec(memory_space=pltpu.HBM)
    count = planes(length)
    params = pltpu.CompilerParams(vmem_limit_bytes=40 * 1024 * 1024)
    alone = pltpu.CompilerParams(vmem_limit_bytes=56 * 1024 * 1024)
    mine, other = pl.pallas_call(
        stack_kernel,
        out_shape=(
            pltpu.VMEM((2, cells, lanes), jnp.float32),
            pltpu.VMEM((2, cells, lanes), jnp.float32),
        ),
        in_specs=[outside] * 2,
        out_specs=[whole] * 2,
        scratch_shapes=[pltpu.SemaphoreType.DMA((4,))],
        compiler_params=alone,
        cost_estimate=pl.CostEstimate(flops=4000, bytes_accessed=500000, transcendentals=0),
        name="stack_arrays",
    )(forcing, previous)
    stacks = [mine]
    for bits in range(1, length):
        stacks.append(exchange(other if bits % 2 else mine, "tm", bits))
    near, far, initial = pl.pallas_call(
        functools.partial(factor_kernel, length),
        out_shape=(
            pltpu.VMEM((count, 2 * near_steps, cells, lanes), jnp.float32),
            pltpu.VMEM((count, 3, cells, lanes), jnp.float32),
            pltpu.VMEM((cells, lanes), jnp.float32),
        ),
        in_specs=[outside] * 6,
        out_specs=[whole] * 3,
        scratch_shapes=[
            pltpu.SMEM(zone_diffusion.shape, jnp.float32),
            pltpu.SMEM(drift_rate.shape, jnp.float32),
            pltpu.VMEM((1, lanes), jnp.int32),
            pltpu.VMEM((1, lanes), jnp.int32),
            pltpu.VMEM((cells, lanes), jnp.int32),
            pltpu.SemaphoreType.DMA((6,)),
        ],
        compiler_params=alone,
        cost_estimate=pl.CostEstimate(flops=4000000, bytes_accessed=3000000, transcendentals=0),
        name="factor_lines",
    )(initial_state, zone_diffusion, drift_rate, column_zone[None], bottom_flag[None], open_faces)
    own, give, squares = pl.pallas_call(
        functools.partial(sweep_kernel, length),
        out_shape=(
            pltpu.VMEM((cells, lanes), jnp.float32),
            pltpu.VMEM((cells, lanes), jnp.float32),
            pltpu.VMEM((1, lanes), jnp.float32),
        ),
        in_specs=[whole] * (length + 3),
        out_specs=[whole] * 3,
        compiler_params=params,
        cost_estimate=pl.CostEstimate(flops=4000000, bytes_accessed=3000000, transcendentals=0),
        name="solve_lines",
    )(*stacks, initial, near, far)
    last = 2 * space - 1
    squares = squares + exchange(squares, "space", 1)
    got = exchange(give, "tm", 1)
    groups = [
        [step * space + index for index in (*reversed(range(3 - core, 2 * space, 2)), core)]
        for step in range(0, length, 2)
        for core in range(2)
    ]
    squares = lax.all_to_all(
        jnp.broadcast_to(squares[None], (space,) + squares.shape),
        ("tm", "space"),
        0,
        0,
        axis_index_groups=groups,
        tiled=True,
    )
    entry_count = length * space * forcing.shape[1] * cells * lanes
    new_iterate, norm = pl.pallas_call(
        functools.partial(join_kernel, entry_count),
        out_shape=(
            jax.ShapeDtypeStruct(forcing.shape, jnp.float32),
            jax.ShapeDtypeStruct((1, 1), jnp.float32),
        ),
        in_specs=[whole] * 3,
        out_specs=(outside, outside),
        scratch_shapes=[pltpu.SMEM((1, 1), jnp.float32), pltpu.SemaphoreType.DMA((3,))],
        compiler_params=params,
        cost_estimate=pl.CostEstimate(flops=4000, bytes_accessed=100000, transcendentals=0),
        name="join_species",
    )(own, got, squares)
    return (new_iterate, norm[0, 0])


def solution(mesh):
    placed = (
        P("tm", None, None, "space"),
        P(None, None, "space"),
        P("tm", None, None, "space"),
        P(),
        P(),
        P("space"),
        P("space"),
        P(None, "space"),
    )
    return jax.shard_map(
        shards,
        mesh=mesh,
        in_specs=placed,
        out_specs=(P("tm", None, None, "space"), P()),
        check_vma=False,
    )
```

```python
import functools
import math

import jax
import jax.numpy as jnp
from jax import lax
from jax.experimental import pallas as pl
from jax.experimental.pallas import tpu as pltpu
from jax.sharding import PartitionSpec as P

alpha_corner = 0.3
tile = 8
near_steps = 3


def roll_down(block, distance):
    return pltpu.roll(block, distance, 0)


def roll_up(block, distance):
    return pltpu.roll(block, block.shape[0] - distance, 0)


def c_mul(x, y):
    if len(x) == 1 and len(y) == 1:
        return (x[0] * y[0],)
    if len(x) == 1:
        return (x[0] * y[0], x[0] * y[1])
    if len(y) == 1:
        return (x[0] * y[0], x[1] * y[0])
    return (x[0] * y[0] - x[1] * y[1], x[0] * y[1] + x[1] * y[0])


def c_add(x, y):
    return tuple(p + q for p, q in zip(x, y))


def c_sub(x, y):
    return tuple(p - q for p, q in zip(x, y))


def c_neg(x):
    return tuple(-p for p in x)


def c_inverse(x):
    if len(x) == 1:
        return (1.0 / x[0],)
    scale = 1.0 / (x[0] * x[0] + x[1] * x[1])
    return (x[0] * scale, -x[1] * scale)


def c_map(f, x):
    return tuple(f(p) for p in x)


def frequencies(length):
    root = math.exp(math.log(alpha_corner) / length)
    listed = []
    for j in range(length // 2 + 1):
        angle = 2.0 * math.pi * j / length
        if j == 0 or 2 * j == length:
            listed.append((j, (1.0 - root * math.cos(angle),)))
        else:
            listed.append((j, (1.0 - root * math.cos(angle), root * math.sin(angle))))
    return listed


def planes(length):
    return sum(len(shift) for unused, shift in frequencies(length))


def turn(j, n, length):
    count = j * n % length
    if 4 * count % length == 0:
        return ((1.0, 0.0), (0.0, 1.0), (-1.0, 0.0), (0.0, -1.0))[4 * count // length]
    angle = 2.0 * math.pi * count / length
    return (math.cos(angle), math.sin(angle))


def weighted(total, weight, value):
    if weight == 0.0:
        return total
    if weight == 1.0:
        term = value
    elif weight == -1.0:
        return -value if total is None else total - value
    else:
        term = weight * value
    return term if total is None else total + term


def start_all(pairs, sems):
    copies = [
        pltpu.make_async_copy(source, target, sems.at[index])
        for index, (source, target) in enumerate(pairs)
    ]
    for copy in copies:
        copy.start()
    return copies


def stack_kernel(
    length,
    forcing_hbm,
    previous_hbm,
    zones_hbm,
    drift_hbm,
    zone_hbm,
    flag_hbm,
    faces_hbm,
    mine_ref,
    other_ref,
    near_ref,
    far_ref,
    zones_ref,
    drift_ref,
    zone_ref,
    flag_ref,
    faces_ref,
    sems,
):
    species = lax.axis_index("tm") % 2
    pairs = (
        (forcing_hbm.at[0, species], mine_ref.at[0]),
        (previous_hbm.at[0, species], mine_ref.at[1]),
        (forcing_hbm.at[0, 1 - species], other_ref.at[0]),
        (previous_hbm.at[0, 1 - species], other_ref.at[1]),
        (zones_hbm, zones_ref),
        (drift_hbm, drift_ref),
        (zone_hbm, zone_ref),
        (flag_hbm, flag_ref),
        (faces_hbm, faces_ref),
    )
    for copy in start_all(pairs, sems):
        copy.wait()

    @pl.when(lax.axis_index("space") % 2 == 1)
    def factor():
        factor_lines(
            length, zones_ref, drift_ref, zone_ref, flag_ref, faces_ref, near_ref, far_ref
        )


def factor_lines(
    length, zones_ref, drift_ref, zone_ref, flag_ref, faces_ref, near_ref, far_ref
):
    species = lax.axis_index("tm") % 2
    zone = zone_ref[...]
    diffusion = jnp.zeros(zone.shape, jnp.float32)
    for index in range(zones_ref.shape[1]):
        diffusion = jnp.where(zone == index, zones_ref[species, index], diffusion)
    drift = drift_ref[species]
    cells, lanes = faces_ref.shape
    faces = faces_ref[...].astype(jnp.float32)
    row = lax.broadcasted_iota(jnp.int32, (cells, lanes), 0)
    link_above = jnp.where(row == cells - 1, 0.0, faces)
    link_below = jnp.where(row == 0, 0.0, roll_down(faces, 1))
    ground = jnp.where(row == 0, flag_ref[...].astype(jnp.float32), 0.0)
    below = -(diffusion + drift) * link_below
    above = -diffusion * link_above
    centre = diffusion * (link_below + link_above) + drift + 2.0 * diffusion * ground
    plane = 0
    for unused, shift in frequencies(length):
        parts = len(shift)
        a = (below,)
        c = (above,)
        b = (centre + shift[0],)
        if parts == 2:
            b = b + (jnp.full_like(centre, shift[1]),)
        for step in range(near_steps):
            distance = 1 << step
            inverse = c_inverse(b)
            low = c_neg(c_mul(a, c_map(lambda p: roll_down(p, distance), inverse)))
            high = c_neg(c_mul(c, c_map(lambda p: roll_up(p, distance), inverse)))
            down_c = c_map(lambda p: roll_down(p, distance), c)
            up_a = c_map(lambda p: roll_up(p, distance), a)
            b = c_add(b, c_add(c_mul(low, down_c), c_mul(high, up_a)))
            a = c_mul(low, c_map(lambda p: roll_down(p, distance), a))
            c = c_mul(high, c_map(lambda p: roll_up(p, distance), c))
            for part in range(parts):
                near_ref[plane + part, 2 * step] = low[part]
                near_ref[plane + part, 2 * step + 1] = high[part]
        carry = None
        for block in range(cells // tile):
            rows = slice(block * tile, (block + 1) * tile)
            ak, bk, ck = (c_map(lambda p: p[rows], item) for item in (a, b, c))
            if carry is None:
                eliminate = c_map(jnp.zeros_like, ak)
            else:
                eliminate = c_mul(ak, carry[0])
                bk = c_sub(bk, c_mul(eliminate, carry[1]))
            inverse = c_inverse(bk)
            substitute = c_mul(ck, inverse)
            for part in range(parts):
                far_ref[plane + part, 0, rows] = eliminate[part]
                far_ref[plane + part, 1, rows] = inverse[part]
                far_ref[plane + part, 2, rows] = substitute[part]
            carry = (inverse, ck)
        plane += parts


def factor_kernel(
    length,
    initial_hbm,
    zones_hbm,
    drift_hbm,
    zone_hbm,
    flag_hbm,
    faces_hbm,
    near_ref,
    far_ref,
    initial_ref,
    zones_ref,
    drift_ref,
    zone_ref,
    flag_ref,
    faces_ref,
    sems,
):
    pairs = (
        (zones_hbm, zones_ref),
        (drift_hbm, drift_ref),
        (zone_hbm, zone_ref),
        (flag_hbm, flag_ref),
        (faces_hbm, faces_ref),
        (initial_hbm.at[lax.axis_index("tm") % 2], initial_ref),
    )
    for copy in start_all(pairs, sems):
        copy.wait()

    @pl.when(lax.axis_index("space") % 2 == 0)
    def factor():
        factor_lines(
            length, zones_ref, drift_ref, zone_ref, flag_ref, faces_ref, near_ref, far_ref
        )


def in_order(me, held):
    bit = 1
    while bit < len(held):
        swap = (me & bit) != 0
        held = [
            jnp.where(swap, held[index ^ bit], held[index]) for index in range(len(held))
        ]
        bit *= 2
    return held


def sweep_kernel(length, *refs):
    *shared, near_even, far_even, near_odd, far_odd, own_ref, give_ref, sum_ref = refs
    odd = lax.axis_index("space") % 2 == 1

    @pl.when(odd)
    def solve_odd():
        sweep_lines(length, *shared, near_odd, far_odd, own_ref, give_ref, sum_ref)

    @pl.when(jnp.logical_not(odd))
    def solve_even():
        sweep_lines(length, *shared, near_even, far_even, own_ref, give_ref, sum_ref)


def sweep_lines(length, *refs):
    stacks = refs[:length]
    initial_ref, near_ref, far_ref, own_ref, give_ref, sum_ref = refs[length:]
    cells, lanes = initial_ref.shape
    log_alpha = math.log(alpha_corner)
    me = lax.axis_index("tm")
    loads = in_order(me, [ref[0] for ref in stacks])
    befores = in_order(me, [ref[1] for ref in stacks])
    loads[0] = loads[0] + (initial_ref[...] - alpha_corner * befores[length - 1])
    scaled = [math.exp(log_alpha * n / length) * load for n, load in enumerate(loads)]
    spectrum = []
    plane = 0
    for j, shift in frequencies(length):
        parts = len(shift)
        rhs = [None] * parts
        for n in range(length):
            weights = turn(j, -n, length)
            for part in range(parts):
                rhs[part] = weighted(rhs[part], weights[part], scaled[n])
        rhs = tuple(rhs)
        for step in range(near_steps):
            distance = 1 << step
            low = tuple(near_ref[plane + p, 2 * step] for p in range(parts))
            high = tuple(near_ref[plane + p, 2 * step + 1] for p in range(parts))
            down = c_map(lambda p: roll_down(p, distance), rhs)
            up = c_map(lambda p: roll_up(p, distance), rhs)
            rhs = c_add(rhs, c_add(c_mul(low, down), c_mul(high, up)))
        blocks = []
        carry = None
        for block in range(cells // tile):
            rows = slice(block * tile, (block + 1) * tile)
            value = c_map(lambda p: p[rows], rhs)
            if carry is not None:
                eliminate = tuple(far_ref[plane + p, 0, rows] for p in range(parts))
                value = c_sub(value, c_mul(eliminate, carry))
            blocks.append(value)
            carry = value
        solved = [None] * len(blocks)
        carry = None
        for block in reversed(range(cells // tile)):
            rows = slice(block * tile, (block + 1) * tile)
            inverse = tuple(far_ref[plane + p, 1, rows] for p in range(parts))
            value = c_mul(inverse, blocks[block])
            if carry is not None:
                substitute = tuple(far_ref[plane + p, 2, rows] for p in range(parts))
                value = c_sub(value, c_mul(substitute, carry))
            solved[block] = value
            carry = value
        spectrum.append((j, parts, solved))
        plane += parts
    total = jnp.zeros((tile, lanes), jnp.float32)
    for block in range(cells // tile):
        rows = slice(block * tile, (block + 1) * tile)
        steps = []
        for n in range(length):
            fresh = None
            for j, parts, solved in spectrum:
                weights = turn(j, n, length)
                fresh = weighted(fresh, parts * weights[0], solved[block][0])
                if parts == 2:
                    fresh = weighted(fresh, -parts * weights[1], solved[block][1])
            fresh = fresh * (math.exp(-log_alpha * n / length) / length)
            steps.append(fresh)
            change = fresh - befores[n][rows]
            total = total + change * change
        own = steps[0]
        give = steps[1]
        for n in range(1, length):
            own = jnp.where(me == n, steps[n], own)
            give = jnp.where(me == n, steps[n ^ 1], give)
        own_ref[rows] = own
        give_ref[rows] = give
    sum_ref[...] = jnp.broadcast_to(jnp.sum(total, axis=0, keepdims=True), sum_ref.shape)


def join_kernel(
    entry_count, own_ref, got_ref, squares_ref, new_hbm, norm_hbm, norm_ref, sems
):
    species = lax.axis_index("tm") % 2
    copies = (
        pltpu.make_async_copy(own_ref, new_hbm.at[0, species], sems.at[0]),
        pltpu.make_async_copy(got_ref, new_hbm.at[0, 1 - species], sems.at[1]),
        pltpu.make_async_copy(norm_ref, norm_hbm, sems.at[2]),
    )
    copies[0].start()
    copies[1].start()
    norm_ref[0, 0] = jnp.sqrt(jnp.sum(squares_ref[...]) / entry_count)
    copies[2].start()
    for copy in copies:
        copy.wait()


def exchange(value, axis, bits):
    pairs = [(index, index ^ bits) for index in range(lax.axis_size(axis))]
    return lax.ppermute(value, axis, pairs)


def shards(
    forcing,
    initial_state,
    previous,
    zone_diffusion,
    drift_rate,
    column_zone,
    bottom_flag,
    open_faces,
):
    length = lax.axis_size("tm")
    space = lax.axis_size("space")
    cells, lanes = open_faces.shape
    whole = pl.BlockSpec(memory_space=pltpu.VMEM)
    outside = pl.BlockSpec(memory_space=pltpu.HBM)
    count = planes(length)
    params = pltpu.CompilerParams(vmem_limit_bytes=40 * 1024 * 1024)
    alone = pltpu.CompilerParams(vmem_limit_bytes=56 * 1024 * 1024)
    near_shape = (count, 2 * near_steps, cells, lanes)
    far_shape = (count, 3, cells, lanes)
    operator_scratch = [
        pltpu.SMEM(zone_diffusion.shape, jnp.float32),
        pltpu.SMEM(drift_rate.shape, jnp.float32),
        pltpu.VMEM((1, lanes), jnp.int32),
        pltpu.VMEM((1, lanes), jnp.int32),
        pltpu.VMEM((cells, lanes), jnp.int32),
    ]
    operator = (zone_diffusion, drift_rate, column_zone[None], bottom_flag[None], open_faces)
    mine, other, near_odd, far_odd = pl.pallas_call(
        functools.partial(stack_kernel, length),
        out_shape=(
            pltpu.VMEM((2, cells, lanes), jnp.float32),
            pltpu.VMEM((2, cells, lanes), jnp.float32),
            pltpu.VMEM(near_shape, jnp.float32),
            pltpu.VMEM(far_shape, jnp.float32),
        ),
        in_specs=[outside] * 7,
        out_specs=[whole] * 4,
        scratch_shapes=[*operator_scratch, pltpu.SemaphoreType.DMA((9,))],
        compiler_params=alone,
        cost_estimate=pl.CostEstimate(flops=4000, bytes_accessed=500000, transcendentals=0),
        name="stack_arrays",
    )(forcing, previous, *operator)
    stacks = [mine]
    for bits in range(1, length):
        stacks.append(exchange(other if bits % 2 else mine, "tm", bits))
    near, far, initial = pl.pallas_call(
        functools.partial(factor_kernel, length),
        out_shape=(
            pltpu.VMEM((count, 2 * near_steps, cells, lanes), jnp.float32),
            pltpu.VMEM((count, 3, cells, lanes), jnp.float32),
            pltpu.VMEM((cells, lanes), jnp.float32),
        ),
        in_specs=[outside] * 6,
        out_specs=[whole] * 3,
        scratch_shapes=[*operator_scratch, pltpu.SemaphoreType.DMA((6,))],
        compiler_params=alone,
        cost_estimate=pl.CostEstimate(flops=4000000, bytes_accessed=3000000, transcendentals=0),
        name="factor_lines",
    )(initial_state, *operator)
    own, give, squares = pl.pallas_call(
        functools.partial(sweep_kernel, length),
        out_shape=(
            pltpu.VMEM((cells, lanes), jnp.float32),
            pltpu.VMEM((cells, lanes), jnp.float32),
            pltpu.VMEM((2 * space, 1, lanes), jnp.float32),
        ),
        in_specs=[whole] * (length + 5),
        out_specs=[whole] * 3,
        compiler_params=params,
        cost_estimate=pl.CostEstimate(flops=4000000, bytes_accessed=3000000, transcendentals=0),
        name="solve_lines",
    )(*stacks, initial, near, far, near_odd, far_odd)
    got = exchange(give, "tm", 1)
    last = 2 * space - 1
    order = [last, *range(2, last, 2), *range(3, last, 2), 1, 0]
    groups = [[step * space + index for index in order] for step in range(0, length, 2)]
    squares = lax.all_to_all(
        squares, ("tm", "space"), 0, 0, axis_index_groups=groups, tiled=True
    )
    entry_count = length * space * forcing.shape[1] * cells * lanes
    new_iterate, norm = pl.pallas_call(
        functools.partial(join_kernel, entry_count),
        out_shape=(
            jax.ShapeDtypeStruct(forcing.shape, jnp.float32),
            jax.ShapeDtypeStruct((1, 1), jnp.float32),
        ),
        in_specs=[whole] * 3,
        out_specs=(outside, outside),
        scratch_shapes=[pltpu.SMEM((1, 1), jnp.float32), pltpu.SemaphoreType.DMA((3,))],
        compiler_params=params,
        cost_estimate=pl.CostEstimate(flops=4000, bytes_accessed=100000, transcendentals=0),
        name="join_species",
    )(own, got, squares)
    return (new_iterate, norm[0, 0])


def solution(mesh):
    placed = (
        P("tm", None, None, "space"),
        P(None, None, "space"),
        P("tm", None, None, "space"),
        P(),
        P(),
        P("space"),
        P("space"),
        P(None, "space"),
    )
    return jax.shard_map(
        shards,
        mesh=mesh,
        in_specs=placed,
        out_specs=(P("tm", None, None, "space"), P()),
        check_vma=False,
    )
```

```python
import functools
import math

import jax
import jax.numpy as jnp
from jax import lax
from jax.experimental import pallas as pl
from jax.experimental.pallas import tpu as pltpu
from jax.sharding import PartitionSpec as P

alpha_corner = 0.3
tile = 8
near_steps = 3


def roll_down(block, distance):
    return pltpu.roll(block, distance, 0)


def roll_up(block, distance):
    return pltpu.roll(block, block.shape[0] - distance, 0)


def c_mul(x, y):
    if len(x) == 1 and len(y) == 1:
        return (x[0] * y[0],)
    if len(x) == 1:
        return (x[0] * y[0], x[0] * y[1])
    if len(y) == 1:
        return (x[0] * y[0], x[1] * y[0])
    return (x[0] * y[0] - x[1] * y[1], x[0] * y[1] + x[1] * y[0])


def c_add(x, y):
    return tuple(p + q for p, q in zip(x, y))


def c_sub(x, y):
    return tuple(p - q for p, q in zip(x, y))


def c_neg(x):
    return tuple(-p for p in x)


def c_inverse(x):
    if len(x) == 1:
        return (1.0 / x[0],)
    scale = 1.0 / (x[0] * x[0] + x[1] * x[1])
    return (x[0] * scale, -x[1] * scale)


def c_map(f, x):
    return tuple(f(p) for p in x)


def frequencies(length):
    root = math.exp(math.log(alpha_corner) / length)
    listed = []
    for j in range(length // 2 + 1):
        angle = 2.0 * math.pi * j / length
        if j == 0 or 2 * j == length:
            listed.append((j, (1.0 - root * math.cos(angle),)))
        else:
            listed.append((j, (1.0 - root * math.cos(angle), root * math.sin(angle))))
    return listed


def planes(length):
    return sum(len(shift) for unused, shift in frequencies(length))


def turn(j, n, length):
    count = j * n % length
    if 4 * count % length == 0:
        return ((1.0, 0.0), (0.0, 1.0), (-1.0, 0.0), (0.0, -1.0))[4 * count // length]
    angle = 2.0 * math.pi * count / length
    return (math.cos(angle), math.sin(angle))


def weighted(total, weight, value):
    if weight == 0.0:
        return total
    if weight == 1.0:
        term = value
    elif weight == -1.0:
        return -value if total is None else total - value
    else:
        term = weight * value
    return term if total is None else total + term


def start_all(pairs, sems):
    copies = [
        pltpu.make_async_copy(source, target, sems.at[index])
        for index, (source, target) in enumerate(pairs)
    ]
    for copy in copies:
        copy.start()
    return copies


def stack_kernel(forcing_hbm, previous_hbm, mine_ref, other_ref, sems):
    species = lax.axis_index("tm") % 2
    half = mine_ref.shape[1] // 2
    pairs = [
        (source.at[0, part, rows], target.at[slot, rows])
        for target, part in ((mine_ref, species), (other_ref, 1 - species))
        for slot, source in enumerate((forcing_hbm, previous_hbm))
        for rows in (pl.ds(0, half), pl.ds(half, half))
    ]
    for copy in start_all(pairs, sems):
        copy.wait()


def factor_kernel(
    length,
    initial_hbm,
    zones_hbm,
    drift_hbm,
    zone_hbm,
    flag_hbm,
    faces_hbm,
    near_ref,
    far_ref,
    initial_ref,
    zones_ref,
    drift_ref,
    zone_ref,
    flag_ref,
    faces_ref,
    sems,
):
    species = lax.axis_index("tm") % 2
    pairs = (
        (zones_hbm, zones_ref),
        (drift_hbm, drift_ref),
        (zone_hbm, zone_ref),
        (flag_hbm, flag_ref),
        (faces_hbm, faces_ref),
        (initial_hbm.at[species], initial_ref),
    )
    for copy in start_all(pairs, sems):
        copy.wait()
    zone = zone_ref[...]
    diffusion = jnp.zeros(zone.shape, jnp.float32)
    for index in range(zones_ref.shape[1]):
        diffusion = jnp.where(zone == index, zones_ref[species, index], diffusion)
    drift = drift_ref[species]
    cells, lanes = faces_ref.shape
    faces = faces_ref[...].astype(jnp.float32)
    row = lax.broadcasted_iota(jnp.int32, (cells, lanes), 0)
    link_above = jnp.where(row == cells - 1, 0.0, faces)
    link_below = jnp.where(row == 0, 0.0, roll_down(faces, 1))
    ground = jnp.where(row == 0, flag_ref[...].astype(jnp.float32), 0.0)
    below = -(diffusion + drift) * link_below
    above = -diffusion * link_above
    centre = diffusion * (link_below + link_above) + drift + 2.0 * diffusion * ground
    plane = 0
    for unused, shift in frequencies(length):
        parts = len(shift)
        a = (below,)
        c = (above,)
        b = (centre + shift[0],)
        if parts == 2:
            b = b + (jnp.full_like(centre, shift[1]),)
        for step in range(near_steps):
            distance = 1 << step
            inverse = c_inverse(b)
            low = c_neg(c_mul(a, c_map(lambda p: roll_down(p, distance), inverse)))
            high = c_neg(c_mul(c, c_map(lambda p: roll_up(p, distance), inverse)))
            down_c = c_map(lambda p: roll_down(p, distance), c)
            up_a = c_map(lambda p: roll_up(p, distance), a)
            b = c_add(b, c_add(c_mul(low, down_c), c_mul(high, up_a)))
            a = c_mul(low, c_map(lambda p: roll_down(p, distance), a))
            c = c_mul(high, c_map(lambda p: roll_up(p, distance), c))
            for part in range(parts):
                near_ref[plane + part, 2 * step] = low[part]
                near_ref[plane + part, 2 * step + 1] = high[part]
        carry = None
        for block in range(cells // tile):
            rows = slice(block * tile, (block + 1) * tile)
            ak, bk, ck = (c_map(lambda p: p[rows], item) for item in (a, b, c))
            if carry is None:
                eliminate = c_map(jnp.zeros_like, ak)
            else:
                eliminate = c_mul(ak, carry[0])
                bk = c_sub(bk, c_mul(eliminate, carry[1]))
            inverse = c_inverse(bk)
            substitute = c_mul(ck, inverse)
            for part in range(parts):
                far_ref[plane + part, 0, rows] = eliminate[part]
                far_ref[plane + part, 1, rows] = inverse[part]
                far_ref[plane + part, 2, rows] = substitute[part]
            carry = (inverse, ck)
        plane += parts


def in_order(me, held):
    bit = 1
    while bit < len(held):
        swap = (me & bit) != 0
        held = [
            jnp.where(swap, held[index ^ bit], held[index]) for index in range(len(held))
        ]
        bit *= 2
    return held


def sweep_kernel(length, *refs):
    stacks = refs[:length]
    initial_ref, near_ref, far_ref, own_ref, give_ref, sum_ref = refs[length:]
    cells, lanes = initial_ref.shape
    log_alpha = math.log(alpha_corner)
    me = lax.axis_index("tm")
    loads = in_order(me, [ref[0] for ref in stacks])
    befores = in_order(me, [ref[1] for ref in stacks])
    loads[0] = loads[0] + (initial_ref[...] - alpha_corner * befores[length - 1])
    scaled = [math.exp(log_alpha * n / length) * load for n, load in enumerate(loads)]
    spectrum = []
    plane = 0
    for j, shift in frequencies(length):
        parts = len(shift)
        rhs = [None] * parts
        for n in range(length):
            weights = turn(j, -n, length)
            for part in range(parts):
                rhs[part] = weighted(rhs[part], weights[part], scaled[n])
        rhs = tuple(rhs)
        for step in range(near_steps):
            distance = 1 << step
            low = tuple(near_ref[plane + p, 2 * step] for p in range(parts))
            high = tuple(near_ref[plane + p, 2 * step + 1] for p in range(parts))
            down = c_map(lambda p: roll_down(p, distance), rhs)
            up = c_map(lambda p: roll_up(p, distance), rhs)
            rhs = c_add(rhs, c_add(c_mul(low, down), c_mul(high, up)))
        blocks = []
        carry = None
        for block in range(cells // tile):
            rows = slice(block * tile, (block + 1) * tile)
            value = c_map(lambda p: p[rows], rhs)
            if carry is not None:
                eliminate = tuple(far_ref[plane + p, 0, rows] for p in range(parts))
                value = c_sub(value, c_mul(eliminate, carry))
            blocks.append(value)
            carry = value
        solved = [None] * len(blocks)
        carry = None
        for block in reversed(range(cells // tile)):
            rows = slice(block * tile, (block + 1) * tile)
            inverse = tuple(far_ref[plane + p, 1, rows] for p in range(parts))
            value = c_mul(inverse, blocks[block])
            if carry is not None:
                substitute = tuple(far_ref[plane + p, 2, rows] for p in range(parts))
                value = c_sub(value, c_mul(substitute, carry))
            solved[block] = value
            carry = value
        spectrum.append((j, parts, solved))
        plane += parts
    total = jnp.zeros((tile, lanes), jnp.float32)
    for block in range(cells // tile):
        rows = slice(block * tile, (block + 1) * tile)
        steps = []
        for n in range(length):
            fresh = None
            for j, parts, solved in spectrum:
                weights = turn(j, n, length)
                fresh = weighted(fresh, parts * weights[0], solved[block][0])
                if parts == 2:
                    fresh = weighted(fresh, -parts * weights[1], solved[block][1])
            fresh = fresh * (math.exp(-log_alpha * n / length) / length)
            steps.append(fresh)
            change = fresh - befores[n][rows]
            total = total + change * change
        own = steps[0]
        give = steps[1]
        for n in range(1, length):
            own = jnp.where(me == n, steps[n], own)
            give = jnp.where(me == n, steps[n ^ 1], give)
        own_ref[rows] = own
        give_ref[rows] = give
    sum_ref[...] = jnp.full(sum_ref.shape, jnp.sum(total), jnp.float32)


def join_kernel(
    entry_count, own_ref, got_ref, squares_ref, new_hbm, norm_hbm, norm_ref, sems
):
    species = lax.axis_index("tm") % 2
    copies = (
        pltpu.make_async_copy(own_ref, new_hbm.at[0, species], sems.at[0]),
        pltpu.make_async_copy(got_ref, new_hbm.at[0, 1 - species], sems.at[1]),
        pltpu.make_async_copy(norm_ref, norm_hbm, sems.at[2]),
    )
    copies[0].start()
    copies[1].start()
    norm_ref[0, 0] = jnp.sqrt(jnp.sum(squares_ref[...], axis=0)[0, 0] / entry_count)
    copies[2].start()
    for copy in copies:
        copy.wait()


def exchange(value, axis, bits):
    pairs = [(index, index ^ bits) for index in range(lax.axis_size(axis))]
    return lax.ppermute(value, axis, pairs)


def shards(
    forcing,
    initial_state,
    previous,
    zone_diffusion,
    drift_rate,
    column_zone,
    bottom_flag,
    open_faces,
):
    length = lax.axis_size("tm")
    space = lax.axis_size("space")
    cells, lanes = open_faces.shape
    whole = pl.BlockSpec(memory_space=pltpu.VMEM)
    outside = pl.BlockSpec(memory_space=pltpu.HBM)
    count = planes(length)
    params = pltpu.CompilerParams(vmem_limit_bytes=40 * 1024 * 1024)
    alone = pltpu.CompilerParams(vmem_limit_bytes=56 * 1024 * 1024)
    mine, other = pl.pallas_call(
        stack_kernel,
        out_shape=(
            pltpu.VMEM((2, cells, lanes), jnp.float32),
            pltpu.VMEM((2, cells, lanes), jnp.float32),
        ),
        in_specs=[outside] * 2,
        out_specs=[whole] * 2,
        scratch_shapes=[pltpu.SemaphoreType.DMA((8,))],
        compiler_params=alone,
        cost_estimate=pl.CostEstimate(flops=4000, bytes_accessed=500000, transcendentals=0),
        name="stack_arrays",
    )(forcing, previous)
    stacks = [mine]
    for bits in range(1, length):
        stacks.append(exchange(other if bits % 2 else mine, "tm", bits))
    near, far, initial = pl.pallas_call(
        functools.partial(factor_kernel, length),
        out_shape=(
            pltpu.VMEM((count, 2 * near_steps, cells, lanes), jnp.float32),
            pltpu.VMEM((count, 3, cells, lanes), jnp.float32),
            pltpu.VMEM((cells, lanes), jnp.float32),
        ),
        in_specs=[outside] * 6,
        out_specs=[whole] * 3,
        scratch_shapes=[
            pltpu.SMEM(zone_diffusion.shape, jnp.float32),
            pltpu.SMEM(drift_rate.shape, jnp.float32),
            pltpu.VMEM((1, lanes), jnp.int32),
            pltpu.VMEM((1, lanes), jnp.int32),
            pltpu.VMEM((cells, lanes), jnp.int32),
            pltpu.SemaphoreType.DMA((6,)),
        ],
        compiler_params=alone,
        cost_estimate=pl.CostEstimate(flops=4000000, bytes_accessed=3000000, transcendentals=0),
        name="factor_lines",
    )(initial_state, zone_diffusion, drift_rate, column_zone[None], bottom_flag[None], open_faces)
    own, give, squares = pl.pallas_call(
        functools.partial(sweep_kernel, length),
        out_shape=(
            pltpu.VMEM((cells, lanes), jnp.float32),
            pltpu.VMEM((cells, lanes), jnp.float32),
            pltpu.VMEM((2 * space, 1, lanes), jnp.float32),
        ),
        in_specs=[whole] * (length + 3),
        out_specs=[whole] * 3,
        compiler_params=params,
        cost_estimate=pl.CostEstimate(flops=4000000, bytes_accessed=3000000, transcendentals=0),
        name="solve_lines",
    )(*stacks, initial, near, far)
    got = exchange(give, "tm", 1)
    last = 2 * space - 1
    order = [last, *range(2, last, 2), *range(3, last, 2), 1, 0]
    groups = [[step * space + index for index in order] for step in range(0, length, 2)]
    squares = lax.all_to_all(
        squares, ("tm", "space"), 0, 0, axis_index_groups=groups, tiled=True
    )
    entry_count = length * space * forcing.shape[1] * cells * lanes
    new_iterate, norm = pl.pallas_call(
        functools.partial(join_kernel, entry_count),
        out_shape=(
            jax.ShapeDtypeStruct(forcing.shape, jnp.float32),
            jax.ShapeDtypeStruct((1, 1), jnp.float32),
        ),
        in_specs=[whole] * 3,
        out_specs=(outside, outside),
        scratch_shapes=[pltpu.SMEM((1, 1), jnp.float32), pltpu.SemaphoreType.DMA((3,))],
        compiler_params=params,
        cost_estimate=pl.CostEstimate(flops=4000, bytes_accessed=100000, transcendentals=0),
        name="join_species",
    )(own, got, squares)
    return (new_iterate, norm[0, 0])


def solution(mesh):
    placed = (
        P("tm", None, None, "space"),
        P(None, None, "space"),
        P("tm", None, None, "space"),
        P(),
        P(),
        P("space"),
        P("space"),
        P(None, "space"),
    )
    return jax.shard_map(
        shards,
        mesh=mesh,
        in_specs=placed,
        out_specs=(P("tm", None, None, "space"), P()),
        check_vma=False,
    )
```

```python
import functools
import math

import jax
import jax.numpy as jnp
from jax import lax
from jax.experimental import pallas as pl
from jax.experimental.pallas import tpu as pltpu
from jax.sharding import PartitionSpec as P

alpha_corner = 0.3
tile = 8
near_steps = 3


def roll_down(block, distance):
    return pltpu.roll(block, distance, 0)


def roll_up(block, distance):
    return pltpu.roll(block, block.shape[0] - distance, 0)


def c_mul(x, y):
    if len(x) == 1 and len(y) == 1:
        return (x[0] * y[0],)
    if len(x) == 1:
        return (x[0] * y[0], x[0] * y[1])
    if len(y) == 1:
        return (x[0] * y[0], x[1] * y[0])
    return (x[0] * y[0] - x[1] * y[1], x[0] * y[1] + x[1] * y[0])


def c_add(x, y):
    return tuple(p + q for p, q in zip(x, y))


def c_sub(x, y):
    return tuple(p - q for p, q in zip(x, y))


def c_neg(x):
    return tuple(-p for p in x)


def c_inverse(x):
    if len(x) == 1:
        return (1.0 / x[0],)
    scale = 1.0 / (x[0] * x[0] + x[1] * x[1])
    return (x[0] * scale, -x[1] * scale)


def c_map(f, x):
    return tuple(f(p) for p in x)


def frequencies(length):
    root = math.exp(math.log(alpha_corner) / length)
    listed = []
    for j in range(length // 2 + 1):
        angle = 2.0 * math.pi * j / length
        if j == 0 or 2 * j == length:
            listed.append((j, (1.0 - root * math.cos(angle),)))
        else:
            listed.append((j, (1.0 - root * math.cos(angle), root * math.sin(angle))))
    return listed


def planes(length):
    return sum(len(shift) for unused, shift in frequencies(length))


def turn(j, n, length):
    count = j * n % length
    if 4 * count % length == 0:
        return ((1.0, 0.0), (0.0, 1.0), (-1.0, 0.0), (0.0, -1.0))[4 * count // length]
    angle = 2.0 * math.pi * count / length
    return (math.cos(angle), math.sin(angle))


def weighted(total, weight, value):
    if weight == 0.0:
        return total
    if weight == 1.0:
        term = value
    elif weight == -1.0:
        return -value if total is None else total - value
    else:
        term = weight * value
    return term if total is None else total + term


def species_of(step):
    return (step ^ (step >> 1)) & 1


def start_all(pairs, sems):
    copies = [
        pltpu.make_async_copy(source, target, sems.at[index])
        for index, (source, target) in enumerate(pairs)
    ]
    for copy in copies:
        copy.start()
    return copies


def stack_kernel(forcing_hbm, previous_hbm, mine_ref, other_ref, sems):
    species = species_of(lax.axis_index("tm"))
    pairs = (
        (forcing_hbm.at[0, species], mine_ref.at[0]),
        (previous_hbm.at[0, species], mine_ref.at[1]),
        (forcing_hbm.at[0, 1 - species], other_ref.at[0]),
        (previous_hbm.at[0, 1 - species], other_ref.at[1]),
    )
    for copy in start_all(pairs, sems):
        copy.wait()


def factor_kernel(
    length,
    initial_hbm,
    zones_hbm,
    drift_hbm,
    zone_hbm,
    flag_hbm,
    faces_hbm,
    near_ref,
    far_ref,
    initial_ref,
    zones_ref,
    drift_ref,
    zone_ref,
    flag_ref,
    faces_ref,
    sems,
):
    species = species_of(lax.axis_index("tm"))
    pairs = (
        (zones_hbm, zones_ref),
        (drift_hbm, drift_ref),
        (zone_hbm, zone_ref),
        (flag_hbm, flag_ref),
        (faces_hbm, faces_ref),
        (initial_hbm.at[species], initial_ref),
    )
    for copy in start_all(pairs, sems):
        copy.wait()
    zone = zone_ref[...]
    diffusion = jnp.zeros(zone.shape, jnp.float32)
    for index in range(zones_ref.shape[1]):
        diffusion = jnp.where(zone == index, zones_ref[species, index], diffusion)
    drift = drift_ref[species]
    cells, lanes = faces_ref.shape
    faces = faces_ref[...].astype(jnp.float32)
    row = lax.broadcasted_iota(jnp.int32, (cells, lanes), 0)
    link_above = jnp.where(row == cells - 1, 0.0, faces)
    link_below = jnp.where(row == 0, 0.0, roll_down(faces, 1))
    ground = jnp.where(row == 0, flag_ref[...].astype(jnp.float32), 0.0)
    below = -(diffusion + drift) * link_below
    above = -diffusion * link_above
    centre = diffusion * (link_below + link_above) + drift + 2.0 * diffusion * ground
    plane = 0
    for unused, shift in frequencies(length):
        parts = len(shift)
        a = (below,)
        c = (above,)
        b = (centre + shift[0],)
        if parts == 2:
            b = b + (jnp.full_like(centre, shift[1]),)
        for step in range(near_steps):
            distance = 1 << step
            inverse = c_inverse(b)
            low = c_neg(c_mul(a, c_map(lambda p: roll_down(p, distance), inverse)))
            high = c_neg(c_mul(c, c_map(lambda p: roll_up(p, distance), inverse)))
            down_c = c_map(lambda p: roll_down(p, distance), c)
            up_a = c_map(lambda p: roll_up(p, distance), a)
            b = c_add(b, c_add(c_mul(low, down_c), c_mul(high, up_a)))
            a = c_mul(low, c_map(lambda p: roll_down(p, distance), a))
            c = c_mul(high, c_map(lambda p: roll_up(p, distance), c))
            for part in range(parts):
                near_ref[plane + part, 2 * step] = low[part]
                near_ref[plane + part, 2 * step + 1] = high[part]
        carry = None
        for block in range(cells // tile):
            rows = slice(block * tile, (block + 1) * tile)
            ak, bk, ck = (c_map(lambda p: p[rows], item) for item in (a, b, c))
            if carry is None:
                eliminate = c_map(jnp.zeros_like, ak)
            else:
                eliminate = c_mul(ak, carry[0])
                bk = c_sub(bk, c_mul(eliminate, carry[1]))
            inverse = c_inverse(bk)
            substitute = c_mul(ck, inverse)
            for part in range(parts):
                far_ref[plane + part, 0, rows] = eliminate[part]
                far_ref[plane + part, 1, rows] = inverse[part]
                far_ref[plane + part, 2, rows] = substitute[part]
            carry = (inverse, ck)
        plane += parts


def in_order(me, held):
    bit = 1
    while bit < len(held):
        swap = (me & bit) != 0
        held = [
            jnp.where(swap, held[index ^ bit], held[index]) for index in range(len(held))
        ]
        bit *= 2
    return held


def sweep_kernel(length, *refs):
    stacks = refs[:length]
    initial_ref, near_ref, far_ref, own_ref, give_ref, sum_ref = refs[length:]
    cells, lanes = initial_ref.shape
    log_alpha = math.log(alpha_corner)
    me = lax.axis_index("tm")
    loads = in_order(me, [ref[0] for ref in stacks])
    befores = in_order(me, [ref[1] for ref in stacks])
    loads[0] = loads[0] + (initial_ref[...] - alpha_corner * befores[length - 1])
    scaled = [math.exp(log_alpha * n / length) * load for n, load in enumerate(loads)]
    spectrum = []
    plane = 0
    for j, shift in frequencies(length):
        parts = len(shift)
        rhs = [None] * parts
        for n in range(length):
            weights = turn(j, -n, length)
            for part in range(parts):
                rhs[part] = weighted(rhs[part], weights[part], scaled[n])
        rhs = tuple(rhs)
        for step in range(near_steps):
            distance = 1 << step
            low = tuple(near_ref[plane + p, 2 * step] for p in range(parts))
            high = tuple(near_ref[plane + p, 2 * step + 1] for p in range(parts))
            down = c_map(lambda p: roll_down(p, distance), rhs)
            up = c_map(lambda p: roll_up(p, distance), rhs)
            rhs = c_add(rhs, c_add(c_mul(low, down), c_mul(high, up)))
        blocks = []
        carry = None
        for block in range(cells // tile):
            rows = slice(block * tile, (block + 1) * tile)
            value = c_map(lambda p: p[rows], rhs)
            if carry is not None:
                eliminate = tuple(far_ref[plane + p, 0, rows] for p in range(parts))
                value = c_sub(value, c_mul(eliminate, carry))
            blocks.append(value)
            carry = value
        solved = [None] * len(blocks)
        carry = None
        for block in reversed(range(cells // tile)):
            rows = slice(block * tile, (block + 1) * tile)
            inverse = tuple(far_ref[plane + p, 1, rows] for p in range(parts))
            value = c_mul(inverse, blocks[block])
            if carry is not None:
                substitute = tuple(far_ref[plane + p, 2, rows] for p in range(parts))
                value = c_sub(value, c_mul(substitute, carry))
            solved[block] = value
            carry = value
        spectrum.append((j, parts, solved))
        plane += parts
    total = jnp.zeros((tile, lanes), jnp.float32)
    for block in range(cells // tile):
        rows = slice(block * tile, (block + 1) * tile)
        steps = []
        for n in range(length):
            fresh = None
            for j, parts, solved in spectrum:
                weights = turn(j, n, length)
                fresh = weighted(fresh, parts * weights[0], solved[block][0])
                if parts == 2:
                    fresh = weighted(fresh, -parts * weights[1], solved[block][1])
            fresh = fresh * (math.exp(-log_alpha * n / length) / length)
            steps.append(fresh)
            change = fresh - befores[n][rows]
            total = total + change * change
        own = steps[0]
        give = steps[1]
        for n in range(1, length):
            own = jnp.where(me == n, steps[n], own)
            give = jnp.where(me == n, steps[n ^ 1], give)
        own_ref[rows] = own
        give_ref[rows] = give
    sum_ref[...] = jnp.broadcast_to(jnp.sum(total, axis=0, keepdims=True), sum_ref.shape)


def join_kernel(
    entry_count, own_ref, got_ref, squares_ref, new_hbm, norm_hbm, norm_ref, sems
):
    species = species_of(lax.axis_index("tm"))
    copies = (
        pltpu.make_async_copy(own_ref, new_hbm.at[0, species], sems.at[0]),
        pltpu.make_async_copy(got_ref, new_hbm.at[0, 1 - species], sems.at[1]),
        pltpu.make_async_copy(norm_ref, norm_hbm, sems.at[2]),
    )
    copies[0].start()
    copies[1].start()
    norm_ref[0, 0] = jnp.sqrt(jnp.sum(squares_ref[...]) / entry_count)
    copies[2].start()
    for copy in copies:
        copy.wait()


def exchange(value, axis, bits):
    pairs = [(index, index ^ bits) for index in range(lax.axis_size(axis))]
    return lax.ppermute(value, axis, pairs)


def shards(
    forcing,
    initial_state,
    previous,
    zone_diffusion,
    drift_rate,
    column_zone,
    bottom_flag,
    open_faces,
):
    length = lax.axis_size("tm")
    space = lax.axis_size("space")
    cells, lanes = open_faces.shape
    whole = pl.BlockSpec(memory_space=pltpu.VMEM)
    outside = pl.BlockSpec(memory_space=pltpu.HBM)
    count = planes(length)
    params = pltpu.CompilerParams(vmem_limit_bytes=40 * 1024 * 1024)
    alone = pltpu.CompilerParams(vmem_limit_bytes=56 * 1024 * 1024)
    mine, other = pl.pallas_call(
        stack_kernel,
        out_shape=(
            pltpu.VMEM((2, cells, lanes), jnp.float32),
            pltpu.VMEM((2, cells, lanes), jnp.float32),
        ),
        in_specs=[outside] * 2,
        out_specs=[whole] * 2,
        scratch_shapes=[pltpu.SemaphoreType.DMA((4,))],
        compiler_params=alone,
        cost_estimate=pl.CostEstimate(flops=4000, bytes_accessed=500000, transcendentals=0),
        name="stack_arrays",
    )(forcing, previous)
    stacks = [mine]
    for bits in range(1, length):
        stacks.append(exchange(other if species_of(bits) else mine, "tm", bits))
    near, far, initial = pl.pallas_call(
        functools.partial(factor_kernel, length),
        out_shape=(
            pltpu.VMEM((count, 2 * near_steps, cells, lanes), jnp.float32),
            pltpu.VMEM((count, 3, cells, lanes), jnp.float32),
            pltpu.VMEM((cells, lanes), jnp.float32),
        ),
        in_specs=[outside] * 6,
        out_specs=[whole] * 3,
        scratch_shapes=[
            pltpu.SMEM(zone_diffusion.shape, jnp.float32),
            pltpu.SMEM(drift_rate.shape, jnp.float32),
            pltpu.VMEM((1, lanes), jnp.int32),
            pltpu.VMEM((1, lanes), jnp.int32),
            pltpu.VMEM((cells, lanes), jnp.int32),
            pltpu.SemaphoreType.DMA((6,)),
        ],
        compiler_params=alone,
        cost_estimate=pl.CostEstimate(flops=4000000, bytes_accessed=3000000, transcendentals=0),
        name="factor_lines",
    )(initial_state, zone_diffusion, drift_rate, column_zone[None], bottom_flag[None], open_faces)
    own, give, squares = pl.pallas_call(
        functools.partial(sweep_kernel, length),
        out_shape=(
            pltpu.VMEM((cells, lanes), jnp.float32),
            pltpu.VMEM((cells, lanes), jnp.float32),
            pltpu.VMEM((2 * space, 1, lanes), jnp.float32),
        ),
        in_specs=[whole] * (length + 3),
        out_specs=[whole] * 3,
        compiler_params=params,
        cost_estimate=pl.CostEstimate(flops=4000000, bytes_accessed=3000000, transcendentals=0),
        name="solve_lines",
    )(*stacks, initial, near, far)
    got = exchange(give, "tm", 1)
    last = 2 * space - 1
    order = [last, *range(2, last, 2), *range(3, last, 2), 1, 0]
    groups = [[step * space + index for index in order] for step in range(0, length, 2)]
    squares = lax.all_to_all(
        squares, ("tm", "space"), 0, 0, axis_index_groups=groups, tiled=True
    )
    entry_count = length * space * forcing.shape[1] * cells * lanes
    new_iterate, norm = pl.pallas_call(
        functools.partial(join_kernel, entry_count),
        out_shape=(
            jax.ShapeDtypeStruct(forcing.shape, jnp.float32),
            jax.ShapeDtypeStruct((1, 1), jnp.float32),
        ),
        in_specs=[whole] * 3,
        out_specs=(outside, outside),
        scratch_shapes=[pltpu.SMEM((1, 1), jnp.float32), pltpu.SemaphoreType.DMA((3,))],
        compiler_params=params,
        cost_estimate=pl.CostEstimate(flops=4000, bytes_accessed=100000, transcendentals=0),
        name="join_species",
    )(own, got, squares)
    return (new_iterate, norm[0, 0])


def solution(mesh):
    placed = (
        P("tm", None, None, "space"),
        P(None, None, "space"),
        P("tm", None, None, "space"),
        P(),
        P(),
        P("space"),
        P("space"),
        P(None, "space"),
    )
    return jax.shard_map(
        shards,
        mesh=mesh,
        in_specs=placed,
        out_specs=(P("tm", None, None, "space"), P()),
        check_vma=False,
    )
```

```python
import functools
import math

import jax
import jax.numpy as jnp
from jax import lax
from jax.experimental import pallas as pl
from jax.experimental.pallas import tpu as pltpu
from jax.sharding import PartitionSpec as P

alpha_corner = 0.3
tile = 8
near_steps = 3


def roll_down(block, distance):
    return pltpu.roll(block, distance, 0)


def roll_up(block, distance):
    return pltpu.roll(block, block.shape[0] - distance, 0)


def c_mul(x, y):
    if len(x) == 1 and len(y) == 1:
        return (x[0] * y[0],)
    if len(x) == 1:
        return (x[0] * y[0], x[0] * y[1])
    if len(y) == 1:
        return (x[0] * y[0], x[1] * y[0])
    return (x[0] * y[0] - x[1] * y[1], x[0] * y[1] + x[1] * y[0])


def c_add(x, y):
    return tuple(p + q for p, q in zip(x, y))


def c_sub(x, y):
    return tuple(p - q for p, q in zip(x, y))


def c_neg(x):
    return tuple(-p for p in x)


def c_inverse(x):
    if len(x) == 1:
        return (1.0 / x[0],)
    scale = 1.0 / (x[0] * x[0] + x[1] * x[1])
    return (x[0] * scale, -x[1] * scale)


def c_map(f, x):
    return tuple(f(p) for p in x)


def frequencies(length):
    root = math.exp(math.log(alpha_corner) / length)
    listed = []
    for j in range(length // 2 + 1):
        angle = 2.0 * math.pi * j / length
        if j == 0 or 2 * j == length:
            listed.append((j, (1.0 - root * math.cos(angle),)))
        else:
            listed.append((j, (1.0 - root * math.cos(angle), root * math.sin(angle))))
    return listed


def planes(length):
    return sum(len(shift) for unused, shift in frequencies(length))


def turn(j, n, length):
    count = j * n % length
    if 4 * count % length == 0:
        return ((1.0, 0.0), (0.0, 1.0), (-1.0, 0.0), (0.0, -1.0))[4 * count // length]
    angle = 2.0 * math.pi * count / length
    return (math.cos(angle), math.sin(angle))


def weighted(total, weight, value):
    if weight == 0.0:
        return total
    if weight == 1.0:
        term = value
    elif weight == -1.0:
        return -value if total is None else total - value
    else:
        term = weight * value
    return term if total is None else total + term


def start_all(pairs, sems):
    copies = [
        pltpu.make_async_copy(source, target, sems.at[index])
        for index, (source, target) in enumerate(pairs)
    ]
    for copy in copies:
        copy.start()
    return copies


def stack_kernel(forcing_hbm, previous_hbm, mine_ref, other_ref, sems):
    species = lax.axis_index("tm") % 2
    pairs = (
        (forcing_hbm.at[0, species], mine_ref.at[0]),
        (previous_hbm.at[0, species], mine_ref.at[1]),
        (forcing_hbm.at[0, 1 - species], other_ref.at[0]),
        (previous_hbm.at[0, 1 - species], other_ref.at[1]),
    )
    for copy in start_all(pairs, sems):
        copy.wait()


def factor_kernel(
    length,
    initial_hbm,
    zones_hbm,
    drift_hbm,
    zone_hbm,
    flag_hbm,
    faces_hbm,
    near_ref,
    far_ref,
    initial_ref,
    zones_ref,
    drift_ref,
    zone_ref,
    flag_ref,
    faces_ref,
    sems,
):
    species = lax.axis_index("tm") % 2
    pairs = (
        (zones_hbm, zones_ref),
        (drift_hbm, drift_ref),
        (zone_hbm, zone_ref),
        (flag_hbm, flag_ref),
        (faces_hbm, faces_ref),
        (initial_hbm.at[species], initial_ref),
    )
    for copy in start_all(pairs, sems):
        copy.wait()
    zone = zone_ref[...]
    diffusion = jnp.zeros(zone.shape, jnp.float32)
    for index in range(zones_ref.shape[1]):
        diffusion = jnp.where(zone == index, zones_ref[species, index], diffusion)
    drift = drift_ref[species]
    cells, lanes = faces_ref.shape
    faces = faces_ref[...].astype(jnp.float32)
    row = lax.broadcasted_iota(jnp.int32, (cells, lanes), 0)
    link_above = jnp.where(row == cells - 1, 0.0, faces)
    link_below = jnp.where(row == 0, 0.0, roll_down(faces, 1))
    ground = jnp.where(row == 0, flag_ref[...].astype(jnp.float32), 0.0)
    below = -(diffusion + drift) * link_below
    above = -diffusion * link_above
    centre = diffusion * (link_below + link_above) + drift + 2.0 * diffusion * ground
    plane = 0
    for unused, shift in frequencies(length):
        parts = len(shift)
        a = (below,)
        c = (above,)
        b = (centre + shift[0],)
        if parts == 2:
            b = b + (jnp.full_like(centre, shift[1]),)
        for step in range(near_steps):
            distance = 1 << step
            inverse = c_inverse(b)
            low = c_neg(c_mul(a, c_map(lambda p: roll_down(p, distance), inverse)))
            high = c_neg(c_mul(c, c_map(lambda p: roll_up(p, distance), inverse)))
            down_c = c_map(lambda p: roll_down(p, distance), c)
            up_a = c_map(lambda p: roll_up(p, distance), a)
            b = c_add(b, c_add(c_mul(low, down_c), c_mul(high, up_a)))
            a = c_mul(low, c_map(lambda p: roll_down(p, distance), a))
            c = c_mul(high, c_map(lambda p: roll_up(p, distance), c))
            for part in range(parts):
                near_ref[plane + part, 2 * step] = low[part]
                near_ref[plane + part, 2 * step + 1] = high[part]
        carry = None
        for block in range(cells // tile):
            rows = slice(block * tile, (block + 1) * tile)
            ak, bk, ck = (c_map(lambda p: p[rows], item) for item in (a, b, c))
            if carry is None:
                eliminate = c_map(jnp.zeros_like, ak)
            else:
                eliminate = c_mul(ak, carry[0])
                bk = c_sub(bk, c_mul(eliminate, carry[1]))
            inverse = c_inverse(bk)
            substitute = c_mul(ck, inverse)
            for part in range(parts):
                far_ref[plane + part, 0, rows] = eliminate[part]
                far_ref[plane + part, 1, rows] = inverse[part]
                far_ref[plane + part, 2, rows] = substitute[part]
            carry = (inverse, ck)
        plane += parts


def in_order(me, held):
    bit = 1
    while bit < len(held):
        swap = (me & bit) != 0
        held = [
            jnp.where(swap, held[index ^ bit], held[index]) for index in range(len(held))
        ]
        bit *= 2
    return held


def sweep_kernel(length, *refs):
    stacks = [refs[0], refs[length - 1], *refs[1 : length - 1]]
    initial_ref, near_ref, far_ref, own_ref, give_ref, sum_ref = refs[length:]
    cells, lanes = initial_ref.shape
    log_alpha = math.log(alpha_corner)
    me = lax.axis_index("tm")
    loads = in_order(me, [ref[0] for ref in stacks])
    befores = in_order(me, [ref[1] for ref in stacks])
    loads[0] = loads[0] + (initial_ref[...] - alpha_corner * befores[length - 1])
    scaled = [math.exp(log_alpha * n / length) * load for n, load in enumerate(loads)]
    spectrum = []
    plane = 0
    for j, shift in frequencies(length):
        parts = len(shift)
        rhs = [None] * parts
        for n in range(length):
            weights = turn(j, -n, length)
            for part in range(parts):
                rhs[part] = weighted(rhs[part], weights[part], scaled[n])
        rhs = tuple(rhs)
        for step in range(near_steps):
            distance = 1 << step
            low = tuple(near_ref[plane + p, 2 * step] for p in range(parts))
            high = tuple(near_ref[plane + p, 2 * step + 1] for p in range(parts))
            down = c_map(lambda p: roll_down(p, distance), rhs)
            up = c_map(lambda p: roll_up(p, distance), rhs)
            rhs = c_add(rhs, c_add(c_mul(low, down), c_mul(high, up)))
        blocks = []
        carry = None
        for block in range(cells // tile):
            rows = slice(block * tile, (block + 1) * tile)
            value = c_map(lambda p: p[rows], rhs)
            if carry is not None:
                eliminate = tuple(far_ref[plane + p, 0, rows] for p in range(parts))
                value = c_sub(value, c_mul(eliminate, carry))
            blocks.append(value)
            carry = value
        solved = [None] * len(blocks)
        carry = None
        for block in reversed(range(cells // tile)):
            rows = slice(block * tile, (block + 1) * tile)
            inverse = tuple(far_ref[plane + p, 1, rows] for p in range(parts))
            value = c_mul(inverse, blocks[block])
            if carry is not None:
                substitute = tuple(far_ref[plane + p, 2, rows] for p in range(parts))
                value = c_sub(value, c_mul(substitute, carry))
            solved[block] = value
            carry = value
        spectrum.append((j, parts, solved))
        plane += parts
    total = jnp.zeros((tile, lanes), jnp.float32)
    for block in range(cells // tile):
        rows = slice(block * tile, (block + 1) * tile)
        steps = []
        for n in range(length):
            fresh = None
            for j, parts, solved in spectrum:
                weights = turn(j, n, length)
                fresh = weighted(fresh, parts * weights[0], solved[block][0])
                if parts == 2:
                    fresh = weighted(fresh, -parts * weights[1], solved[block][1])
            fresh = fresh * (math.exp(-log_alpha * n / length) / length)
            steps.append(fresh)
            change = fresh - befores[n][rows]
            total = total + change * change
        own = steps[0]
        give = steps[1]
        for n in range(1, length):
            own = jnp.where(me == n, steps[n], own)
            give = jnp.where(me == n, steps[n ^ 1], give)
        own_ref[rows] = own
        give_ref[rows] = give
    sum_ref[...] = jnp.broadcast_to(jnp.sum(total, axis=0, keepdims=True), sum_ref.shape)


def join_kernel(
    entry_count, own_ref, got_ref, squares_ref, new_hbm, norm_hbm, norm_ref, sems
):
    species = lax.axis_index("tm") % 2
    copies = (
        pltpu.make_async_copy(own_ref, new_hbm.at[0, species], sems.at[0]),
        pltpu.make_async_copy(got_ref, new_hbm.at[0, 1 - species], sems.at[1]),
        pltpu.make_async_copy(norm_ref, norm_hbm, sems.at[2]),
    )
    copies[0].start()
    copies[1].start()
    norm_ref[0, 0] = jnp.sqrt(jnp.sum(squares_ref[...]) / entry_count)
    copies[2].start()
    for copy in copies:
        copy.wait()


def exchange(value, axis, bits):
    pairs = [(index, index ^ bits) for index in range(lax.axis_size(axis))]
    return lax.ppermute(value, axis, pairs)


def shards(
    forcing,
    initial_state,
    previous,
    zone_diffusion,
    drift_rate,
    column_zone,
    bottom_flag,
    open_faces,
):
    length = lax.axis_size("tm")
    space = lax.axis_size("space")
    cells, lanes = open_faces.shape
    whole = pl.BlockSpec(memory_space=pltpu.VMEM)
    outside = pl.BlockSpec(memory_space=pltpu.HBM)
    count = planes(length)
    params = pltpu.CompilerParams(vmem_limit_bytes=40 * 1024 * 1024)
    alone = pltpu.CompilerParams(vmem_limit_bytes=56 * 1024 * 1024)
    mine, other = pl.pallas_call(
        stack_kernel,
        out_shape=(
            pltpu.VMEM((2, cells, lanes), jnp.float32),
            pltpu.VMEM((2, cells, lanes), jnp.float32),
        ),
        in_specs=[outside] * 2,
        out_specs=[whole] * 2,
        scratch_shapes=[pltpu.SemaphoreType.DMA((4,))],
        compiler_params=alone,
        cost_estimate=pl.CostEstimate(flops=4000, bytes_accessed=500000, transcendentals=0),
        name="stack_arrays",
    )(forcing, previous)
    stacks = [mine]
    for bits in range(1, length):
        stacks.append(exchange(other if bits % 2 else mine, "tm", bits))
    near, far, initial = pl.pallas_call(
        functools.partial(factor_kernel, length),
        out_shape=(
            pltpu.VMEM((count, 2 * near_steps, cells, lanes), jnp.float32),
            pltpu.VMEM((count, 3, cells, lanes), jnp.float32),
            pltpu.VMEM((cells, lanes), jnp.float32),
        ),
        in_specs=[outside] * 6,
        out_specs=[whole] * 3,
        scratch_shapes=[
            pltpu.SMEM(zone_diffusion.shape, jnp.float32),
            pltpu.SMEM(drift_rate.shape, jnp.float32),
            pltpu.VMEM((1, lanes), jnp.int32),
            pltpu.VMEM((1, lanes), jnp.int32),
            pltpu.VMEM((cells, lanes), jnp.int32),
            pltpu.SemaphoreType.DMA((6,)),
        ],
        compiler_params=alone,
        cost_estimate=pl.CostEstimate(flops=4000000, bytes_accessed=3000000, transcendentals=0),
        name="factor_lines",
    )(initial_state, zone_diffusion, drift_rate, column_zone[None], bottom_flag[None], open_faces)
    own, give, squares = pl.pallas_call(
        functools.partial(sweep_kernel, length),
        out_shape=(
            pltpu.VMEM((cells, lanes), jnp.float32),
            pltpu.VMEM((cells, lanes), jnp.float32),
            pltpu.VMEM((2 * space, 1, lanes), jnp.float32),
        ),
        in_specs=[whole] * (length + 3),
        out_specs=[whole] * 3,
        compiler_params=params,
        cost_estimate=pl.CostEstimate(flops=4000000, bytes_accessed=3000000, transcendentals=0),
        name="solve_lines",
    )(stacks[0], *stacks[2:], stacks[1], initial, near, far)
    got = exchange(give, "tm", 1)
    last = 2 * space - 1
    order = [last, *range(2, last, 2), *range(3, last, 2), 1, 0]
    groups = [[step * space + index for index in order] for step in range(0, length, 2)]
    squares = lax.all_to_all(
        squares, ("tm", "space"), 0, 0, axis_index_groups=groups, tiled=True
    )
    entry_count = length * space * forcing.shape[1] * cells * lanes
    new_iterate, norm = pl.pallas_call(
        functools.partial(join_kernel, entry_count),
        out_shape=(
            jax.ShapeDtypeStruct(forcing.shape, jnp.float32),
            jax.ShapeDtypeStruct((1, 1), jnp.float32),
        ),
        in_specs=[whole] * 3,
        out_specs=(outside, outside),
        scratch_shapes=[pltpu.SMEM((1, 1), jnp.float32), pltpu.SemaphoreType.DMA((3,))],
        compiler_params=params,
        cost_estimate=pl.CostEstimate(flops=4000, bytes_accessed=100000, transcendentals=0),
        name="join_species",
    )(own, got, squares)
    return (new_iterate, norm[0, 0])


def solution(mesh):
    placed = (
        P("tm", None, None, "space"),
        P(None, None, "space"),
        P("tm", None, None, "space"),
        P(),
        P(),
        P("space"),
        P("space"),
        P(None, "space"),
    )
    return jax.shard_map(
        shards,
        mesh=mesh,
        in_specs=placed,
        out_specs=(P("tm", None, None, "space"), P()),
        check_vma=False,
    )
```

```python
import functools
import math

import jax
import jax.numpy as jnp
from jax import lax
from jax.experimental import pallas as pl
from jax.experimental.pallas import tpu as pltpu
from jax.sharding import PartitionSpec as P

alpha_corner = 0.3
tile = 8
near_steps = 3


def roll_down(block, distance):
    return pltpu.roll(block, distance, 0)


def roll_up(block, distance):
    return pltpu.roll(block, block.shape[0] - distance, 0)


def c_mul(x, y):
    if len(x) == 1 and len(y) == 1:
        return (x[0] * y[0],)
    if len(x) == 1:
        return (x[0] * y[0], x[0] * y[1])
    if len(y) == 1:
        return (x[0] * y[0], x[1] * y[0])
    return (x[0] * y[0] - x[1] * y[1], x[0] * y[1] + x[1] * y[0])


def c_add(x, y):
    return tuple(p + q for p, q in zip(x, y))


def c_sub(x, y):
    return tuple(p - q for p, q in zip(x, y))


def c_neg(x):
    return tuple(-p for p in x)


def c_inverse(x):
    if len(x) == 1:
        return (1.0 / x[0],)
    scale = 1.0 / (x[0] * x[0] + x[1] * x[1])
    return (x[0] * scale, -x[1] * scale)


def c_map(f, x):
    return tuple(f(p) for p in x)


def frequencies(length):
    root = math.exp(math.log(alpha_corner) / length)
    listed = []
    for j in range(length // 2 + 1):
        angle = 2.0 * math.pi * j / length
        if j == 0 or 2 * j == length:
            listed.append((j, (1.0 - root * math.cos(angle),)))
        else:
            listed.append((j, (1.0 - root * math.cos(angle), root * math.sin(angle))))
    return listed


def planes(length):
    return sum(len(shift) for unused, shift in frequencies(length))


def turn(j, n, length):
    count = j * n % length
    if 4 * count % length == 0:
        return ((1.0, 0.0), (0.0, 1.0), (-1.0, 0.0), (0.0, -1.0))[4 * count // length]
    angle = 2.0 * math.pi * count / length
    return (math.cos(angle), math.sin(angle))


def weighted(total, weight, value):
    if weight == 0.0:
        return total
    if weight == 1.0:
        term = value
    elif weight == -1.0:
        return -value if total is None else total - value
    else:
        term = weight * value
    return term if total is None else total + term


def start_all(pairs, sems):
    copies = [
        pltpu.make_async_copy(source, target, sems.at[index])
        for index, (source, target) in enumerate(pairs)
    ]
    for copy in copies:
        copy.start()
    return copies


def stack_kernel(forcing_hbm, previous_hbm, mine_ref, other_ref, sems):
    species = lax.axis_index("tm") % 2
    pairs = (
        (forcing_hbm.at[0, species], mine_ref.at[0]),
        (previous_hbm.at[0, species], mine_ref.at[1]),
        (forcing_hbm.at[0, 1 - species], other_ref.at[0]),
        (previous_hbm.at[0, 1 - species], other_ref.at[1]),
    )
    for copy in start_all(pairs, sems):
        copy.wait()


def factor_kernel(
    length,
    initial_hbm,
    zones_hbm,
    drift_hbm,
    zone_hbm,
    flag_hbm,
    faces_hbm,
    near_ref,
    far_ref,
    initial_ref,
    zones_ref,
    drift_ref,
    zone_ref,
    flag_ref,
    faces_ref,
    sems,
):
    species = lax.axis_index("tm") % 2
    pairs = (
        (zones_hbm, zones_ref),
        (drift_hbm, drift_ref),
        (zone_hbm, zone_ref),
        (flag_hbm, flag_ref),
        (faces_hbm, faces_ref),
        (initial_hbm.at[species], initial_ref),
    )
    for copy in start_all(pairs, sems):
        copy.wait()
    zone = zone_ref[...]
    diffusion = jnp.zeros(zone.shape, jnp.float32)
    for index in range(zones_ref.shape[1]):
        diffusion = jnp.where(zone == index, zones_ref[species, index], diffusion)
    drift = drift_ref[species]
    cells, lanes = faces_ref.shape
    faces = faces_ref[...].astype(jnp.float32)
    row = lax.broadcasted_iota(jnp.int32, (cells, lanes), 0)
    link_above = jnp.where(row == cells - 1, 0.0, faces)
    link_below = jnp.where(row == 0, 0.0, roll_down(faces, 1))
    ground = jnp.where(row == 0, flag_ref[...].astype(jnp.float32), 0.0)
    below = -(diffusion + drift) * link_below
    above = -diffusion * link_above
    centre = diffusion * (link_below + link_above) + drift + 2.0 * diffusion * ground
    plane = 0
    for unused, shift in frequencies(length):
        parts = len(shift)
        a = (below,)
        c = (above,)
        b = (centre + shift[0],)
        if parts == 2:
            b = b + (jnp.full_like(centre, shift[1]),)
        for step in range(near_steps):
            distance = 1 << step
            inverse = c_inverse(b)
            low = c_neg(c_mul(a, c_map(lambda p: roll_down(p, distance), inverse)))
            high = c_neg(c_mul(c, c_map(lambda p: roll_up(p, distance), inverse)))
            down_c = c_map(lambda p: roll_down(p, distance), c)
            up_a = c_map(lambda p: roll_up(p, distance), a)
            b = c_add(b, c_add(c_mul(low, down_c), c_mul(high, up_a)))
            a = c_mul(low, c_map(lambda p: roll_down(p, distance), a))
            c = c_mul(high, c_map(lambda p: roll_up(p, distance), c))
            for part in range(parts):
                near_ref[plane + part, 2 * step] = low[part]
                near_ref[plane + part, 2 * step + 1] = high[part]
        carry = None
        for block in range(cells // tile):
            rows = slice(block * tile, (block + 1) * tile)
            ak, bk, ck = (c_map(lambda p: p[rows], item) for item in (a, b, c))
            if carry is None:
                eliminate = c_map(jnp.zeros_like, ak)
            else:
                eliminate = c_mul(ak, carry[0])
                bk = c_sub(bk, c_mul(eliminate, carry[1]))
            inverse = c_inverse(bk)
            substitute = c_mul(ck, inverse)
            for part in range(parts):
                far_ref[plane + part, 0, rows] = eliminate[part]
                far_ref[plane + part, 1, rows] = inverse[part]
                far_ref[plane + part, 2, rows] = substitute[part]
            carry = (inverse, ck)
        plane += parts


def in_order(me, held):
    bit = 1
    while bit < len(held):
        swap = (me & bit) != 0
        held = [
            jnp.where(swap, held[index ^ bit], held[index]) for index in range(len(held))
        ]
        bit *= 2
    return held


def sweep_kernel(length, *refs):
    stacks = refs[:length]
    initial_ref, near_ref, far_ref, own_ref, give_ref, sum_ref = refs[length:]
    cells, lanes = initial_ref.shape
    log_alpha = math.log(alpha_corner)
    me = lax.axis_index("tm")
    loads = in_order(me, [ref[0] for ref in stacks])
    befores = in_order(me, [ref[1] for ref in stacks])
    loads[0] = loads[0] + (initial_ref[...] - alpha_corner * befores[length - 1])
    scaled = [math.exp(log_alpha * n / length) * load for n, load in enumerate(loads)]
    spectrum = []
    plane = 0
    for j, shift in frequencies(length):
        parts = len(shift)
        rhs = [None] * parts
        for n in range(length):
            weights = turn(j, -n, length)
            for part in range(parts):
                rhs[part] = weighted(rhs[part], weights[part], scaled[n])
        rhs = tuple(rhs)
        for step in range(near_steps):
            distance = 1 << step
            low = tuple(near_ref[plane + p, 2 * step] for p in range(parts))
            high = tuple(near_ref[plane + p, 2 * step + 1] for p in range(parts))
            down = c_map(lambda p: roll_down(p, distance), rhs)
            up = c_map(lambda p: roll_up(p, distance), rhs)
            rhs = c_add(rhs, c_add(c_mul(low, down), c_mul(high, up)))
        blocks = []
        carry = None
        for block in range(cells // tile):
            rows = slice(block * tile, (block + 1) * tile)
            value = c_map(lambda p: p[rows], rhs)
            if carry is not None:
                eliminate = tuple(far_ref[plane + p, 0, rows] for p in range(parts))
                value = c_sub(value, c_mul(eliminate, carry))
            blocks.append(value)
            carry = value
        solved = [None] * len(blocks)
        carry = None
        for block in reversed(range(cells // tile)):
            rows = slice(block * tile, (block + 1) * tile)
            inverse = tuple(far_ref[plane + p, 1, rows] for p in range(parts))
            value = c_mul(inverse, blocks[block])
            if carry is not None:
                substitute = tuple(far_ref[plane + p, 2, rows] for p in range(parts))
                value = c_sub(value, c_mul(substitute, carry))
            solved[block] = value
            carry = value
        spectrum.append((j, parts, solved))
        plane += parts
    total = jnp.zeros((tile, lanes), jnp.float32)
    for block in range(cells // tile):
        rows = slice(block * tile, (block + 1) * tile)
        steps = []
        for n in range(length):
            fresh = None
            for j, parts, solved in spectrum:
                weights = turn(j, n, length)
                fresh = weighted(fresh, parts * weights[0], solved[block][0])
                if parts == 2:
                    fresh = weighted(fresh, -parts * weights[1], solved[block][1])
            fresh = fresh * (math.exp(-log_alpha * n / length) / length)
            steps.append(fresh)
            change = fresh - befores[n][rows]
            total = total + change * change
        own = steps[0]
        give = steps[1]
        for n in range(1, length):
            own = jnp.where(me == n, steps[n], own)
            give = jnp.where(me == n, steps[n ^ 1], give)
        own_ref[rows] = own
        give_ref[rows] = give
    sum_ref[...] = jnp.broadcast_to(jnp.sum(total, axis=0, keepdims=True), sum_ref.shape)


def join_kernel(
    entry_count, own_ref, got_ref, squares_ref, new_hbm, norm_hbm, norm_ref, sems
):
    species = lax.axis_index("tm") % 2
    copies = (
        pltpu.make_async_copy(own_ref, new_hbm.at[0, species], sems.at[0]),
        pltpu.make_async_copy(got_ref, new_hbm.at[0, 1 - species], sems.at[1]),
        pltpu.make_async_copy(norm_ref, norm_hbm, sems.at[2]),
    )
    copies[0].start()
    copies[1].start()
    norm_ref[0, 0] = jnp.sqrt(jnp.sum(squares_ref[...]) / entry_count)
    copies[2].start()
    for copy in copies:
        copy.wait()


def exchange(value, axis, bits):
    pairs = [(index, index ^ bits) for index in range(lax.axis_size(axis))]
    return lax.ppermute(value, axis, pairs)


def shards(
    forcing,
    initial_state,
    previous,
    zone_diffusion,
    drift_rate,
    column_zone,
    bottom_flag,
    open_faces,
):
    length = lax.axis_size("tm")
    space = lax.axis_size("space")
    cells, lanes = open_faces.shape
    whole = pl.BlockSpec(memory_space=pltpu.VMEM)
    outside = pl.BlockSpec(memory_space=pltpu.HBM)
    count = planes(length)
    params = pltpu.CompilerParams(vmem_limit_bytes=40 * 1024 * 1024)
    alone = pltpu.CompilerParams(vmem_limit_bytes=56 * 1024 * 1024)
    mine, other = pl.pallas_call(
        stack_kernel,
        out_shape=(
            pltpu.VMEM((2, cells, lanes), jnp.float32),
            pltpu.VMEM((2, cells, lanes), jnp.float32),
        ),
        in_specs=[outside] * 2,
        out_specs=[whole] * 2,
        scratch_shapes=[pltpu.SemaphoreType.DMA((4,))],
        compiler_params=alone,
        cost_estimate=pl.CostEstimate(flops=4000, bytes_accessed=500000, transcendentals=0),
        name="stack_arrays",
    )(forcing, previous)
    stacks = [mine]
    for bits in range(1, length):
        stacks.append(exchange(other if bits % 2 else mine, "tm", bits))
    near, far, initial = pl.pallas_call(
        functools.partial(factor_kernel, length),
        out_shape=(
            pltpu.VMEM((count, 2 * near_steps, cells, lanes), jnp.float32),
            pltpu.VMEM((count, 3, cells, lanes), jnp.float32),
            pltpu.VMEM((cells, lanes), jnp.float32),
        ),
        in_specs=[outside] * 6,
        out_specs=[whole] * 3,
        scratch_shapes=[
            pltpu.SMEM(zone_diffusion.shape, jnp.float32),
            pltpu.SMEM(drift_rate.shape, jnp.float32),
            pltpu.VMEM((1, lanes), jnp.int32),
            pltpu.VMEM((1, lanes), jnp.int32),
            pltpu.VMEM((cells, lanes), jnp.int32),
            pltpu.SemaphoreType.DMA((6,)),
        ],
        compiler_params=alone,
        cost_estimate=pl.CostEstimate(flops=4000000, bytes_accessed=3000000, transcendentals=0),
        name="factor_lines",
    )(initial_state, zone_diffusion, drift_rate, column_zone[None], bottom_flag[None], open_faces)
    own, give, squares = pl.pallas_call(
        functools.partial(sweep_kernel, length),
        out_shape=(
            pltpu.VMEM((cells, lanes), jnp.float32),
            pltpu.VMEM((cells, lanes), jnp.float32),
            pltpu.VMEM((1, lanes), jnp.float32),
        ),
        in_specs=[whole] * (length + 3),
        out_specs=[whole] * 3,
        compiler_params=params,
        cost_estimate=pl.CostEstimate(flops=4000000, bytes_accessed=3000000, transcendentals=0),
        name="solve_lines",
    )(*stacks, initial, near, far)
    last = 2 * space - 1
    squares = squares + exchange(squares, "space", 1)
    got = exchange(give, "tm", 1)
    first = [space * 2 - 1 - 2 * chip for chip in range(space - 1)] + [0]
    first[space // 2] = space - 2
    second = [space - 1] + [index ^ 1 for index in first if index != space - 2]
    groups = [
        [step * space + index for index in order]
        for step in range(0, length, 2)
        for order in (first, second)
    ]
    squares = lax.all_to_all(
        jnp.broadcast_to(squares[None], (space,) + squares.shape),
        ("tm", "space"),
        0,
        0,
        axis_index_groups=groups,
        tiled=True,
    )
    entry_count = length * space * forcing.shape[1] * cells * lanes
    new_iterate, norm = pl.pallas_call(
        functools.partial(join_kernel, entry_count),
        out_shape=(
            jax.ShapeDtypeStruct(forcing.shape, jnp.float32),
            jax.ShapeDtypeStruct((1, 1), jnp.float32),
        ),
        in_specs=[whole] * 3,
        out_specs=(outside, outside),
        scratch_shapes=[pltpu.SMEM((1, 1), jnp.float32), pltpu.SemaphoreType.DMA((3,))],
        compiler_params=params,
        cost_estimate=pl.CostEstimate(flops=4000, bytes_accessed=100000, transcendentals=0),
        name="join_species",
    )(own, got, squares)
    return (new_iterate, norm[0, 0])


def solution(mesh):
    placed = (
        P("tm", None, None, "space"),
        P(None, None, "space"),
        P("tm", None, None, "space"),
        P(),
        P(),
        P("space"),
        P("space"),
        P(None, "space"),
    )
    return jax.shard_map(
        shards,
        mesh=mesh,
        in_specs=placed,
        out_specs=(P("tm", None, None, "space"), P()),
        check_vma=False,
    )
```

```python
import functools
import math

import jax
import jax.numpy as jnp
from jax import lax
from jax.experimental import pallas as pl
from jax.experimental.pallas import tpu as pltpu
from jax.sharding import PartitionSpec as P

alpha_corner = 0.3
tile = 8
near_steps = 3


def roll_down(block, distance):
    return pltpu.roll(block, distance, 0)


def roll_up(block, distance):
    return pltpu.roll(block, block.shape[0] - distance, 0)


def c_mul(x, y):
    if len(x) == 1 and len(y) == 1:
        return (x[0] * y[0],)
    if len(x) == 1:
        return (x[0] * y[0], x[0] * y[1])
    if len(y) == 1:
        return (x[0] * y[0], x[1] * y[0])
    return (x[0] * y[0] - x[1] * y[1], x[0] * y[1] + x[1] * y[0])


def c_add(x, y):
    return tuple(p + q for p, q in zip(x, y))


def c_sub(x, y):
    return tuple(p - q for p, q in zip(x, y))


def c_neg(x):
    return tuple(-p for p in x)


def c_inverse(x):
    if len(x) == 1:
        return (1.0 / x[0],)
    scale = 1.0 / (x[0] * x[0] + x[1] * x[1])
    return (x[0] * scale, -x[1] * scale)


def c_map(f, x):
    return tuple(f(p) for p in x)


def frequencies(length):
    root = math.exp(math.log(alpha_corner) / length)
    listed = []
    for j in range(length // 2 + 1):
        angle = 2.0 * math.pi * j / length
        if j == 0 or 2 * j == length:
            listed.append((j, (1.0 - root * math.cos(angle),)))
        else:
            listed.append((j, (1.0 - root * math.cos(angle), root * math.sin(angle))))
    return listed


def planes(length):
    return sum(len(shift) for unused, shift in frequencies(length))


def turn(j, n, length):
    count = j * n % length
    if 4 * count % length == 0:
        return ((1.0, 0.0), (0.0, 1.0), (-1.0, 0.0), (0.0, -1.0))[4 * count // length]
    angle = 2.0 * math.pi * count / length
    return (math.cos(angle), math.sin(angle))


def weighted(total, weight, value):
    if weight == 0.0:
        return total
    if weight == 1.0:
        term = value
    elif weight == -1.0:
        return -value if total is None else total - value
    else:
        term = weight * value
    return term if total is None else total + term


def start_all(pairs, sems):
    copies = [
        pltpu.make_async_copy(source, target, sems.at[index])
        for index, (source, target) in enumerate(pairs)
    ]
    for copy in copies:
        copy.start()
    return copies


def stack_kernel(forcing_hbm, previous_hbm, mine_ref, other_ref, sems):
    species = lax.axis_index("tm") % 2
    pairs = (
        (forcing_hbm.at[0, species], mine_ref.at[0]),
        (previous_hbm.at[0, species], mine_ref.at[1]),
        (forcing_hbm.at[0, 1 - species], other_ref.at[0]),
        (previous_hbm.at[0, 1 - species], other_ref.at[1]),
    )
    for copy in start_all(pairs, sems):
        copy.wait()


def factor_kernel(
    length,
    initial_hbm,
    zones_hbm,
    drift_hbm,
    zone_hbm,
    flag_hbm,
    faces_hbm,
    near_ref,
    far_ref,
    initial_ref,
    zones_ref,
    drift_ref,
    zone_ref,
    flag_ref,
    faces_ref,
    sems,
):
    species = lax.axis_index("tm") % 2
    pairs = (
        (zones_hbm, zones_ref),
        (drift_hbm, drift_ref),
        (zone_hbm, zone_ref),
        (flag_hbm, flag_ref),
        (faces_hbm, faces_ref),
        (initial_hbm.at[species], initial_ref),
    )
    for copy in start_all(pairs, sems):
        copy.wait()
    zone = zone_ref[...]
    diffusion = jnp.zeros(zone.shape, jnp.float32)
    for index in range(zones_ref.shape[1]):
        diffusion = jnp.where(zone == index, zones_ref[species, index], diffusion)
    drift = drift_ref[species]
    cells, lanes = faces_ref.shape
    faces = faces_ref[...].astype(jnp.float32)
    row = lax.broadcasted_iota(jnp.int32, (cells, lanes), 0)
    link_above = jnp.where(row == cells - 1, 0.0, faces)
    link_below = jnp.where(row == 0, 0.0, roll_down(faces, 1))
    ground = jnp.where(row == 0, flag_ref[...].astype(jnp.float32), 0.0)
    below = -(diffusion + drift) * link_below
    above = -diffusion * link_above
    centre = diffusion * (link_below + link_above) + drift + 2.0 * diffusion * ground
    plane = 0
    for unused, shift in frequencies(length):
        parts = len(shift)
        a = (below,)
        c = (above,)
        b = (centre + shift[0],)
        if parts == 2:
            b = b + (jnp.full_like(centre, shift[1]),)
        for step in range(near_steps):
            distance = 1 << step
            inverse = c_inverse(b)
            low = c_neg(c_mul(a, c_map(lambda p: roll_down(p, distance), inverse)))
            high = c_neg(c_mul(c, c_map(lambda p: roll_up(p, distance), inverse)))
            down_c = c_map(lambda p: roll_down(p, distance), c)
            up_a = c_map(lambda p: roll_up(p, distance), a)
            b = c_add(b, c_add(c_mul(low, down_c), c_mul(high, up_a)))
            a = c_mul(low, c_map(lambda p: roll_down(p, distance), a))
            c = c_mul(high, c_map(lambda p: roll_up(p, distance), c))
            for part in range(parts):
                near_ref[plane + part, 2 * step] = low[part]
                near_ref[plane + part, 2 * step + 1] = high[part]
        carry = None
        for block in range(cells // tile):
            rows = slice(block * tile, (block + 1) * tile)
            ak, bk, ck = (c_map(lambda p: p[rows], item) for item in (a, b, c))
            if carry is None:
                eliminate = c_map(jnp.zeros_like, ak)
            else:
                eliminate = c_mul(ak, carry[0])
                bk = c_sub(bk, c_mul(eliminate, carry[1]))
            inverse = c_inverse(bk)
            substitute = c_mul(ck, inverse)
            for part in range(parts):
                far_ref[plane + part, 0, rows] = eliminate[part]
                far_ref[plane + part, 1, rows] = inverse[part]
                far_ref[plane + part, 2, rows] = substitute[part]
            carry = (inverse, ck)
        plane += parts


def in_order(me, held):
    bit = 1
    while bit < len(held):
        swap = (me & bit) != 0
        held = [
            jnp.where(swap, held[index ^ bit], held[index]) for index in range(len(held))
        ]
        bit *= 2
    return held


def sweep_kernel(length, *refs):
    stacks = refs[:length]
    initial_ref, near_ref, far_ref, own_ref, give_ref, sum_ref = refs[length:]
    cells, lanes = initial_ref.shape
    log_alpha = math.log(alpha_corner)
    me = lax.axis_index("tm")
    loads = in_order(me, [ref[0] for ref in stacks])
    befores = in_order(me, [ref[1] for ref in stacks])
    loads[0] = loads[0] + (initial_ref[...] - alpha_corner * befores[length - 1])
    scaled = [math.exp(log_alpha * n / length) * load for n, load in enumerate(loads)]
    spectrum = []
    plane = 0
    for j, shift in frequencies(length):
        parts = len(shift)
        rhs = [None] * parts
        for n in range(length):
            weights = turn(j, -n, length)
            for part in range(parts):
                rhs[part] = weighted(rhs[part], weights[part], scaled[n])
        rhs = tuple(rhs)
        for step in range(near_steps):
            distance = 1 << step
            low = tuple(near_ref[plane + p, 2 * step] for p in range(parts))
            high = tuple(near_ref[plane + p, 2 * step + 1] for p in range(parts))
            down = c_map(lambda p: roll_down(p, distance), rhs)
            up = c_map(lambda p: roll_up(p, distance), rhs)
            rhs = c_add(rhs, c_add(c_mul(low, down), c_mul(high, up)))
        blocks = []
        carry = None
        for block in range(cells // tile):
            rows = slice(block * tile, (block + 1) * tile)
            value = c_map(lambda p: p[rows], rhs)
            if carry is not None:
                eliminate = tuple(far_ref[plane + p, 0, rows] for p in range(parts))
                value = c_sub(value, c_mul(eliminate, carry))
            blocks.append(value)
            carry = value
        solved = [None] * len(blocks)
        carry = None
        for block in reversed(range(cells // tile)):
            rows = slice(block * tile, (block + 1) * tile)
            inverse = tuple(far_ref[plane + p, 1, rows] for p in range(parts))
            value = c_mul(inverse, blocks[block])
            if carry is not None:
                substitute = tuple(far_ref[plane + p, 2, rows] for p in range(parts))
                value = c_sub(value, c_mul(substitute, carry))
            solved[block] = value
            carry = value
        spectrum.append((j, parts, solved))
        plane += parts
    total = jnp.zeros((tile, lanes), jnp.float32)
    for block in range(cells // tile):
        rows = slice(block * tile, (block + 1) * tile)
        steps = []
        for n in range(length):
            fresh = None
            for j, parts, solved in spectrum:
                weights = turn(j, n, length)
                fresh = weighted(fresh, parts * weights[0], solved[block][0])
                if parts == 2:
                    fresh = weighted(fresh, -parts * weights[1], solved[block][1])
            fresh = fresh * (math.exp(-log_alpha * n / length) / length)
            steps.append(fresh)
            change = fresh - befores[n][rows]
            total = total + change * change
        own = steps[0]
        give = steps[1]
        for n in range(1, length):
            own = jnp.where(me == n, steps[n], own)
            give = jnp.where(me == n, steps[n ^ 1], give)
        own_ref[rows] = own
        give_ref[rows] = give
    sum_ref[...] = jnp.broadcast_to(total[None], sum_ref.shape)


def join_kernel(
    entry_count, own_ref, got_ref, squares_ref, new_hbm, norm_hbm, norm_ref, sems
):
    species = lax.axis_index("tm") % 2
    copies = (
        pltpu.make_async_copy(own_ref, new_hbm.at[0, species], sems.at[0]),
        pltpu.make_async_copy(got_ref, new_hbm.at[0, 1 - species], sems.at[1]),
        pltpu.make_async_copy(norm_ref, norm_hbm, sems.at[2]),
    )
    copies[0].start()
    copies[1].start()
    norm_ref[0, 0] = jnp.sqrt(jnp.sum(jnp.sum(squares_ref[...], axis=0)) / entry_count)
    copies[2].start()
    for copy in copies:
        copy.wait()


def exchange(value, axis, bits):
    pairs = [(index, index ^ bits) for index in range(lax.axis_size(axis))]
    return lax.ppermute(value, axis, pairs)


def shards(
    forcing,
    initial_state,
    previous,
    zone_diffusion,
    drift_rate,
    column_zone,
    bottom_flag,
    open_faces,
):
    length = lax.axis_size("tm")
    space = lax.axis_size("space")
    cells, lanes = open_faces.shape
    whole = pl.BlockSpec(memory_space=pltpu.VMEM)
    outside = pl.BlockSpec(memory_space=pltpu.HBM)
    count = planes(length)
    params = pltpu.CompilerParams(vmem_limit_bytes=40 * 1024 * 1024)
    alone = pltpu.CompilerParams(vmem_limit_bytes=56 * 1024 * 1024)
    mine, other = pl.pallas_call(
        stack_kernel,
        out_shape=(
            pltpu.VMEM((2, cells, lanes), jnp.float32),
            pltpu.VMEM((2, cells, lanes), jnp.float32),
        ),
        in_specs=[outside] * 2,
        out_specs=[whole] * 2,
        scratch_shapes=[pltpu.SemaphoreType.DMA((4,))],
        compiler_params=alone,
        cost_estimate=pl.CostEstimate(flops=4000, bytes_accessed=500000, transcendentals=0),
        name="stack_arrays",
    )(forcing, previous)
    stacks = [mine]
    for bits in range(1, length):
        stacks.append(exchange(other if bits % 2 else mine, "tm", bits))
    near, far, initial = pl.pallas_call(
        functools.partial(factor_kernel, length),
        out_shape=(
            pltpu.VMEM((count, 2 * near_steps, cells, lanes), jnp.float32),
            pltpu.VMEM((count, 3, cells, lanes), jnp.float32),
            pltpu.VMEM((cells, lanes), jnp.float32),
        ),
        in_specs=[outside] * 6,
        out_specs=[whole] * 3,
        scratch_shapes=[
            pltpu.SMEM(zone_diffusion.shape, jnp.float32),
            pltpu.SMEM(drift_rate.shape, jnp.float32),
            pltpu.VMEM((1, lanes), jnp.int32),
            pltpu.VMEM((1, lanes), jnp.int32),
            pltpu.VMEM((cells, lanes), jnp.int32),
            pltpu.SemaphoreType.DMA((6,)),
        ],
        compiler_params=alone,
        cost_estimate=pl.CostEstimate(flops=4000000, bytes_accessed=3000000, transcendentals=0),
        name="factor_lines",
    )(initial_state, zone_diffusion, drift_rate, column_zone[None], bottom_flag[None], open_faces)
    own, give, squares = pl.pallas_call(
        functools.partial(sweep_kernel, length),
        out_shape=(
            pltpu.VMEM((cells, lanes), jnp.float32),
            pltpu.VMEM((cells, lanes), jnp.float32),
            pltpu.VMEM((2 * space, tile, lanes), jnp.float32),
        ),
        in_specs=[whole] * (length + 3),
        out_specs=[whole] * 3,
        compiler_params=params,
        cost_estimate=pl.CostEstimate(flops=4000000, bytes_accessed=3000000, transcendentals=0),
        name="solve_lines",
    )(*stacks, initial, near, far)
    got = exchange(give, "tm", 1)
    last = 2 * space - 1
    order = [last, *range(2, last, 2), *range(3, last, 2), 1, 0]
    groups = [[step * space + index for index in order] for step in range(0, length, 2)]
    squares = lax.all_to_all(
        squares, ("tm", "space"), 0, 0, axis_index_groups=groups, tiled=True
    )
    entry_count = length * space * forcing.shape[1] * cells * lanes
    new_iterate, norm = pl.pallas_call(
        functools.partial(join_kernel, entry_count),
        out_shape=(
            jax.ShapeDtypeStruct(forcing.shape, jnp.float32),
            jax.ShapeDtypeStruct((1, 1), jnp.float32),
        ),
        in_specs=[whole] * 3,
        out_specs=(outside, outside),
        scratch_shapes=[pltpu.SMEM((1, 1), jnp.float32), pltpu.SemaphoreType.DMA((3,))],
        compiler_params=params,
        cost_estimate=pl.CostEstimate(flops=4000, bytes_accessed=100000, transcendentals=0),
        name="join_species",
    )(own, got, squares)
    return (new_iterate, norm[0, 0])


def solution(mesh):
    placed = (
        P("tm", None, None, "space"),
        P(None, None, "space"),
        P("tm", None, None, "space"),
        P(),
        P(),
        P("space"),
        P("space"),
        P(None, "space"),
    )
    return jax.shard_map(
        shards,
        mesh=mesh,
        in_specs=placed,
        out_specs=(P("tm", None, None, "space"), P()),
        check_vma=False,
    )
```

```python
import functools
import math

import jax
import jax.numpy as jnp
from jax import lax
from jax.experimental import pallas as pl
from jax.experimental.pallas import tpu as pltpu
from jax.sharding import PartitionSpec as P

alpha_corner = 0.3
tile = 8
near_steps = 3


def roll_down(block, distance):
    return pltpu.roll(block, distance, 0)


def roll_up(block, distance):
    return pltpu.roll(block, block.shape[0] - distance, 0)


def c_mul(x, y):
    if len(x) == 1 and len(y) == 1:
        return (x[0] * y[0],)
    if len(x) == 1:
        return (x[0] * y[0], x[0] * y[1])
    if len(y) == 1:
        return (x[0] * y[0], x[1] * y[0])
    return (x[0] * y[0] - x[1] * y[1], x[0] * y[1] + x[1] * y[0])


def c_add(x, y):
    return tuple(p + q for p, q in zip(x, y))


def c_sub(x, y):
    return tuple(p - q for p, q in zip(x, y))


def c_neg(x):
    return tuple(-p for p in x)


def c_inverse(x):
    if len(x) == 1:
        return (1.0 / x[0],)
    scale = 1.0 / (x[0] * x[0] + x[1] * x[1])
    return (x[0] * scale, -x[1] * scale)


def c_map(f, x):
    return tuple(f(p) for p in x)


def frequencies(length):
    root = math.exp(math.log(alpha_corner) / length)
    listed = []
    for j in range(length // 2 + 1):
        angle = 2.0 * math.pi * j / length
        if j == 0 or 2 * j == length:
            listed.append((j, (1.0 - root * math.cos(angle),)))
        else:
            listed.append((j, (1.0 - root * math.cos(angle), root * math.sin(angle))))
    return listed


def planes(length):
    return sum(len(shift) for unused, shift in frequencies(length))


def turn(j, n, length):
    count = j * n % length
    if 4 * count % length == 0:
        return ((1.0, 0.0), (0.0, 1.0), (-1.0, 0.0), (0.0, -1.0))[4 * count // length]
    angle = 2.0 * math.pi * count / length
    return (math.cos(angle), math.sin(angle))


def weighted(total, weight, value):
    if weight == 0.0:
        return total
    if weight == 1.0:
        term = value
    elif weight == -1.0:
        return -value if total is None else total - value
    else:
        term = weight * value
    return term if total is None else total + term


def start_all(pairs, sems):
    copies = [
        pltpu.make_async_copy(source, target, sems.at[index])
        for index, (source, target) in enumerate(pairs)
    ]
    for copy in copies:
        copy.start()
    return copies


def stack_kernel(forcing_hbm, previous_hbm, mine_ref, other_ref, sems):
    species = lax.axis_index("tm") % 2
    pairs = (
        (forcing_hbm.at[0, species], mine_ref.at[0]),
        (previous_hbm.at[0, species], mine_ref.at[1]),
        (forcing_hbm.at[0, 1 - species], other_ref.at[0]),
        (previous_hbm.at[0, 1 - species], other_ref.at[1]),
    )
    for copy in start_all(pairs, sems):
        copy.wait()


def factor_kernel(
    length,
    initial_hbm,
    zones_hbm,
    drift_hbm,
    zone_hbm,
    flag_hbm,
    faces_hbm,
    near_ref,
    far_ref,
    initial_ref,
    zones_ref,
    drift_ref,
    zone_ref,
    flag_ref,
    faces_ref,
    sems,
):
    species = lax.axis_index("tm") % 2
    pairs = (
        (zones_hbm, zones_ref),
        (drift_hbm, drift_ref),
        (zone_hbm, zone_ref),
        (flag_hbm, flag_ref),
        (faces_hbm, faces_ref),
        (initial_hbm.at[species], initial_ref),
    )
    for copy in start_all(pairs, sems):
        copy.wait()
    zone = zone_ref[...]
    diffusion = jnp.zeros(zone.shape, jnp.float32)
    for index in range(zones_ref.shape[1]):
        diffusion = jnp.where(zone == index, zones_ref[species, index], diffusion)
    drift = drift_ref[species]
    cells, lanes = faces_ref.shape
    faces = faces_ref[...].astype(jnp.float32)
    row = lax.broadcasted_iota(jnp.int32, (cells, lanes), 0)
    link_above = jnp.where(row == cells - 1, 0.0, faces)
    link_below = jnp.where(row == 0, 0.0, roll_down(faces, 1))
    ground = jnp.where(row == 0, flag_ref[...].astype(jnp.float32), 0.0)
    below = -(diffusion + drift) * link_below
    above = -diffusion * link_above
    centre = diffusion * (link_below + link_above) + drift + 2.0 * diffusion * ground
    plane = 0
    for unused, shift in frequencies(length):
        parts = len(shift)
        a = (below,)
        c = (above,)
        b = (centre + shift[0],)
        if parts == 2:
            b = b + (jnp.full_like(centre, shift[1]),)
        for step in range(near_steps):
            distance = 1 << step
            inverse = c_inverse(b)
            low = c_neg(c_mul(a, c_map(lambda p: roll_down(p, distance), inverse)))
            high = c_neg(c_mul(c, c_map(lambda p: roll_up(p, distance), inverse)))
            down_c = c_map(lambda p: roll_down(p, distance), c)
            up_a = c_map(lambda p: roll_up(p, distance), a)
            b = c_add(b, c_add(c_mul(low, down_c), c_mul(high, up_a)))
            a = c_mul(low, c_map(lambda p: roll_down(p, distance), a))
            c = c_mul(high, c_map(lambda p: roll_up(p, distance), c))
            for part in range(parts):
                near_ref[plane + part, 2 * step] = low[part]
                near_ref[plane + part, 2 * step + 1] = high[part]
        carry = None
        for block in range(cells // tile):
            rows = slice(block * tile, (block + 1) * tile)
            ak, bk, ck = (c_map(lambda p: p[rows], item) for item in (a, b, c))
            if carry is None:
                eliminate = c_map(jnp.zeros_like, ak)
            else:
                eliminate = c_mul(ak, carry[0])
                bk = c_sub(bk, c_mul(eliminate, carry[1]))
            inverse = c_inverse(bk)
            substitute = c_mul(ck, inverse)
            for part in range(parts):
                far_ref[plane + part, 0, rows] = eliminate[part]
                far_ref[plane + part, 1, rows] = inverse[part]
                far_ref[plane + part, 2, rows] = substitute[part]
            carry = (inverse, ck)
        plane += parts


def in_order(me, held):
    bit = 1
    while bit < len(held):
        swap = (me & bit) != 0
        held = [
            jnp.where(swap, held[index ^ bit], held[index]) for index in range(len(held))
        ]
        bit *= 2
    return held


def sweep_kernel(length, *refs):
    stacks = refs[:length]
    initial_ref, near_ref, far_ref, own_ref, give_ref, sum_ref = refs[length:]
    cells, lanes = initial_ref.shape
    log_alpha = math.log(alpha_corner)
    me = lax.axis_index("tm")
    loads = in_order(me, [ref[0] for ref in stacks])
    befores = in_order(me, [ref[1] for ref in stacks])
    loads[0] = loads[0] + (initial_ref[...] - alpha_corner * befores[length - 1])
    scaled = [math.exp(log_alpha * n / length) * load for n, load in enumerate(loads)]
    spectrum = []
    plane = 0
    for j, shift in frequencies(length):
        parts = len(shift)
        rhs = [None] * parts
        for n in range(length):
            weights = turn(j, -n, length)
            for part in range(parts):
                rhs[part] = weighted(rhs[part], weights[part], scaled[n])
        rhs = tuple(rhs)
        for step in range(near_steps):
            distance = 1 << step
            low = tuple(near_ref[plane + p, 2 * step] for p in range(parts))
            high = tuple(near_ref[plane + p, 2 * step + 1] for p in range(parts))
            down = c_map(lambda p: roll_down(p, distance), rhs)
            up = c_map(lambda p: roll_up(p, distance), rhs)
            rhs = c_add(rhs, c_add(c_mul(low, down), c_mul(high, up)))
        blocks = []
        carry = None
        for block in range(cells // tile):
            rows = slice(block * tile, (block + 1) * tile)
            value = c_map(lambda p: p[rows], rhs)
            if carry is not None:
                eliminate = tuple(far_ref[plane + p, 0, rows] for p in range(parts))
                value = c_sub(value, c_mul(eliminate, carry))
            blocks.append(value)
            carry = value
        solved = [None] * len(blocks)
        carry = None
        for block in reversed(range(cells // tile)):
            rows = slice(block * tile, (block + 1) * tile)
            inverse = tuple(far_ref[plane + p, 1, rows] for p in range(parts))
            value = c_mul(inverse, blocks[block])
            if carry is not None:
                substitute = tuple(far_ref[plane + p, 2, rows] for p in range(parts))
                value = c_sub(value, c_mul(substitute, carry))
            solved[block] = value
            carry = value
        spectrum.append((j, parts, solved))
        plane += parts
    total = jnp.zeros((tile, lanes), jnp.float32)
    for block in range(cells // tile):
        rows = slice(block * tile, (block + 1) * tile)
        steps = []
        for n in range(length):
            fresh = None
            for j, parts, solved in spectrum:
                weights = turn(j, n, length)
                fresh = weighted(fresh, parts * weights[0], solved[block][0])
                if parts == 2:
                    fresh = weighted(fresh, -parts * weights[1], solved[block][1])
            fresh = fresh * (math.exp(-log_alpha * n / length) / length)
            steps.append(fresh)
            change = fresh - befores[n][rows]
            total = total + change * change
        own = steps[0]
        give = steps[1]
        for n in range(1, length):
            own = jnp.where(me == n, steps[n], own)
            give = jnp.where(me == n, steps[n ^ 1], give)
        own_ref[rows] = own
        give_ref[rows] = give
    row = jnp.sum(total, axis=0, keepdims=True)
    shift = lanes // 2
    while shift >= tile:
        row = row + pltpu.roll(row, shift, 1)
        shift //= 2
    sum_ref[...] = jnp.broadcast_to(row[:, :tile], sum_ref.shape)


def join_kernel(
    entry_count, own_ref, got_ref, squares_ref, new_hbm, norm_hbm, norm_ref, sems
):
    species = lax.axis_index("tm") % 2
    copies = (
        pltpu.make_async_copy(own_ref, new_hbm.at[0, species], sems.at[0]),
        pltpu.make_async_copy(got_ref, new_hbm.at[0, 1 - species], sems.at[1]),
        pltpu.make_async_copy(norm_ref, norm_hbm, sems.at[2]),
    )
    copies[0].start()
    copies[1].start()
    norm_ref[0, 0] = jnp.sqrt(jnp.sum(squares_ref[...]) / entry_count)
    copies[2].start()
    for copy in copies:
        copy.wait()


def exchange(value, axis, bits):
    pairs = [(index, index ^ bits) for index in range(lax.axis_size(axis))]
    return lax.ppermute(value, axis, pairs)


def shards(
    forcing,
    initial_state,
    previous,
    zone_diffusion,
    drift_rate,
    column_zone,
    bottom_flag,
    open_faces,
):
    length = lax.axis_size("tm")
    space = lax.axis_size("space")
    cells, lanes = open_faces.shape
    whole = pl.BlockSpec(memory_space=pltpu.VMEM)
    outside = pl.BlockSpec(memory_space=pltpu.HBM)
    count = planes(length)
    params = pltpu.CompilerParams(vmem_limit_bytes=40 * 1024 * 1024)
    alone = pltpu.CompilerParams(vmem_limit_bytes=56 * 1024 * 1024)
    mine, other = pl.pallas_call(
        stack_kernel,
        out_shape=(
            pltpu.VMEM((2, cells, lanes), jnp.float32),
            pltpu.VMEM((2, cells, lanes), jnp.float32),
        ),
        in_specs=[outside] * 2,
        out_specs=[whole] * 2,
        scratch_shapes=[pltpu.SemaphoreType.DMA((4,))],
        compiler_params=alone,
        cost_estimate=pl.CostEstimate(flops=4000, bytes_accessed=500000, transcendentals=0),
        name="stack_arrays",
    )(forcing, previous)
    stacks = [mine]
    for bits in range(1, length):
        stacks.append(exchange(other if bits % 2 else mine, "tm", bits))
    near, far, initial = pl.pallas_call(
        functools.partial(factor_kernel, length),
        out_shape=(
            pltpu.VMEM((count, 2 * near_steps, cells, lanes), jnp.float32),
            pltpu.VMEM((count, 3, cells, lanes), jnp.float32),
            pltpu.VMEM((cells, lanes), jnp.float32),
        ),
        in_specs=[outside] * 6,
        out_specs=[whole] * 3,
        scratch_shapes=[
            pltpu.SMEM(zone_diffusion.shape, jnp.float32),
            pltpu.SMEM(drift_rate.shape, jnp.float32),
            pltpu.VMEM((1, lanes), jnp.int32),
            pltpu.VMEM((1, lanes), jnp.int32),
            pltpu.VMEM((cells, lanes), jnp.int32),
            pltpu.SemaphoreType.DMA((6,)),
        ],
        compiler_params=alone,
        cost_estimate=pl.CostEstimate(flops=4000000, bytes_accessed=3000000, transcendentals=0),
        name="factor_lines",
    )(initial_state, zone_diffusion, drift_rate, column_zone[None], bottom_flag[None], open_faces)
    own, give, squares = pl.pallas_call(
        functools.partial(sweep_kernel, length),
        out_shape=(
            pltpu.VMEM((cells, lanes), jnp.float32),
            pltpu.VMEM((cells, lanes), jnp.float32),
            pltpu.VMEM((2 * space, 1, tile), jnp.float32),
        ),
        in_specs=[whole] * (length + 3),
        out_specs=[whole] * 3,
        compiler_params=params,
        cost_estimate=pl.CostEstimate(flops=4000000, bytes_accessed=3000000, transcendentals=0),
        name="solve_lines",
    )(*stacks, initial, near, far)
    got = exchange(give, "tm", 1)
    last = 2 * space - 1
    order = [last, *range(2, last, 2), *range(3, last, 2), 1, 0]
    groups = [[step * space + index for index in order] for step in range(0, length, 2)]
    squares = lax.all_to_all(
        squares, ("tm", "space"), 0, 0, axis_index_groups=groups, tiled=True
    )
    entry_count = length * space * forcing.shape[1] * cells * lanes
    new_iterate, norm = pl.pallas_call(
        functools.partial(join_kernel, entry_count),
        out_shape=(
            jax.ShapeDtypeStruct(forcing.shape, jnp.float32),
            jax.ShapeDtypeStruct((1, 1), jnp.float32),
        ),
        in_specs=[whole] * 3,
        out_specs=(outside, outside),
        scratch_shapes=[pltpu.SMEM((1, 1), jnp.float32), pltpu.SemaphoreType.DMA((3,))],
        compiler_params=params,
        cost_estimate=pl.CostEstimate(flops=4000, bytes_accessed=100000, transcendentals=0),
        name="join_species",
    )(own, got, squares)
    return (new_iterate, norm[0, 0])


def solution(mesh):
    placed = (
        P("tm", None, None, "space"),
        P(None, None, "space"),
        P("tm", None, None, "space"),
        P(),
        P(),
        P("space"),
        P("space"),
        P(None, "space"),
    )
    return jax.shard_map(
        shards,
        mesh=mesh,
        in_specs=placed,
        out_specs=(P("tm", None, None, "space"), P()),
        check_vma=False,
    )
```

```python
import functools
import math

import jax
import jax.numpy as jnp
from jax import lax
from jax.experimental import pallas as pl
from jax.experimental.pallas import tpu as pltpu
from jax.sharding import PartitionSpec as P

alpha_corner = 0.3
tile = 8
near_steps = 3


def roll_down(block, distance):
    return pltpu.roll(block, distance, 0)


def roll_up(block, distance):
    return pltpu.roll(block, block.shape[0] - distance, 0)


def c_mul(x, y):
    if len(x) == 1 and len(y) == 1:
        return (x[0] * y[0],)
    if len(x) == 1:
        return (x[0] * y[0], x[0] * y[1])
    if len(y) == 1:
        return (x[0] * y[0], x[1] * y[0])
    return (x[0] * y[0] - x[1] * y[1], x[0] * y[1] + x[1] * y[0])


def c_add(x, y):
    return tuple(p + q for p, q in zip(x, y))


def c_sub(x, y):
    return tuple(p - q for p, q in zip(x, y))


def c_neg(x):
    return tuple(-p for p in x)


def c_inverse(x):
    if len(x) == 1:
        return (1.0 / x[0],)
    scale = 1.0 / (x[0] * x[0] + x[1] * x[1])
    return (x[0] * scale, -x[1] * scale)


def c_map(f, x):
    return tuple(f(p) for p in x)


def frequencies(length):
    root = math.exp(math.log(alpha_corner) / length)
    listed = []
    for j in range(length // 2 + 1):
        angle = 2.0 * math.pi * j / length
        if j == 0 or 2 * j == length:
            listed.append((j, (1.0 - root * math.cos(angle),)))
        else:
            listed.append((j, (1.0 - root * math.cos(angle), root * math.sin(angle))))
    return listed


def planes(length):
    return sum(len(shift) for unused, shift in frequencies(length))


def turn(j, n, length):
    count = j * n % length
    if 4 * count % length == 0:
        return ((1.0, 0.0), (0.0, 1.0), (-1.0, 0.0), (0.0, -1.0))[4 * count // length]
    angle = 2.0 * math.pi * count / length
    return (math.cos(angle), math.sin(angle))


def weighted(total, weight, value):
    if weight == 0.0:
        return total
    if weight == 1.0:
        term = value
    elif weight == -1.0:
        return -value if total is None else total - value
    else:
        term = weight * value
    return term if total is None else total + term


def start_all(pairs, sems):
    copies = [
        pltpu.make_async_copy(source, target, sems.at[index])
        for index, (source, target) in enumerate(pairs)
    ]
    for copy in copies:
        copy.start()
    return copies


def stack_kernel(forcing_hbm, previous_hbm, mine_ref, other_ref, sems):
    species = lax.axis_index("tm") % 2
    pairs = (
        (forcing_hbm.at[0, species], mine_ref.at[0]),
        (previous_hbm.at[0, species], mine_ref.at[1]),
        (forcing_hbm.at[0, 1 - species], other_ref.at[0]),
        (previous_hbm.at[0, 1 - species], other_ref.at[1]),
    )
    for copy in start_all(pairs, sems):
        copy.wait()


def factor_kernel(
    length,
    initial_hbm,
    zones_hbm,
    drift_hbm,
    zone_hbm,
    flag_hbm,
    faces_hbm,
    near_ref,
    far_ref,
    initial_ref,
    zones_ref,
    drift_ref,
    zone_ref,
    flag_ref,
    faces_ref,
    sems,
):
    species = lax.axis_index("tm") % 2
    pairs = (
        (zones_hbm, zones_ref),
        (drift_hbm, drift_ref),
        (zone_hbm, zone_ref),
        (flag_hbm, flag_ref),
        (faces_hbm, faces_ref),
        (initial_hbm.at[species], initial_ref),
    )
    for copy in start_all(pairs, sems):
        copy.wait()
    zone = zone_ref[...]
    diffusion = jnp.zeros(zone.shape, jnp.float32)
    for index in range(zones_ref.shape[1]):
        diffusion = jnp.where(zone == index, zones_ref[species, index], diffusion)
    drift = drift_ref[species]
    cells, lanes = faces_ref.shape
    faces = faces_ref[...].astype(jnp.float32)
    row = lax.broadcasted_iota(jnp.int32, (cells, lanes), 0)
    link_above = jnp.where(row == cells - 1, 0.0, faces)
    link_below = jnp.where(row == 0, 0.0, roll_down(faces, 1))
    ground = jnp.where(row == 0, flag_ref[...].astype(jnp.float32), 0.0)
    below = -(diffusion + drift) * link_below
    above = -diffusion * link_above
    centre = diffusion * (link_below + link_above) + drift + 2.0 * diffusion * ground
    plane = 0
    for unused, shift in frequencies(length):
        parts = len(shift)
        a = (below,)
        c = (above,)
        b = (centre + shift[0],)
        if parts == 2:
            b = b + (jnp.full_like(centre, shift[1]),)
        for step in range(near_steps):
            distance = 1 << step
            inverse = c_inverse(b)
            low = c_neg(c_mul(a, c_map(lambda p: roll_down(p, distance), inverse)))
            high = c_neg(c_mul(c, c_map(lambda p: roll_up(p, distance), inverse)))
            down_c = c_map(lambda p: roll_down(p, distance), c)
            up_a = c_map(lambda p: roll_up(p, distance), a)
            b = c_add(b, c_add(c_mul(low, down_c), c_mul(high, up_a)))
            a = c_mul(low, c_map(lambda p: roll_down(p, distance), a))
            c = c_mul(high, c_map(lambda p: roll_up(p, distance), c))
            for part in range(parts):
                near_ref[plane + part, 2 * step] = low[part]
                near_ref[plane + part, 2 * step + 1] = high[part]
        carry = None
        for block in range(cells // tile):
            rows = slice(block * tile, (block + 1) * tile)
            ak, bk, ck = (c_map(lambda p: p[rows], item) for item in (a, b, c))
            if carry is None:
                eliminate = c_map(jnp.zeros_like, ak)
            else:
                eliminate = c_mul(ak, carry[0])
                bk = c_sub(bk, c_mul(eliminate, carry[1]))
            inverse = c_inverse(bk)
            substitute = c_mul(ck, inverse)
            for part in range(parts):
                far_ref[plane + part, 0, rows] = eliminate[part]
                far_ref[plane + part, 1, rows] = inverse[part]
                far_ref[plane + part, 2, rows] = substitute[part]
            carry = (inverse, ck)
        plane += parts


def in_order(me, held):
    bit = 1
    while bit < len(held):
        swap = (me & bit) != 0
        held = [
            jnp.where(swap, held[index ^ bit], held[index]) for index in range(len(held))
        ]
        bit *= 2
    return held


def sweep_kernel(length, *refs):
    stacks = refs[:length]
    initial_ref, near_ref, far_ref, own_ref, give_ref, sum_ref = refs[length:]
    cells, lanes = initial_ref.shape
    log_alpha = math.log(alpha_corner)
    me = lax.axis_index("tm")
    loads = in_order(me, [ref[0] for ref in stacks])
    befores = in_order(me, [ref[1] for ref in stacks])
    loads[0] = loads[0] + (initial_ref[...] - alpha_corner * befores[length - 1])
    scaled = [math.exp(log_alpha * n / length) * load for n, load in enumerate(loads)]
    spectrum = []
    plane = 0
    for j, shift in frequencies(length):
        parts = len(shift)
        rhs = [None] * parts
        for n in range(length):
            weights = turn(j, -n, length)
            for part in range(parts):
                rhs[part] = weighted(rhs[part], weights[part], scaled[n])
        rhs = tuple(rhs)
        for step in range(near_steps):
            distance = 1 << step
            low = tuple(near_ref[plane + p, 2 * step] for p in range(parts))
            high = tuple(near_ref[plane + p, 2 * step + 1] for p in range(parts))
            down = c_map(lambda p: roll_down(p, distance), rhs)
            up = c_map(lambda p: roll_up(p, distance), rhs)
            rhs = c_add(rhs, c_add(c_mul(low, down), c_mul(high, up)))
        blocks = []
        carry = None
        for block in range(cells // tile):
            rows = slice(block * tile, (block + 1) * tile)
            value = c_map(lambda p: p[rows], rhs)
            if carry is not None:
                eliminate = tuple(far_ref[plane + p, 0, rows] for p in range(parts))
                value = c_sub(value, c_mul(eliminate, carry))
            blocks.append(value)
            carry = value
        solved = [None] * len(blocks)
        carry = None
        for block in reversed(range(cells // tile)):
            rows = slice(block * tile, (block + 1) * tile)
            inverse = tuple(far_ref[plane + p, 1, rows] for p in range(parts))
            value = c_mul(inverse, blocks[block])
            if carry is not None:
                substitute = tuple(far_ref[plane + p, 2, rows] for p in range(parts))
                value = c_sub(value, c_mul(substitute, carry))
            solved[block] = value
            carry = value
        spectrum.append((j, parts, solved))
        plane += parts
    total = jnp.zeros((tile, lanes), jnp.float32)
    for block in range(cells // tile):
        rows = slice(block * tile, (block + 1) * tile)
        steps = []
        for n in range(length):
            fresh = None
            for j, parts, solved in spectrum:
                weights = turn(j, n, length)
                fresh = weighted(fresh, parts * weights[0], solved[block][0])
                if parts == 2:
                    fresh = weighted(fresh, -parts * weights[1], solved[block][1])
            fresh = fresh * (math.exp(-log_alpha * n / length) / length)
            steps.append(fresh)
            change = fresh - befores[n][rows]
            total = total + change * change
        own = steps[0]
        give = steps[1]
        for n in range(1, length):
            own = jnp.where(me == n, steps[n], own)
            give = jnp.where(me == n, steps[n ^ 1], give)
        own_ref[rows] = own
        give_ref[rows] = give
    sum_ref[...] = jnp.broadcast_to(jnp.sum(total, axis=0, keepdims=True), sum_ref.shape)


def join_kernel(
    entry_count, own_ref, got_ref, squares_ref, new_hbm, norm_hbm, norm_ref, sems
):
    species = lax.axis_index("tm") % 2
    copies = (
        pltpu.make_async_copy(own_ref, new_hbm.at[0, species], sems.at[0]),
        pltpu.make_async_copy(got_ref, new_hbm.at[0, 1 - species], sems.at[1]),
        pltpu.make_async_copy(norm_ref, norm_hbm, sems.at[2]),
    )
    copies[0].start()
    copies[1].start()
    norm_ref[0, 0] = jnp.sqrt(jnp.sum(squares_ref[...]) / entry_count)
    copies[2].start()
    for copy in copies:
        copy.wait()


def exchange(value, axis, bits):
    pairs = [(index, index ^ bits) for index in range(lax.axis_size(axis))]
    return lax.ppermute(value, axis, pairs)


def shards(
    forcing,
    initial_state,
    previous,
    zone_diffusion,
    drift_rate,
    column_zone,
    bottom_flag,
    open_faces,
):
    length = lax.axis_size("tm")
    space = lax.axis_size("space")
    cells, lanes = open_faces.shape
    whole = pl.BlockSpec(memory_space=pltpu.VMEM)
    outside = pl.BlockSpec(memory_space=pltpu.HBM)
    count = planes(length)
    params = pltpu.CompilerParams(vmem_limit_bytes=40 * 1024 * 1024)
    alone = pltpu.CompilerParams(vmem_limit_bytes=56 * 1024 * 1024)
    mine, other = pl.pallas_call(
        stack_kernel,
        out_shape=(
            pltpu.VMEM((2, cells, lanes), jnp.float32),
            pltpu.VMEM((2, cells, lanes), jnp.float32),
        ),
        in_specs=[outside] * 2,
        out_specs=[whole] * 2,
        scratch_shapes=[pltpu.SemaphoreType.DMA((4,))],
        compiler_params=alone,
        cost_estimate=pl.CostEstimate(flops=4000, bytes_accessed=500000, transcendentals=0),
        name="stack_arrays",
    )(forcing, previous)
    stacks = [mine]
    for bits in range(1, length):
        stacks.append(exchange(other if bits % 2 else mine, "tm", bits))
    near, far, initial = pl.pallas_call(
        functools.partial(factor_kernel, length),
        out_shape=(
            pltpu.VMEM((count, 2 * near_steps, cells, lanes), jnp.float32),
            pltpu.VMEM((count, 3, cells, lanes), jnp.float32),
            pltpu.VMEM((cells, lanes), jnp.float32),
        ),
        in_specs=[outside] * 6,
        out_specs=[whole] * 3,
        scratch_shapes=[
            pltpu.SMEM(zone_diffusion.shape, jnp.float32),
            pltpu.SMEM(drift_rate.shape, jnp.float32),
            pltpu.VMEM((1, lanes), jnp.int32),
            pltpu.VMEM((1, lanes), jnp.int32),
            pltpu.VMEM((cells, lanes), jnp.int32),
            pltpu.SemaphoreType.DMA((6,)),
        ],
        compiler_params=alone,
        cost_estimate=pl.CostEstimate(flops=4000000, bytes_accessed=3000000, transcendentals=0),
        name="factor_lines",
    )(initial_state, zone_diffusion, drift_rate, column_zone[None], bottom_flag[None], open_faces)
    own, give, squares = pl.pallas_call(
        functools.partial(sweep_kernel, length),
        out_shape=(
            pltpu.VMEM((cells, lanes), jnp.float32),
            pltpu.VMEM((cells, lanes), jnp.float32),
            pltpu.VMEM((2 * space, lanes), jnp.float32),
        ),
        in_specs=[whole] * (length + 3),
        out_specs=[whole] * 3,
        compiler_params=params,
        cost_estimate=pl.CostEstimate(flops=4000000, bytes_accessed=3000000, transcendentals=0),
        name="solve_lines",
    )(*stacks, initial, near, far)
    got = exchange(give, "tm", 1)
    last = 2 * space - 1
    order = [last, *range(2, last, 2), *range(3, last, 2), 1, 0]
    groups = [[step * space + index for index in order] for step in range(0, length, 2)]
    squares = lax.all_to_all(
        squares, ("tm", "space"), 0, 0, axis_index_groups=groups, tiled=True
    )
    entry_count = length * space * forcing.shape[1] * cells * lanes
    new_iterate, norm = pl.pallas_call(
        functools.partial(join_kernel, entry_count),
        out_shape=(
            jax.ShapeDtypeStruct(forcing.shape, jnp.float32),
            jax.ShapeDtypeStruct((1, 1), jnp.float32),
        ),
        in_specs=[whole] * 3,
        out_specs=(outside, outside),
        scratch_shapes=[pltpu.SMEM((1, 1), jnp.float32), pltpu.SemaphoreType.DMA((3,))],
        compiler_params=params,
        cost_estimate=pl.CostEstimate(flops=4000, bytes_accessed=100000, transcendentals=0),
        name="join_species",
    )(own, got, squares)
    return (new_iterate, norm[0, 0])


def solution(mesh):
    placed = (
        P("tm", None, None, "space"),
        P(None, None, "space"),
        P("tm", None, None, "space"),
        P(),
        P(),
        P("space"),
        P("space"),
        P(None, "space"),
    )
    return jax.shard_map(
        shards,
        mesh=mesh,
        in_specs=placed,
        out_specs=(P("tm", None, None, "space"), P()),
        check_vma=False,
    )
```

```python
import functools
import math

import jax
import jax.numpy as jnp
from jax import lax
from jax.experimental import pallas as pl
from jax.experimental.pallas import tpu as pltpu
from jax.sharding import PartitionSpec as P

alpha_corner = 0.3
tile = 8
near_steps = 3


def roll_down(block, distance):
    return pltpu.roll(block, distance, 0)


def roll_up(block, distance):
    return pltpu.roll(block, block.shape[0] - distance, 0)


def c_mul(x, y):
    if len(x) == 1 and len(y) == 1:
        return (x[0] * y[0],)
    if len(x) == 1:
        return (x[0] * y[0], x[0] * y[1])
    if len(y) == 1:
        return (x[0] * y[0], x[1] * y[0])
    return (x[0] * y[0] - x[1] * y[1], x[0] * y[1] + x[1] * y[0])


def c_add(x, y):
    return tuple(p + q for p, q in zip(x, y))


def c_sub(x, y):
    return tuple(p - q for p, q in zip(x, y))


def c_neg(x):
    return tuple(-p for p in x)


def c_inverse(x):
    if len(x) == 1:
        return (1.0 / x[0],)
    scale = 1.0 / (x[0] * x[0] + x[1] * x[1])
    return (x[0] * scale, -x[1] * scale)


def c_map(f, x):
    return tuple(f(p) for p in x)


def frequencies(length):
    root = math.exp(math.log(alpha_corner) / length)
    listed = []
    for j in range(length // 2 + 1):
        angle = 2.0 * math.pi * j / length
        if j == 0 or 2 * j == length:
            listed.append((j, (1.0 - root * math.cos(angle),)))
        else:
            listed.append((j, (1.0 - root * math.cos(angle), root * math.sin(angle))))
    return listed


def planes(length):
    return sum(len(shift) for unused, shift in frequencies(length))


def turn(j, n, length):
    count = j * n % length
    if 4 * count % length == 0:
        return ((1.0, 0.0), (0.0, 1.0), (-1.0, 0.0), (0.0, -1.0))[4 * count // length]
    angle = 2.0 * math.pi * count / length
    return (math.cos(angle), math.sin(angle))


def weighted(total, weight, value):
    if weight == 0.0:
        return total
    if weight == 1.0:
        term = value
    elif weight == -1.0:
        return -value if total is None else total - value
    else:
        term = weight * value
    return term if total is None else total + term


def start_all(pairs, sems):
    copies = [
        pltpu.make_async_copy(source, target, sems.at[index])
        for index, (source, target) in enumerate(pairs)
    ]
    for copy in copies:
        copy.start()
    return copies


def stack_kernel(forcing_hbm, previous_hbm, mine_ref, other_ref, sems):
    species = lax.axis_index("tm") % 2
    pairs = (
        (forcing_hbm.at[0, species], mine_ref.at[0]),
        (previous_hbm.at[0, species], mine_ref.at[1]),
        (forcing_hbm.at[0, 1 - species], other_ref.at[0]),
        (previous_hbm.at[0, 1 - species], other_ref.at[1]),
    )
    for copy in start_all(pairs, sems):
        copy.wait()


def factor_kernel(
    length,
    initial_hbm,
    zones_hbm,
    drift_hbm,
    zone_hbm,
    flag_hbm,
    faces_hbm,
    near_ref,
    far_ref,
    initial_ref,
    zones_ref,
    drift_ref,
    zone_ref,
    flag_ref,
    faces_ref,
    sems,
):
    species = lax.axis_index("tm") % 2
    pairs = (
        (zones_hbm, zones_ref),
        (drift_hbm, drift_ref),
        (zone_hbm, zone_ref),
        (flag_hbm, flag_ref),
        (faces_hbm, faces_ref),
        (initial_hbm.at[species], initial_ref),
    )
    for copy in start_all(pairs, sems):
        copy.wait()
    zone = zone_ref[...]
    diffusion = jnp.zeros(zone.shape, jnp.float32)
    for index in range(zones_ref.shape[1]):
        diffusion = jnp.where(zone == index, zones_ref[species, index], diffusion)
    drift = drift_ref[species]
    cells, lanes = faces_ref.shape
    faces = faces_ref[...].astype(jnp.float32)
    row = lax.broadcasted_iota(jnp.int32, (cells, lanes), 0)
    link_above = jnp.where(row == cells - 1, 0.0, faces)
    link_below = jnp.where(row == 0, 0.0, roll_down(faces, 1))
    ground = jnp.where(row == 0, flag_ref[...].astype(jnp.float32), 0.0)
    below = -(diffusion + drift) * link_below
    above = -diffusion * link_above
    centre = diffusion * (link_below + link_above) + drift + 2.0 * diffusion * ground
    plane = 0
    for unused, shift in frequencies(length):
        parts = len(shift)
        a = (below,)
        c = (above,)
        b = (centre + shift[0],)
        if parts == 2:
            b = b + (jnp.full_like(centre, shift[1]),)
        for step in range(near_steps):
            distance = 1 << step
            inverse = c_inverse(b)
            low = c_neg(c_mul(a, c_map(lambda p: roll_down(p, distance), inverse)))
            high = c_neg(c_mul(c, c_map(lambda p: roll_up(p, distance), inverse)))
            down_c = c_map(lambda p: roll_down(p, distance), c)
            up_a = c_map(lambda p: roll_up(p, distance), a)
            b = c_add(b, c_add(c_mul(low, down_c), c_mul(high, up_a)))
            a = c_mul(low, c_map(lambda p: roll_down(p, distance), a))
            c = c_mul(high, c_map(lambda p: roll_up(p, distance), c))
            for part in range(parts):
                near_ref[plane + part, 2 * step] = low[part]
                near_ref[plane + part, 2 * step + 1] = high[part]
        carry = None
        for block in range(cells // tile):
            rows = slice(block * tile, (block + 1) * tile)
            ak, bk, ck = (c_map(lambda p: p[rows], item) for item in (a, b, c))
            if carry is None:
                eliminate = c_map(jnp.zeros_like, ak)
            else:
                eliminate = c_mul(ak, carry[0])
                bk = c_sub(bk, c_mul(eliminate, carry[1]))
            inverse = c_inverse(bk)
            substitute = c_mul(ck, inverse)
            for part in range(parts):
                far_ref[plane + part, 0, rows] = eliminate[part]
                far_ref[plane + part, 1, rows] = inverse[part]
                far_ref[plane + part, 2, rows] = substitute[part]
            carry = (inverse, ck)
        plane += parts


def in_order(me, held):
    bit = 1
    while bit < len(held):
        swap = (me & bit) != 0
        held = [
            jnp.where(swap, held[index ^ bit], held[index]) for index in range(len(held))
        ]
        bit *= 2
    return held


def sweep_kernel(length, *refs):
    stacks = refs[:length]
    initial_ref, near_ref, far_ref, own_ref, give_ref, sum_ref = refs[length:]
    cells, lanes = initial_ref.shape
    log_alpha = math.log(alpha_corner)
    me = lax.axis_index("tm")
    loads = in_order(me, [ref[0] for ref in stacks])
    befores = in_order(me, [ref[1] for ref in stacks])
    loads[0] = loads[0] + (initial_ref[...] - alpha_corner * befores[length - 1])
    scaled = [math.exp(log_alpha * n / length) * load for n, load in enumerate(loads)]
    spectrum = []
    plane = 0
    for j, shift in frequencies(length):
        parts = len(shift)
        rhs = [None] * parts
        for n in range(length):
            weights = turn(j, -n, length)
            for part in range(parts):
                rhs[part] = weighted(rhs[part], weights[part], scaled[n])
        rhs = tuple(rhs)
        for step in range(near_steps):
            distance = 1 << step
            low = tuple(near_ref[plane + p, 2 * step] for p in range(parts))
            high = tuple(near_ref[plane + p, 2 * step + 1] for p in range(parts))
            down = c_map(lambda p: roll_down(p, distance), rhs)
            up = c_map(lambda p: roll_up(p, distance), rhs)
            rhs = c_add(rhs, c_add(c_mul(low, down), c_mul(high, up)))
        blocks = []
        carry = None
        for block in range(cells // tile):
            rows = slice(block * tile, (block + 1) * tile)
            value = c_map(lambda p: p[rows], rhs)
            if carry is not None:
                eliminate = tuple(far_ref[plane + p, 0, rows] for p in range(parts))
                value = c_sub(value, c_mul(eliminate, carry))
            blocks.append(value)
            carry = value
        solved = [None] * len(blocks)
        carry = None
        for block in reversed(range(cells // tile)):
            rows = slice(block * tile, (block + 1) * tile)
            inverse = tuple(far_ref[plane + p, 1, rows] for p in range(parts))
            value = c_mul(inverse, blocks[block])
            if carry is not None:
                substitute = tuple(far_ref[plane + p, 2, rows] for p in range(parts))
                value = c_sub(value, c_mul(substitute, carry))
            solved[block] = value
            carry = value
        spectrum.append((j, parts, solved))
        plane += parts
    total = jnp.zeros((tile, lanes), jnp.float32)
    for block in range(cells // tile):
        rows = slice(block * tile, (block + 1) * tile)
        steps = []
        for n in range(length):
            fresh = None
            for j, parts, solved in spectrum:
                weights = turn(j, n, length)
                fresh = weighted(fresh, parts * weights[0], solved[block][0])
                if parts == 2:
                    fresh = weighted(fresh, -parts * weights[1], solved[block][1])
            fresh = fresh * (math.exp(-log_alpha * n / length) / length)
            steps.append(fresh)
            change = fresh - befores[n][rows]
            total = total + change * change
        own = steps[0]
        give = steps[1]
        for n in range(1, length):
            own = jnp.where(me == n, steps[n], own)
            give = jnp.where(me == n, steps[n ^ 1], give)
        own_ref[rows] = own
        give_ref[rows] = give
    sum_ref[...] = jnp.broadcast_to(jnp.sum(total, axis=0, keepdims=True), sum_ref.shape)


def join_kernel(
    entry_count, own_ref, got_ref, squares_ref, new_hbm, norm_hbm, norm_ref, sems
):
    species = lax.axis_index("tm") % 2
    copies = (
        pltpu.make_async_copy(own_ref, new_hbm.at[0, species], sems.at[0]),
        pltpu.make_async_copy(got_ref, new_hbm.at[0, 1 - species], sems.at[1]),
        pltpu.make_async_copy(norm_ref, norm_hbm, sems.at[2]),
    )
    copies[0].start()
    copies[1].start()
    norm_ref[0, 0] = jnp.sqrt(jnp.sum(squares_ref[...]) * (1.0 / entry_count))
    copies[2].start()
    for copy in copies:
        copy.wait()


def exchange(value, axis, bits):
    pairs = [(index, index ^ bits) for index in range(lax.axis_size(axis))]
    return lax.ppermute(value, axis, pairs)


def shards(
    forcing,
    initial_state,
    previous,
    zone_diffusion,
    drift_rate,
    column_zone,
    bottom_flag,
    open_faces,
):
    length = lax.axis_size("tm")
    space = lax.axis_size("space")
    cells, lanes = open_faces.shape
    whole = pl.BlockSpec(memory_space=pltpu.VMEM)
    outside = pl.BlockSpec(memory_space=pltpu.HBM)
    count = planes(length)
    params = pltpu.CompilerParams(vmem_limit_bytes=40 * 1024 * 1024)
    alone = pltpu.CompilerParams(vmem_limit_bytes=56 * 1024 * 1024)
    mine, other = pl.pallas_call(
        stack_kernel,
        out_shape=(
            pltpu.VMEM((2, cells, lanes), jnp.float32),
            pltpu.VMEM((2, cells, lanes), jnp.float32),
        ),
        in_specs=[outside] * 2,
        out_specs=[whole] * 2,
        scratch_shapes=[pltpu.SemaphoreType.DMA((4,))],
        compiler_params=alone,
        cost_estimate=pl.CostEstimate(flops=4000, bytes_accessed=500000, transcendentals=0),
        name="stack_arrays",
    )(forcing, previous)
    stacks = [mine]
    for bits in range(1, length):
        stacks.append(exchange(other if bits % 2 else mine, "tm", bits))
    near, far, initial = pl.pallas_call(
        functools.partial(factor_kernel, length),
        out_shape=(
            pltpu.VMEM((count, 2 * near_steps, cells, lanes), jnp.float32),
            pltpu.VMEM((count, 3, cells, lanes), jnp.float32),
            pltpu.VMEM((cells, lanes), jnp.float32),
        ),
        in_specs=[outside] * 6,
        out_specs=[whole] * 3,
        scratch_shapes=[
            pltpu.SMEM(zone_diffusion.shape, jnp.float32),
            pltpu.SMEM(drift_rate.shape, jnp.float32),
            pltpu.VMEM((1, lanes), jnp.int32),
            pltpu.VMEM((1, lanes), jnp.int32),
            pltpu.VMEM((cells, lanes), jnp.int32),
            pltpu.SemaphoreType.DMA((6,)),
        ],
        compiler_params=alone,
        cost_estimate=pl.CostEstimate(flops=4000000, bytes_accessed=3000000, transcendentals=0),
        name="factor_lines",
    )(initial_state, zone_diffusion, drift_rate, column_zone[None], bottom_flag[None], open_faces)
    own, give, squares = pl.pallas_call(
        functools.partial(sweep_kernel, length),
        out_shape=(
            pltpu.VMEM((cells, lanes), jnp.float32),
            pltpu.VMEM((cells, lanes), jnp.float32),
            pltpu.VMEM((2 * space, 1, lanes), jnp.float32),
        ),
        in_specs=[whole] * (length + 3),
        out_specs=[whole] * 3,
        compiler_params=params,
        cost_estimate=pl.CostEstimate(flops=4000000, bytes_accessed=3000000, transcendentals=0),
        name="solve_lines",
    )(*stacks, initial, near, far)
    got = exchange(give, "tm", 1)
    last = 2 * space - 1
    order = [last, *range(2, last, 2), *range(3, last, 2), 1, 0]
    groups = [[step * space + index for index in order] for step in range(0, length, 2)]
    squares = lax.all_to_all(
        squares, ("tm", "space"), 0, 0, axis_index_groups=groups, tiled=True
    )
    entry_count = length * space * forcing.shape[1] * cells * lanes
    new_iterate, norm = pl.pallas_call(
        functools.partial(join_kernel, entry_count),
        out_shape=(
            jax.ShapeDtypeStruct(forcing.shape, jnp.float32),
            jax.ShapeDtypeStruct((1, 1), jnp.float32),
        ),
        in_specs=[whole] * 3,
        out_specs=(outside, outside),
        scratch_shapes=[pltpu.SMEM((1, 1), jnp.float32), pltpu.SemaphoreType.DMA((3,))],
        compiler_params=params,
        cost_estimate=pl.CostEstimate(flops=4000, bytes_accessed=100000, transcendentals=0),
        name="join_species",
    )(own, got, squares)
    return (new_iterate, norm[0, 0])


def solution(mesh):
    placed = (
        P("tm", None, None, "space"),
        P(None, None, "space"),
        P("tm", None, None, "space"),
        P(),
        P(),
        P("space"),
        P("space"),
        P(None, "space"),
    )
    return jax.shard_map(
        shards,
        mesh=mesh,
        in_specs=placed,
        out_specs=(P("tm", None, None, "space"), P()),
        check_vma=False,
    )
```
